32 devices in a mesh: blk: 8 (over z, y), tp: 4 (over x, core).
Axes of the slice: x: 2, y: 2, z: 4, core: 2. Of those that a mesh axis runs over, the one named last changes fastest.
Arguments:
- layer_input: bfloat16 [4096, 2048], P('blk'), may hold values from -6 to 6
- ln1_gain: float32 [2048], replicated, may hold values from 0.5 to 1.5
- ln1_bias: float32 [2048], replicated, may hold values from -1.75 to 1.75
- w_qkv: bfloat16 [3, 2048, 2048], P(None, None, 'tp'), may hold values from -0.1875 to 0.1875
- w_out: bfloat16 [2048, 2048], P('tp'), may hold values from -0.5 to 0.5
- ln2_gain: float32 [2048], replicated, may hold values from 0.5 to 1.5
- ln2_bias: float32 [2048], replicated, may hold values from -1.75 to 1.75
- w_up: bfloat16 [2048, 8192], P(None, 'tp'), may hold values from -0.125 to 0.125
- w_down: bfloat16 [8192, 2048], P('tp'), may hold values from -0.0625 to 0.0625
- buckets: int32 [4096], P('blk'), may hold values from 0 to 3
- lengths: int32 [3], replicated, may hold values from 256 to 2048, as said below
- block_order: int32 [16], replicated, may hold values from 0 to 15, as said below
- grad_out: bfloat16 [4096, 2048], P('blk'), may hold values from -6 to 6
Outputs:
- layer_output: bfloat16 [4096, 2048], P('blk')
- grad_input: float32 [4096, 2048], P('blk')
- grad_ln1_gain: float32 [2048], replicated
- grad_ln1_bias: float32 [2048], replicated
- grad_qkv: float32 [3, 2048, 2048], P(None, 'blk', 'tp')
- grad_w_out: float32 [2048, 2048], P('tp', 'blk')
- grad_ln2_gain: float32 [2048], replicated
- grad_ln2_bias: float32 [2048], replicated
- grad_up: float32 [2048, 8192], P('blk', 'tp')
- grad_down: float32 [8192, 2048], P('tp', 'blk')
- bucket_counts: int32 [4], replicated
The draws below stay inside these ranges and needn't reach their ends.
Inputs may be any that keep to these rules, and one draw needn't show every extreme that they name: 3 lengths in packed order summing to 4096; exactly one is 2048, and its document holds tokens of the first, the middle and the last device of blk. a permutation of the 2 * 8 blocks of 256 packed positions; device d of blk holds block_order[2 d] and then block_order[2 d + 1].
All inputs are finite; a program needn't handle non-finite values.
Results may differ from the reference program's by a relative error of at most 0.028.
Values may be sent and summed in bfloat16 or wider, within the bound.
No kernel may reach another device: no remote copies, remote signals or barrier semaphores. Data moves between devices by JAX's collectives and lax.ppermute only.
A program may use at most 256 MiB of HBM per device.

```python
import math
import jax
import jax.numpy as jnp
from jax import lax

D = 2048
H = 16
HD = 128
FF = 8192
NB = 4
TOK_DEV = 512
MINLEN = 256
TOKENS = 4096
MAXLEN = 2048


def packing(key):
    pair_count = TOKENS // MAXLEN - 1
    span_room = MAXLEN - 2 * MINLEN
    keys = jax.random.split(key, 5)
    first_draw = jax.random.randint(keys[0], (pair_count,), 0, span_room + 1)
    second_draw = jax.random.randint(keys[1], (pair_count,), 0, span_room + 1)
    shorter = MINLEN + first_draw * second_draw // span_room
    flips = jax.random.randint(keys[2], (pair_count,), 0, 2)
    leading = jnp.where(flips == 1, shorter, MAXLEN - shorter)
    trailing = MAXLEN - leading
    paired = jnp.stack([leading, trailing], axis=1).reshape(-1)
    long_slot = jax.random.randint(keys[3], (), 0, 2 * pair_count + 1)
    doc_ids = jnp.arange(2 * pair_count + 1, dtype=jnp.int32)
    source = jnp.clip(jnp.where(doc_ids > long_slot, doc_ids - 1, doc_ids), 0, 2 * pair_count - 1)
    lengths = jnp.where(doc_ids == long_slot, MAXLEN, paired[source]).astype(jnp.int32)
    begin = jnp.sum(jnp.where(doc_ids < long_slot, lengths, 0)).astype(jnp.int32)
    block_len = TOK_DEV // 2
    block_total = TOKENS // block_len
    first_full = (begin + block_len - 1) // block_len
    last_full = (begin + MAXLEN) // block_len - 1
    middle_full = (first_full + last_full) // 2
    order = jax.random.permutation(keys[4], block_total).astype(jnp.int32)
    device_total = block_total // 2
    for slot_at, wanted in ((0, first_full), (2 * (device_total // 2), middle_full), (block_total - 1, last_full)):
        found = jnp.argmax(order == wanted).astype(jnp.int32)
        held = order[slot_at]
        order = order.at[found].set(held)
        order = order.at[slot_at].set(wanted)
    return (lengths, order)


def draw_lengths(key, part):
    shared = packing(key)
    return shared[0]


def draw_block_order(key, part):
    shared = packing(key)
    return shared[1]


def plant(drawn, own_key, least, largest):
    index_at = [jax.random.randint(jax.random.fold_in(own_key, axis), (), 0, length) for axis, length in enumerate(drawn.shape)]
    main_axis = drawn.shape.index(max(drawn.shape))
    next_to = index_at[:main_axis] + [(index_at[main_axis] + 1) % drawn.shape[main_axis]] + index_at[main_axis + 1:]
    return drawn.at[tuple(index_at)].set(least).at[tuple(next_to)].set(largest)


def block_scale(own_key, shape, pieces, least, high):
    def one(axis_at, shards_of):
        heights = jax.random.uniform(jax.random.fold_in(jax.random.fold_in(own_key, 6), axis_at), (shards_of,), jnp.float32, least / len(pieces), high / len(pieces))
        return jnp.repeat(jnp.exp(heights), shape[axis_at] // shards_of).reshape((-1,) + (1,) * (len(shape) - axis_at - 1))

    level = one(*pieces[0])
    for cut in pieces[1:]:
        level = level * one(*cut)
    return level


def gaussian(stream_key, shape, width, bound, shards=(), held_as=jnp.bfloat16):
    factor_of = block_scale(stream_key, shape, shards, -0.22, 0.18) if shards else 1.0
    values = jax.random.normal(stream_key, shape, jnp.float32) * width * factor_of
    return jnp.minimum(jnp.maximum(values, -bound), bound).astype(held_as)


def setup_inputs(seed: int = 0) -> dict:
    arg_keys = jax.random.split(jax.random.key(seed), 14)
    return {
        "layer_input": gaussian(arg_keys[0], (TOKENS, D), 1.0, 6.0, ((0, 8),)),
        "ln1_gain": jnp.clip(1.0 + 0.1 * jax.random.normal(arg_keys[1], (D,), jnp.float32), 0.5, 1.5),
        "ln1_bias": gaussian(arg_keys[2], (D,), 0.3, 1.75, (), jnp.float32),
        "w_qkv": gaussian(arg_keys[3], (3, D, D), (D // 2) ** -0.5, 0.1875, ((2, 4),)),
        "w_out": gaussian(arg_keys[4], (D, D), (D // 16) ** -0.5, 0.5, ((0, 4),)),
        "ln2_gain": jnp.clip(1.0 + 0.1 * jax.random.normal(arg_keys[5], (D,), jnp.float32), 0.5, 1.5),
        "ln2_bias": gaussian(arg_keys[6], (D,), 0.3, 1.75, (), jnp.float32),
        "w_up": gaussian(arg_keys[7], (D, FF), D ** -0.5, 0.125, ((1, 4),)),
        "w_down": gaussian(arg_keys[8], (FF, D), FF ** -0.5, 0.0625, ((0, 4),)),
        "buckets": plant(jax.random.randint(arg_keys[9], (TOKENS,), 0, NB), jax.random.fold_in(arg_keys[9], 1), 0, NB - 1).astype(jnp.int32),
        "lengths": draw_lengths(jax.random.fold_in(arg_keys[13], 71), 0),
        "block_order": draw_block_order(jax.random.fold_in(arg_keys[13], 71), 0),
        "grad_out": gaussian(arg_keys[12], (TOKENS, D), 1.0, 6.0, ((0, 8),)),
    }


EPSILON = 1e-05
ROPE_BASE = 10000.0
HIGHEST = lax.Precision.HIGHEST

@jax.custom_vjp
def low(v):
    return lax.optimization_barrier(v.astype(jnp.bfloat16)).astype(jnp.float32)

@jax.custom_vjp
def low_back(v):
    return v

def low_keep(v):
    return (low(v), None)

def low_pass(kept, grad):
    return (grad,)

def back_keep(v):
    return (v, None)

def back_low(kept, grad):
    return (low(grad),)
low.defvjp(low_keep, low_pass)
low_back.defvjp(back_keep, back_low)

def layer_norm(values, gain, bias):
    centre = values - lax.optimization_barrier(jnp.mean(values, axis=-1, keepdims=True))
    spread = lax.optimization_barrier(jnp.mean(centre * centre, axis=-1, keepdims=True))
    return centre * lax.rsqrt(spread + EPSILON) * gain + bias

def rotate(values, cosine, sine):
    half_dim = HD // 2
    first_half = values[..., :half_dim]
    second_half = values[..., half_dim:]
    return jnp.concatenate([first_half * cosine - second_half * sine, second_half * cosine + first_half * sine], axis=-1)

def reference(layer_input, ln1_gain, ln1_bias, w_qkv, w_out, ln2_gain, ln2_bias, w_up, w_down, buckets, lengths, block_order, grad_out):
    block_len = TOK_DEV // 2
    row_ids = jnp.arange(TOKENS, dtype=jnp.int32)
    places = (block_order[row_ids // block_len] * block_len + row_ids % block_len).astype(jnp.int32)
    device_row = jnp.zeros((TOKENS,), jnp.int32).at[places].set(row_ids)
    packed_input = layer_input[device_row].astype(jnp.float32)
    packed_grad = grad_out[device_row].astype(jnp.float32)
    packed_buckets = buckets[device_row]
    starts = (jnp.cumsum(lengths) - lengths).astype(jnp.int32)
    packed_pos = jnp.arange(TOKENS, dtype=jnp.int32)
    firsts = lax.optimization_barrier(jnp.max(jnp.where(starts[None, :] <= packed_pos[:, None], starts[None, :], 0), axis=1)).astype(jnp.int32)
    freqs = ROPE_BASE ** (-(jnp.arange(HD // 2, dtype=jnp.float32) * 2.0 / HD))
    angles = (packed_pos - firsts).astype(jnp.float32)[:, None] * freqs[None, :]
    cosine = jnp.cos(angles)[:, None, :]
    sine = jnp.sin(angles)[:, None, :]
    units = jnp.arange(FF, dtype=jnp.int32)
    unit_mask = (units[None, :] < (packed_buckets[:, None] + 1) * (FF // NB)).astype(jnp.float32)
    q_block = min(512, MAXLEN)
    key_span = MAXLEN + q_block
    scale = 1.0 / math.sqrt(HD)

    def attend(queries, keys, values):

        def one_block(blk_index):
            q_start = blk_index * q_block
            k_start = jnp.clip(q_start + q_block - key_span, 0, TOKENS - key_span).astype(jnp.int32)
            q_rows = lax.dynamic_slice_in_dim(queries, q_start, q_block, 0)
            k_rows = lax.dynamic_slice_in_dim(keys, k_start, key_span, 0)
            v_rows = lax.dynamic_slice_in_dim(values, k_start, key_span, 0)
            q_first = lax.dynamic_slice_in_dim(firsts, q_start, q_block, 0)
            k_first = lax.dynamic_slice_in_dim(firsts, k_start, key_span, 0)
            q_place = q_start + jnp.arange(q_block, dtype=jnp.int32)
            k_place = k_start + jnp.arange(key_span, dtype=jnp.int32)
            visible = (k_first[None, :] == q_first[:, None]) & (k_place[None, :] <= q_place[:, None])
            scores = jnp.einsum('qhd,khd->hqk', q_rows, k_rows, precision=HIGHEST) * scale
            scores = low_back(scores)
            scores = jnp.where(visible[None], scores, -1e+30)
            weights = jax.nn.softmax(scores, axis=-1)
            return jnp.einsum('hqk,khd->qhd', low(weights), v_rows, precision=HIGHEST)
        blocks = lax.map(jax.checkpoint(one_block), jnp.arange(TOKENS // q_block, dtype=jnp.int32))
        return blocks.reshape(TOKENS, D)

    def forward(x_in, gain_one, bias_one, qkv_weight, out_weight, gain_two, bias_two, up_weight, down_weight):
        h_one = low(layer_norm(x_in, gain_one, bias_one))
        projected = jnp.einsum('td,sde->ste', h_one, qkv_weight, precision=HIGHEST)
        q_pre = low_back(projected[0]).reshape(TOKENS, H, HD)
        k_pre = low_back(projected[1]).reshape(TOKENS, H, HD)
        v_pre = low_back(projected[2]).reshape(TOKENS, H, HD)
        queries = low(rotate(q_pre, cosine, sine))
        keys = low(rotate(k_pre, cosine, sine))
        values = low(v_pre)
        attended = low(low_back(attend(queries, keys, values)))
        branch = low_back(jnp.dot(attended, out_weight, precision=HIGHEST))
        x_mid = x_in + branch
        h_two = low(layer_norm(x_mid, gain_two, bias_two))
        up_val = low_back(jnp.dot(h_two, up_weight, precision=HIGHEST))
        relu_up = jnp.maximum(up_val, 0.0)
        act = low(relu_up * relu_up * unit_mask)
        feed = low_back(jnp.dot(act, down_weight, precision=HIGHEST))
        return x_mid + feed
    params = (packed_input, ln1_gain.astype(jnp.float32), ln1_bias.astype(jnp.float32), w_qkv.astype(jnp.float32), w_out.astype(jnp.float32), ln2_gain.astype(jnp.float32), ln2_bias.astype(jnp.float32), w_up.astype(jnp.float32), w_down.astype(jnp.float32))
    result, pullback = jax.vjp(forward, *params)
    grads = pullback(packed_grad)
    layer_output = result[places].astype(jnp.bfloat16)
    grad_input = grads[0][places]
    counts = lax.optimization_barrier(jnp.sum((buckets[:, None] == jnp.arange(NB, dtype=jnp.int32)[None, :]).astype(jnp.int32), axis=0)).astype(jnp.int32)
    return (layer_output, grad_input, grads[1], grads[2], grads[3], grads[4], grads[5], grads[6], grads[7], grads[8], counts)
```

```python
import functools
import math

import jax
import jax.numpy as jnp
from jax import lax
from jax.experimental import pallas as pl
from jax.experimental.pallas import tpu as pltpu
from jax.sharding import Mesh
from jax.sharding import PartitionSpec as P

HD = 128
FF = 8192
NB = 4
HEADS = 4
EPSILON = 1e-05
ROPE_BASE = 10000.0
SWAP = [(0, 1), (1, 0)]
BLK = ("r", "h", "y")
TP = ("x", "c")
F32 = jnp.float32
BF16 = jnp.bfloat16


def swap(value, axis):
    return lax.ppermute(value, axis, SWAP)


def ordered(first, second):
    return lax.optimization_barrier((first, second))


def rotary_tables(positions):
    freqs = ROPE_BASE ** (-(jnp.arange(HD // 2, dtype=F32) * 2.0 / HD))
    angles = positions.astype(F32)[:, None] * freqs[None, :]
    return (jnp.cos(angles), jnp.sin(angles))


def rotate(values, cosine, sine):
    first_half, second_half = values[..., : HD // 2], values[..., HD // 2 :]
    return jnp.concatenate(
        [first_half * cosine - second_half * sine, second_half * cosine + first_half * sine],
        axis=-1,
    )


def norm_parts(values):
    centre = values - jnp.mean(values, axis=-1, keepdims=True)
    inverse = lax.rsqrt(jnp.mean(centre * centre, axis=-1, keepdims=True) + EPSILON)
    return (centre * inverse, inverse)


def layer_norm_back(grad, normed, inverse, gain):
    grad_normed = grad * gain
    grad_in = inverse * (
        grad_normed
        - jnp.mean(grad_normed, axis=-1, keepdims=True)
        - normed * jnp.mean(grad_normed * normed, axis=-1, keepdims=True)
    )
    return (grad_in, jnp.sum(grad * normed, axis=0), jnp.sum(grad, axis=0))


def nt(lhs, rhs):
    return lax.dot_general(lhs, rhs, (((1,), (1,)), ((), ())), preferred_element_type=F32)


def tn(lhs, rhs):
    return lax.dot_general(lhs, rhs, (((0,), (0,)), ((), ())), preferred_element_type=F32)


def nn(lhs, rhs):
    return lax.dot_general(lhs, rhs, (((1,), (0,)), ((), ())), preferred_element_type=F32)


def visible_of(tile, key_block, query_places, query_firsts):
    key_places = key_block * tile + lax.broadcasted_iota(jnp.int32, (tile, 1), 0)
    return (key_places <= query_places) & (key_places >= query_firsts)


def attend_kernel(tile, scale, at_ref, low_ref, row_ref, q_ref, first_ref, kv_ref, o_ref, lse_ref):
    lanes = lax.broadcasted_iota(jnp.int32, (1, tile), 1)

    def one_block(i, carry):
        rows = pl.ds(pl.multiple_of(i * tile, tile), tile)
        queries = q_ref[rows, :HD]
        firsts = first_ref[i]
        places = at_ref[i] * tile + lanes

        def one_step(b, state):
            run_max, run_sum, run_acc = state
            krows = pl.ds(pl.multiple_of(row_ref[b] * tile, tile), tile)
            scores = nt(kv_ref[krows, :HD], queries) * scale
            visible = visible_of(tile, b, places, firsts)
            scores = jnp.where(visible, scores, -1e30)
            new_max = jnp.maximum(run_max, jnp.max(scores, axis=0, keepdims=True))
            factor = jnp.exp(run_max - new_max)
            probs = jnp.where(visible, jnp.exp(scores - new_max), 0.0)
            new_sum = run_sum * factor + jnp.sum(probs, axis=0, keepdims=True)
            new_acc = run_acc * factor + tn(kv_ref[krows, HD:], probs.astype(BF16))
            return (new_max, new_sum, new_acc)

        run_max, run_sum, run_acc = lax.fori_loop(
            low_ref[i],
            at_ref[i] + 1,
            one_step,
            (
                jnp.full((1, tile), -1e30, F32),
                jnp.zeros((1, tile), F32),
                jnp.zeros((HD, tile), F32),
            ),
        )
        o_ref[rows, :] = (run_acc / run_sum).T.astype(BF16)
        lse_ref[i] = run_max + jnp.log(run_sum)
        return carry

    lax.fori_loop(0, q_ref.shape[0] // tile, one_block, 0)


def attend_back_kernel(
    tile,
    scale,
    at_ref,
    low_ref,
    row_ref,
    q_ref,
    first_ref,
    kv_ref,
    o_ref,
    lse_ref,
    do_ref,
    dq_ref,
    dkv_ref,
    far_ref,
    acc_ref,
):
    lanes = lax.broadcasted_iota(jnp.int32, (1, tile), 1)
    acc_ref[...] = jnp.zeros_like(acc_ref)

    def one_block(i, carry):
        rows = pl.ds(pl.multiple_of(i * tile, tile), tile)
        queries = q_ref[rows, :HD]
        grads = do_ref[rows, :]
        firsts = first_ref[i]
        places = at_ref[i] * tile + lanes
        log_sums = lse_ref[i]
        products = grads.astype(F32) * o_ref[rows, :].astype(F32)
        deltas = jnp.sum(products.T, axis=0, keepdims=True)

        def one_step(b, grad_q):
            krows = pl.ds(pl.multiple_of(row_ref[b] * tile, tile), tile)
            keys = kv_ref[krows, :HD]
            scores = nt(keys, queries) * scale
            visible = visible_of(tile, b, places, firsts)
            probs = jnp.where(visible, jnp.exp(scores - log_sums), 0.0)
            grad_probs = nt(kv_ref[krows, HD:], grads)
            grad_scores = (probs * (grad_probs - deltas)).astype(BF16)
            acc_ref[krows, HD:] += nn(probs.astype(BF16), grads)
            acc_ref[krows, :HD] += nn(grad_scores, queries)
            return grad_q + tn(keys, grad_scores)

        grad_q = lax.fori_loop(low_ref[i], at_ref[i] + 1, one_step, jnp.zeros((HD, tile), F32))
        dq_ref[rows, :] = (grad_q * scale).T
        return carry

    lax.fori_loop(0, q_ref.shape[0] // tile, one_block, 0)
    near = dkv_ref.shape[0]
    dkv_ref[:, :HD] = acc_ref[:near, :HD] * scale
    dkv_ref[:, HD:] = acc_ref[:near, HD:]
    far_ref[:, :HD] = (acc_ref[near:, :HD] * scale).astype(BF16)
    far_ref[:, HD:] = acc_ref[near:, HD:].astype(BF16)


SMEM = pl.BlockSpec(memory_space=pltpu.SMEM)
VMEM = pl.BlockSpec(memory_space=pltpu.VMEM)


def attend(tile, scale, at, low, row, queries, firsts, keys_values):
    rows = queries.shape[0]
    return pl.pallas_call(
        functools.partial(attend_kernel, tile, scale),
        out_shape=(
            jax.ShapeDtypeStruct((rows, HD), BF16),
            jax.ShapeDtypeStruct((rows // tile, 1, tile), F32),
        ),
        in_specs=[SMEM] * 3 + [VMEM] * 3,
        out_specs=(VMEM, VMEM),
        compiler_params=pltpu.CompilerParams(vmem_limit_bytes=40 * 2**20),
        cost_estimate=pl.CostEstimate(
            flops=4 * rows * 1280 * HD, bytes_accessed=4 * 2**20, transcendentals=rows * 1280
        ),
        name="attend",
    )(at, low, row, queries, firsts, keys_values)


def attend_back(tile, scale, at, low, row, queries, firsts, keys_values, outs, lse, grads):
    rows = queries.shape[0]
    near = keys_values.shape[0] // 2
    return pl.pallas_call(
        functools.partial(attend_back_kernel, tile, scale),
        out_shape=(
            jax.ShapeDtypeStruct((rows, HD), F32),
            jax.ShapeDtypeStruct((near, 2 * HD), F32),
            jax.ShapeDtypeStruct((near, 2 * HD), BF16),
        ),
        in_specs=[SMEM] * 3 + [VMEM] * 6,
        out_specs=(VMEM, VMEM, VMEM),
        scratch_shapes=[pltpu.VMEM(keys_values.shape, F32)],
        compiler_params=pltpu.CompilerParams(vmem_limit_bytes=50 * 2**20),
        cost_estimate=pl.CostEstimate(
            flops=10 * rows * 1280 * HD, bytes_accessed=8 * 2**20, transcendentals=rows * 1280
        ),
        name="attend_back",
    )(at, low, row, queries, firsts, keys_values, outs, lse, grads)


def body(
    depth,
    layer_input,
    ln1_gain,
    ln1_bias,
    w_qkv,
    w_out,
    ln2_gain,
    ln2_bias,
    w_up,
    w_down,
    buckets,
    lengths,
    block_order,
    grad_out,
):
    tok, dim = layer_input.shape
    head_cols = w_qkv.shape[2]
    ffn_here = w_up.shape[1]
    half = tok // 2
    outer = HEADS * depth
    scale = 1.0 / math.sqrt(HD)
    r, h, y, c = (lax.axis_index(a) for a in ("r", "h", "y", "c"))
    blk = lax.axis_index(BLK)

    def parity(values, which):
        split = values.reshape(tok, outer, 2, dim // (2 * outer))
        return lax.dynamic_index_in_dim(split, which, 2, keepdims=False).reshape(tok, dim // 2)

    def my_half(values):
        return lax.dynamic_slice_in_dim(values, c * half, half, 0)

    def other_half(values):
        return lax.dynamic_slice_in_dim(values, (1 - c) * half, half, 0)

    def join_halves(mine):
        other = swap(mine, "c")
        return jnp.where(
            c == 0, jnp.concatenate([mine, other]), jnp.concatenate([other, mine])
        )

    def reduce_tp(part):
        got = swap(other_half(part), "c")
        chip = (my_half(part).astype(F32) + got.astype(F32)).astype(BF16)
        return chip.astype(F32) + swap(chip, "x").astype(F32)

    starts = jnp.cumsum(lengths) - lengths

    def firsts_of(places):
        return jnp.max(jnp.where(starts <= places[..., None], starts, 0), axis=-1)

    inside = jnp.arange(half, dtype=jnp.int32)
    own_places = (
        lax.dynamic_slice_in_dim(block_order, 2 * blk, 2, 0)[:, None] * half + inside
    ).reshape(tok)
    cosine, sine = rotary_tables(own_places - firsts_of(own_places))
    group_order = lax.dynamic_slice_in_dim(
        block_order.reshape(depth, HEADS, 2, 2), r, 1, 0
    )
    query_at = lax.dynamic_slice_in_dim(group_order, y, 1, 2).reshape(2 * HEADS)
    query_places = query_at[:, None] * half + inside
    query_firsts = firsts_of(query_places)
    query_low = query_firsts[:, 0] // half
    block_count = block_order.shape[0]
    slots = jnp.argmax(
        block_order[None, :] == jnp.arange(block_count, dtype=jnp.int32)[:, None], axis=1
    ).astype(jnp.int32)
    slot_dev = slots // 2
    key_row = jnp.where(slot_dev % 2 == y, 0, block_count // 2) + slot_dev // 2 * 2 + slots % 2
    group_cos, group_sin = rotary_tables((query_places - query_firsts).reshape(2 * HEADS * half))

    grad_near = parity(grad_out, y)
    grad_far = swap(parity(grad_out, 1 - y), "y")

    input_float = layer_input.astype(F32)
    normed_one, _ = norm_parts(input_float)
    h_one = (normed_one * ln1_gain + ln1_bias).astype(BF16)
    projected = jnp.einsum(
        "td,sdhe->shte", h_one, w_qkv.reshape(3, dim, HEADS, HD), preferred_element_type=F32
    )
    packed = jnp.concatenate(
        [
            rotate(projected[0], cosine, sine).astype(BF16),
            rotate(projected[1], cosine, sine).astype(BF16),
            projected[2].astype(BF16),
        ],
        axis=-1,
    )
    packed = lax.all_to_all(packed, "h", 0, 0, tiled=True)
    packed = packed.reshape(HEADS * tok, 3 * HD)
    near_kv = packed[:, HD:]
    if depth > 1:
        near_kv = lax.all_gather(near_kv, "r", axis=0, tiled=True)
    far_kv = swap(near_kv, "y")
    all_kv = jnp.concatenate([near_kv, far_kv], axis=0)
    first_rows = query_firsts.reshape(2 * HEADS, 1, half)
    attended, lse = attend(
        half, scale, query_at, query_low, key_row, packed, first_rows, all_kv
    )
    heads_out = lax.all_to_all(attended.reshape(HEADS, tok, HD), "h", 0, 0, tiled=True)
    attended_flat = heads_out.transpose(1, 0, 2).reshape(tok, head_cols)
    part = jnp.dot(attended_flat, w_out, preferred_element_type=F32).astype(BF16)
    branch = reduce_tp(part)
    x_mid = my_half(input_float) + branch
    normed_two, inverse_two = norm_parts(x_mid)
    h_two = join_halves((normed_two * ln2_gain + ln2_bias).astype(BF16))

    up_val = jnp.dot(h_two, w_up, preferred_element_type=F32)
    units = lax.axis_index(TP) * ffn_here + jnp.arange(ffn_here, dtype=jnp.int32)
    unit_mask = (units[None, :] < (buckets[:, None] + 1) * (FF // NB)).astype(F32)
    relu_up = jnp.maximum(up_val, 0.0) * unit_mask
    act = (relu_up * relu_up).astype(BF16)
    grad_act = nt(grad_out, w_down)
    grad_upval = (grad_act * 2.0 * relu_up).astype(BF16)
    act_far = swap(act, "y")
    h_one_far = swap(parity(h_one, 1 - y), "y")
    h_two_far = swap(parity(h_two, 1 - y), "y")
    att_far = swap(attended_flat, "y")

    def pair_product(near, far, cols_near, cols_far):
        return tn(jnp.concatenate([near, far]), jnp.concatenate([cols_near, cols_far]))

    def scatter(values, dimension):
        return lax.psum_scatter(
            values.astype(BF16), ("r", "h"), scatter_dimension=dimension, tiled=True
        ).astype(F32)

    grad_h_two = reduce_tp(nt(grad_upval, w_up).astype(BF16))
    down_part = scatter(pair_product(act, act_far, grad_near, grad_far), 1)
    grad_mid_ln, gain_two_grad, bias_two_grad = layer_norm_back(
        grad_h_two, normed_two, inverse_two, ln2_gain
    )
    grad_mid = my_half(grad_out).astype(F32) + grad_mid_ln
    grad_branch = join_halves(grad_mid.astype(BF16))
    grad_att = jnp.einsum(
        "td,hcd->htc", grad_branch, w_out.reshape(HEADS, HD, dim), preferred_element_type=F32
    ).astype(BF16)
    grad_att = lax.all_to_all(grad_att, "h", 0, 0, tiled=True).reshape(HEADS * tok, HD)
    grad_up_far = swap(grad_upval, "y")
    up_part = scatter(
        pair_product(parity(h_two, y), h_two_far, grad_upval, grad_up_far), 0
    )
    feed = reduce_tp(jnp.dot(act, w_down, preferred_element_type=F32).astype(BF16))
    layer_output = join_halves((x_mid + feed).astype(BF16))
    branch_far = swap(parity(grad_branch, 1 - y), "y")
    wout_part = scatter(
        pair_product(attended_flat, att_far, parity(grad_branch, y), branch_far), 1
    )

    grad_q, grad_kv, grad_kv_far = attend_back(
        half, scale, query_at, query_low, key_row, packed, first_rows, all_kv, attended, lse, grad_att
    )
    grad_kv = grad_kv + swap(grad_kv_far, "y").astype(F32)
    if depth > 1:
        grad_kv = lax.psum_scatter(grad_kv, "r", scatter_dimension=0, tiled=True)
    grad_packed = jnp.concatenate(
        [
            rotate(grad_q, group_cos, -group_sin).astype(BF16),
            rotate(grad_kv[:, :HD], group_cos, -group_sin).astype(BF16),
            grad_kv[:, HD:].astype(BF16),
        ],
        axis=-1,
    )
    grad_packed = lax.all_to_all(
        grad_packed.reshape(HEADS, tok, 3 * HD), "h", 0, 0, tiled=True
    )
    grad_proj = (
        grad_packed.reshape(HEADS, tok, 3, HD).transpose(1, 2, 0, 3).reshape(tok, 3, head_cols)
    )
    grad_h_one = reduce_tp(
        jnp.einsum("tse,sde->td", grad_proj, w_qkv, preferred_element_type=F32).astype(BF16)
    )
    proj_far = swap(grad_proj, "y")
    qkv_part = scatter(
        jnp.einsum(
            "td,tse->sde",
            jnp.concatenate([parity(h_one, y), h_one_far]),
            jnp.concatenate([grad_proj, proj_far]),
            preferred_element_type=F32,
        ),
        1,
    )
    normed_own, inverse_own = norm_parts(my_half(input_float))
    grad_in_ln, gain_one_grad, bias_one_grad = layer_norm_back(
        grad_h_one, normed_own, inverse_own, ln1_gain
    )
    grad_input = join_halves((grad_mid + grad_in_ln).astype(BF16)).astype(F32)
    local_counts = jnp.sum(
        (my_half(buckets)[:, None] == jnp.arange(NB, dtype=jnp.int32)[None, :]).astype(F32), axis=0
    )
    sums = lax.psum(
        jnp.concatenate(
            [gain_one_grad, bias_one_grad, gain_two_grad, bias_two_grad, local_counts]
        ),
        BLK + ("c",),
    )
    return (
        layer_output,
        grad_input,
        sums[:dim],
        sums[dim : 2 * dim],
        qkv_part,
        wout_part,
        sums[2 * dim : 3 * dim],
        sums[3 * dim : 4 * dim],
        up_part,
        down_part,
        sums[4 * dim :].astype(jnp.int32),
    )


def solution(mesh):
    depth = mesh.shape["blk"] // (2 * HEADS)
    fine = Mesh(mesh.devices.reshape(depth, HEADS, 2, 2, 2), BLK + TP)
    return jax.shard_map(
        functools.partial(body, depth),
        mesh=fine,
        in_specs=(
            P(BLK, None),
            P(),
            P(),
            P(None, None, TP),
            P(TP, None),
            P(),
            P(),
            P(None, TP),
            P(TP, None),
            P(BLK),
            P(),
            P(),
            P(BLK, None),
        ),
        out_specs=(
            P(BLK, None),
            P(BLK, None),
            P(),
            P(),
            P(None, BLK, TP),
            P(TP, BLK),
            P(),
            P(),
            P(BLK, TP),
            P(TP, BLK),
            P(),
        ),
        check_vma=False,
    )
```

```python
import functools
import math

import jax
import jax.numpy as jnp
from jax import lax
from jax.experimental import pallas as pl
from jax.experimental.pallas import tpu as pltpu
from jax.sharding import Mesh
from jax.sharding import PartitionSpec as P

HD = 128
FF = 8192
NB = 4
HEADS = 4
EPSILON = 1e-05
ROPE_BASE = 10000.0
BLK = ("r", "h", "y")
TP = ("x", "c")
F32 = jnp.float32
BF16 = jnp.bfloat16
SMEM = pl.BlockSpec(memory_space=pltpu.SMEM)
VMEM = pl.BlockSpec(memory_space=pltpu.VMEM)


def swap(value, axis):
    return lax.ppermute(value, axis, [(0, 1), (1, 0)])


def plane_swap(value, k):
    return lax.ppermute(value, "h", [(i, i ^ k) for i in range(HEADS)])


def ordered(*values):
    return lax.optimization_barrier(values)


def nt(lhs, rhs):
    return lax.dot_general(lhs, rhs, (((1,), (1,)), ((), ())), preferred_element_type=F32)


def tn(lhs, rhs):
    return lax.dot_general(lhs, rhs, (((0,), (0,)), ((), ())), preferred_element_type=F32)


def nn(lhs, rhs):
    return lax.dot_general(lhs, rhs, (((1,), (0,)), ((), ())), preferred_element_type=F32)


def params(mib, **more):
    return pltpu.CompilerParams(vmem_limit_bytes=mib * 2**20, **more)


def cost(flops, moved):
    return pl.CostEstimate(flops=int(flops), bytes_accessed=int(moved), transcendentals=0)


def whole(shape):
    return pl.BlockSpec(shape, lambda *_: (0,) * len(shape))


def normalise(values):
    centre = values - jnp.mean(values, axis=-1, keepdims=True)
    inverse = lax.rsqrt(jnp.mean(centre * centre, axis=-1, keepdims=True) + EPSILON)
    return (centre * inverse, inverse)


def rotary_tables(positions):
    freqs = ROPE_BASE ** (-(jnp.arange(HD // 2, dtype=F32) * 2.0 / HD))
    angles = positions.astype(F32)[:, None] * freqs[None, :]
    cosine, sine = jnp.cos(angles), jnp.sin(angles)
    return (
        jnp.concatenate([cosine, cosine], axis=-1),
        jnp.concatenate([-sine, sine], axis=-1),
    )


def rotate(values, cosine, sine):
    return values * cosine + pltpu.roll(values, HD // 2, 1) * sine


def project_kernel(idx, x_ref, gain_ref, bias_ref, cos_ref, sin_ref, w_ref, *refs):
    outs, h_ref = refs[:HEADS], refs[HEADS]
    step = pl.program_id(0)

    @pl.when(step == 0)
    def _():
        normed, _ = normalise(x_ref[...].astype(F32))
        h_ref[...] = (normed * gain_ref[...] + bias_ref[...]).astype(BF16)

    both = nn(h_ref[...], jnp.concatenate([w_ref[0], w_ref[1]], axis=1))
    cosine, sine = cos_ref[...], sin_ref[...]
    queries = rotate(both[:, :HD], cosine, sine).astype(BF16)
    keys = rotate(both[:, HD:], cosine, sine).astype(BF16)
    values = nn(h_ref[...], w_ref[2]).astype(BF16)
    for k, out in enumerate(outs):

        @pl.when(step == k)
        def _(out=out):
            out[:, :HD] = queries
            out[:, HD : 2 * HD] = keys
            out[:, 2 * HD :] = values


def project(idx, x, gain, bias, cosine, sine, w_qkv):
    tok, dim = x.shape
    return pl.pallas_call(
        project_kernel,
        grid_spec=pltpu.PrefetchScalarGridSpec(
            num_scalar_prefetch=1,
            grid=(HEADS,),
            in_specs=[
                whole((tok, dim)),
                whole((1, dim)),
                whole((1, dim)),
                whole((tok, HD)),
                whole((tok, HD)),
                pl.BlockSpec((3, dim, HD), lambda k, idx: (0, 0, idx[0] ^ k)),
            ],
            out_specs=[whole((tok, 3 * HD))] * HEADS,
            scratch_shapes=[pltpu.VMEM((tok, dim), BF16)],
        ),
        out_shape=[jax.ShapeDtypeStruct((tok, 3 * HD), BF16)] * HEADS,
        compiler_params=params(40),
        cost_estimate=cost(2 * tok * dim * 12 * HD, 10 * 2**20),
        name="project",
    )(idx, x, gain, bias, cosine, sine, w_qkv)


def visible_of(tile, key_block, query_places, query_firsts):
    key_places = key_block * tile + lax.broadcasted_iota(jnp.int32, (tile, 1), 0)
    return (key_places <= query_places) & (key_places >= query_firsts)


def gather_refs(q_refs, kv_refs, lane0s, q_all, kv_all):
    at = 0
    for ref in q_refs:
        q_all[at : at + ref.shape[0], :] = ref[:, :HD]
        at += ref.shape[0]
    at = 0
    for ref, lane0 in zip(kv_refs, lane0s, strict=True):
        kv_all[at : at + ref.shape[0], :] = ref[:, lane0 : lane0 + 2 * HD]
        at += ref.shape[0]


def attend_kernel(tile, scale, lane0s, near_is_q, at_ref, low_ref, row_ref, first_ref, *refs):
    n_kv = len(lane0s)
    q_refs = refs[:HEADS]
    kv_refs = refs[:n_kv] if near_is_q else refs[HEADS : HEADS + n_kv]
    n_in = n_kv if near_is_q else HEADS + n_kv
    outs = refs[n_in : n_in + HEADS]
    lse_ref, q_all, kv_all = refs[n_in + HEADS :]
    gather_refs(q_refs, kv_refs, lane0s, q_all, kv_all)
    lanes = lax.broadcasted_iota(jnp.int32, (1, tile), 1)
    per_out = outs[0].shape[0] // tile

    for k, out in enumerate(outs):

        def one_block(j, carry, k=k, out=out):
            i = k * per_out + j
            queries = q_all[pl.ds(pl.multiple_of(i * tile, tile), tile), :]
            firsts = first_ref[i]
            places = at_ref[i] * tile + lanes

            def one_step(b, state):
                run_max, run_sum, run_acc = state
                krows = pl.ds(pl.multiple_of(row_ref[b] * tile, tile), tile)
                scores = nt(kv_all[krows, :HD], queries) * scale
                visible = visible_of(tile, b, places, firsts)
                scores = jnp.where(visible, scores, -1e30)
                new_max = jnp.maximum(run_max, jnp.max(scores, axis=0, keepdims=True))
                factor = jnp.exp(run_max - new_max)
                probs = jnp.where(visible, jnp.exp(scores - new_max), 0.0)
                new_sum = run_sum * factor + jnp.sum(probs, axis=0, keepdims=True)
                new_acc = run_acc * factor + tn(kv_all[krows, HD:], probs.astype(BF16))
                return (new_max, new_sum, new_acc)

            run_max, run_sum, run_acc = lax.fori_loop(
                low_ref[i],
                at_ref[i] + 1,
                one_step,
                (
                    jnp.full((1, tile), -1e30, F32),
                    jnp.zeros((1, tile), F32),
                    jnp.zeros((HD, tile), F32),
                ),
            )
            out[pl.ds(pl.multiple_of(j * tile, tile), tile), :] = (run_acc / run_sum).T.astype(BF16)
            lse_ref[i] = run_max + jnp.log(run_sum)
            return carry

        lax.fori_loop(0, per_out, one_block, 0)


def attend_back_kernel(
    tile, scale, lane0s, near_is_q, at_ref, low_ref, row_ref, first_ref, lse_ref, cos_ref, sin_ref, *refs
):
    n_kv = len(lane0s)
    q_refs = refs[:HEADS]
    kv_refs = refs[:n_kv] if near_is_q else refs[HEADS : HEADS + n_kv]
    refs = refs[n_kv if near_is_q else HEADS + n_kv :]
    o_refs, do_refs, dq_refs = refs[:HEADS], refs[HEADS : 2 * HEADS], refs[2 * HEADS : 3 * HEADS]
    near_ref, far_ref, q_all, kv_all, acc_ref = refs[3 * HEADS :]
    gather_refs(q_refs, kv_refs, lane0s, q_all, kv_all)
    acc_ref[...] = jnp.zeros_like(acc_ref)
    lanes = lax.broadcasted_iota(jnp.int32, (1, tile), 1)
    per_out = dq_refs[0].shape[0] // tile

    for k in range(HEADS):

        def one_block(j, carry, k=k):
            i = k * per_out + j
            rows = pl.ds(pl.multiple_of(i * tile, tile), tile)
            piece = pl.ds(pl.multiple_of(j * tile, tile), tile)
            queries = q_all[rows, :]
            grads = do_refs[k][piece, :]
            firsts = first_ref[i]
            places = at_ref[i] * tile + lanes
            log_sums = lse_ref[i]
            products = grads.astype(F32) * o_refs[k][piece, :].astype(F32)
            deltas = jnp.sum(products.T, axis=0, keepdims=True)

            def one_step(b, grad_q):
                krows = pl.ds(pl.multiple_of(row_ref[b] * tile, tile), tile)
                keys = kv_all[krows, :HD]
                scores = nt(keys, queries) * scale
                visible = visible_of(tile, b, places, firsts)
                probs = jnp.where(visible, jnp.exp(scores - log_sums), 0.0)
                grad_probs = nt(kv_all[krows, HD:], grads)
                grad_scores = (probs * (grad_probs - deltas)).astype(BF16)
                acc_ref[krows, HD:] += nn(probs.astype(BF16), grads)
                acc_ref[krows, :HD] += nn(grad_scores, queries)
                return grad_q + tn(keys, grad_scores)

            grad_q = lax.fori_loop(low_ref[i], at_ref[i] + 1, one_step, jnp.zeros((HD, tile), F32))
            dq_refs[k][piece, :] = rotate(
                (grad_q * scale).T, cos_ref[rows, :], -sin_ref[rows, :]
            ).astype(BF16)
            return carry

        lax.fori_loop(0, per_out, one_block, 0)
    near = near_ref.shape[0]
    near_ref[:, :HD] = (acc_ref[:near, :HD] * scale).astype(BF16)
    near_ref[:, HD:] = acc_ref[:near, HD:].astype(BF16)
    far_ref[:, :HD] = (acc_ref[near:, :HD] * scale).astype(BF16)
    far_ref[:, HD:] = acc_ref[near:, HD:].astype(BF16)


def attend(tile, scale, tables, pieces, keys_values, lane0s, near_is_q):
    rows = HEADS * pieces[0].shape[0]
    kv_rows = sum(a.shape[0] for a in keys_values)
    operands = keys_values if near_is_q else pieces + keys_values
    return pl.pallas_call(
        functools.partial(attend_kernel, tile, scale, lane0s, near_is_q),
        out_shape=[jax.ShapeDtypeStruct((rows // HEADS, HD), BF16)] * HEADS
        + [jax.ShapeDtypeStruct((rows // tile, 1, tile), F32)],
        in_specs=[SMEM] * 3 + [VMEM] * (1 + len(operands)),
        out_specs=[VMEM] * (HEADS + 1),
        scratch_shapes=[pltpu.VMEM((rows, HD), BF16), pltpu.VMEM((kv_rows, 2 * HD), BF16)],
        compiler_params=params(50),
        cost_estimate=cost(4 * rows * 1280 * HD, 4 * 2**20),
        name="attend",
    )(*tables, *operands)


def attend_back(
    tile, scale, tables, lse, cosine, sine, pieces, keys_values, lane0s, near_is_q, outs, grads
):
    rows = HEADS * pieces[0].shape[0]
    kv_rows = sum(a.shape[0] for a in keys_values)
    operands = (keys_values if near_is_q else pieces + keys_values) + outs + grads
    return pl.pallas_call(
        functools.partial(attend_back_kernel, tile, scale, lane0s, near_is_q),
        out_shape=[jax.ShapeDtypeStruct((rows // HEADS, HD), BF16)] * HEADS
        + [jax.ShapeDtypeStruct((kv_rows // 2, 2 * HD), BF16)] * 2,
        in_specs=[SMEM] * 3 + [VMEM] * (4 + len(operands)),
        out_specs=[VMEM] * (HEADS + 2),
        scratch_shapes=[
            pltpu.VMEM((rows, HD), BF16),
            pltpu.VMEM((kv_rows, 2 * HD), BF16),
            pltpu.VMEM((kv_rows, 2 * HD), F32),
        ],
        compiler_params=params(56),
        cost_estimate=cost(10 * rows * 1280 * HD, 8 * 2**20),
        name="attend_back",
    )(*tables, lse, cosine, sine, *operands)


def settle_kernel(near_ref, got_ref, cos_ref, sin_ref, out_ref):
    total = near_ref[...].astype(F32) + got_ref[...].astype(F32)
    out_ref[:, :HD] = rotate(total[:, :HD], cos_ref[...], -sin_ref[...]).astype(BF16)
    out_ref[:, HD:] = total[:, HD:].astype(BF16)


def settle(near, got, cosine, sine):
    rows = near.shape[0]
    tile = rows // HEADS
    spec = pl.BlockSpec((tile, 2 * HD), lambda k: (k, 0))
    table = pl.BlockSpec((tile, HD), lambda k: (k, 0))
    return pl.pallas_call(
        settle_kernel,
        grid=(HEADS,),
        out_shape=jax.ShapeDtypeStruct(near.shape, BF16),
        in_specs=[spec, spec, table, table],
        out_specs=spec,
        compiler_params=params(24),
        cost_estimate=cost(rows * 1024, 5 * 2**20),
        name="settle",
    )(near, got, cosine, sine)


def out_project_kernel(idx, w_ref, *refs):
    pieces, (flat_ref, keep_ref, give_ref) = refs[:HEADS], refs[HEADS:]
    for k, piece in enumerate(pieces):
        flat_ref[:, pl.ds(pl.multiple_of((idx[0] ^ k) * HD, HD), HD)] = piece[...]
    half = keep_ref.shape[0]
    core = idx[2]
    mine = flat_ref[pl.ds(pl.multiple_of(core * half, half), half), :]
    other = flat_ref[pl.ds(pl.multiple_of((1 - core) * half, half), half), :]
    give_ref[...] = nn(other, w_ref[...]).astype(BF16)
    keep_ref[...] = nn(mine, w_ref[...]).astype(BF16)


def out_project(idx, w_out, pieces):
    cols, dim = w_out.shape
    tok = pieces[0].shape[0]
    half = jax.ShapeDtypeStruct((tok // 2, dim), BF16)
    return pl.pallas_call(
        out_project_kernel,
        out_shape=[jax.ShapeDtypeStruct((tok, cols), BF16), half, half],
        in_specs=[SMEM] + [VMEM] * (1 + HEADS),
        out_specs=[VMEM] * 3,
        compiler_params=params(40),
        cost_estimate=cost(2 * tok * dim * cols, 6 * 2**20),
        name="out_project",
    )(idx, w_out, *pieces)


def out_back_kernel(idx, w_ref, mine_ref, other_ref, *outs):
    half = mine_ref.shape[0]
    core = idx[2]
    for k, out in enumerate(outs):
        weights = w_ref[pl.ds(pl.multiple_of((idx[0] ^ k) * HD, HD), HD), :]
        out[pl.ds(pl.multiple_of(core * half, half), half), :] = nt(mine_ref[...], weights).astype(BF16)
        out[pl.ds(pl.multiple_of((1 - core) * half, half), half), :] = nt(
            other_ref[...], weights
        ).astype(BF16)


def out_back(idx, w_out, mine, other):
    half, dim = mine.shape
    return pl.pallas_call(
        out_back_kernel,
        out_shape=[jax.ShapeDtypeStruct((2 * half, HD), BF16)] * HEADS,
        in_specs=[SMEM] + [VMEM] * 3,
        out_specs=[VMEM] * HEADS,
        compiler_params=params(40),
        cost_estimate=cost(4 * half * dim * HEADS * HD, 5 * 2**20),
        name="out_back",
    )(idx, w_out, mine, other)


def norm_kernel(x_ref, chip_ref, far_ref, gain_ref, bias_ref, sum_ref, out_ref):
    total = x_ref[...].astype(F32) + (chip_ref[...].astype(F32) + far_ref[...].astype(F32))
    sum_ref[...] = total
    normed, _ = normalise(total)
    out_ref[...] = (normed * gain_ref[...] + bias_ref[...]).astype(BF16)


def norm(x, chip, far, gain, bias):
    rows, dim = x.shape
    tile = rows // 4
    spec = pl.BlockSpec((tile, dim), lambda i: (i, 0))
    return pl.pallas_call(
        norm_kernel,
        grid=(4,),
        out_shape=[jax.ShapeDtypeStruct((rows, dim), F32), jax.ShapeDtypeStruct((rows, dim), BF16)],
        in_specs=[spec, spec, spec, whole((1, dim)), whole((1, dim))],
        out_specs=[spec, spec],
        compiler_params=params(24),
        cost_estimate=cost(16 * rows * dim, 12 * rows * dim),
        name="norm",
    )(x, chip, far, gain, bias)


def norm_all_kernel(x_ref, gain_ref, bias_ref, out_ref):
    normed, _ = normalise(x_ref[...].astype(F32))
    out_ref[...] = (normed * gain_ref[...] + bias_ref[...]).astype(BF16)


def norm_all(x, gain, bias):
    rows, dim = x.shape
    tile = 128
    spec = pl.BlockSpec((tile, dim), lambda i: (i, 0))
    return pl.pallas_call(
        norm_all_kernel,
        grid=(rows // tile,),
        out_shape=jax.ShapeDtypeStruct((rows, dim), BF16),
        in_specs=[spec, whole((1, dim)), whole((1, dim))],
        out_specs=spec,
        compiler_params=params(24),
        cost_estimate=cost(16 * rows * dim, 4 * rows * dim),
        name="norm_all",
    )(x, gain, bias)


def norm_back_kernel(chip_ref, far_ref, x_ref, base_ref, gain_ref, wide_ref, low_ref, dg_ref, db_ref):
    grad = chip_ref[...].astype(F32) + far_ref[...].astype(F32)
    normed, inverse = normalise(x_ref[...].astype(F32))
    scaled = grad * gain_ref[...]
    back = inverse * (
        scaled
        - jnp.mean(scaled, axis=-1, keepdims=True)
        - normed * jnp.mean(scaled * normed, axis=-1, keepdims=True)
    )
    total = base_ref[...].astype(F32) + back
    wide_ref[...] = total
    low_ref[...] = total.astype(BF16)

    @pl.when(pl.program_id(0) == 0)
    def _():
        dg_ref[...] = jnp.zeros_like(dg_ref)
        db_ref[...] = jnp.zeros_like(db_ref)

    dg_ref[...] += jnp.sum(grad * normed, axis=0, keepdims=True)
    db_ref[...] += jnp.sum(grad, axis=0, keepdims=True)


def norm_back(chip, far, x, base, gain):
    rows, dim = chip.shape
    tile = rows // 4
    spec = pl.BlockSpec((tile, dim), lambda i: (i, 0))
    row = whole((1, dim))
    return pl.pallas_call(
        norm_back_kernel,
        grid=(4,),
        out_shape=[
            jax.ShapeDtypeStruct((rows, dim), F32),
            jax.ShapeDtypeStruct((rows, dim), BF16),
            jax.ShapeDtypeStruct((1, dim), F32),
            jax.ShapeDtypeStruct((1, dim), F32),
        ],
        in_specs=[spec] * 4 + [row],
        out_specs=[spec, spec, row, row],
        compiler_params=params(24),
        cost_estimate=cost(30 * rows * dim, 18 * rows * dim),
        name="norm_back",
    )(chip, far, x, base, gain)


def feed_kernel(mine_ref, other_ref, w_ref, gact_ref, keep_ref, act_ref, du_ref, *refs):
    half = mine_ref.shape[0]
    weights = w_ref[...]
    for at, ref in ((0, mine_ref), (half, other_ref)):
        rows = slice(at, at + half)
        relu = jnp.maximum(nn(ref[...], weights), 0.0) * keep_ref[rows, :]
        act_ref[rows, :] = (relu * relu).astype(BF16)
        du_ref[rows, :] = (gact_ref[rows, :].astype(F32) * 2.0 * relu).astype(BF16)
    if refs:
        keep_out, give_out, acc_ref = refs
        step = pl.program_id(0)

        @pl.when(step == 0)
        def _():
            acc_ref[...] = nt(du_ref[...], weights)

        @pl.when(step > 0)
        def _():
            acc_ref[...] += nt(du_ref[...], weights)

        @pl.when(step == pl.num_programs(0) - 1)
        def _():
            keep_out[...] = acc_ref[:half, :].astype(BF16)
            give_out[...] = acc_ref[half:, :].astype(BF16)


def feed_forward(mine, other, w_up, gact, keep, with_back):
    half, dim = mine.shape
    hidden = w_up.shape[1]
    tile = min(hidden, 512)
    tall = jax.ShapeDtypeStruct((2 * half, hidden), BF16)
    part = jax.ShapeDtypeStruct((half, dim), BF16)
    spec = pl.BlockSpec((2 * half, tile), lambda i: (0, i))
    return pl.pallas_call(
        feed_kernel,
        grid=(hidden // tile,),
        out_shape=[tall, tall] + ([part, part] if with_back else []),
        in_specs=[
            whole((half, dim)),
            whole((half, dim)),
            pl.BlockSpec((dim, tile), lambda i: (0, i)),
            spec,
            whole((2 * half, 1)),
        ],
        out_specs=[spec, spec] + ([whole((half, dim))] * 2 if with_back else []),
        scratch_shapes=[pltpu.VMEM((2 * half, dim), F32)] if with_back else [],
        compiler_params=params(48),
        cost_estimate=cost((8 if with_back else 4) * half * dim * hidden, 16 * 2**20),
        name="feed_own" if with_back else "feed_far",
    )(mine, other, w_up, gact, keep)


def product_kernel(idx, *refs):
    cols, near_ref, far_ref, out_ref, turn_ref = refs[:4], refs[4], refs[5], refs[6], refs[7]
    half = cols[0].shape[0]
    for k, ref in enumerate(cols):
        turn_ref[:, k * half : (k + 1) * half] = ref[...].astype(F32).T.astype(BF16)
    width = out_ref.shape[1]
    tile = min(width, 512)
    starts = [pl.multiple_of(idx[3 + j] * half, half) for j in range(2)]
    for at in range(0, width, tile):
        lanes = slice(at, at + tile)
        total = None
        for k in range(4):
            rows = (near_ref, far_ref)[k // 2][pl.ds(starts[k % 2], half), lanes]
            term = nn(turn_ref[:, k * half : (k + 1) * half], rows)
            total = term if total is None else total + term
        out_ref[:, lanes] = total.astype(BF16)


def product(idx, cols, near, far):
    half, dim = cols[0].shape
    tok, width = near.shape
    block = dim // (2 * HEADS)
    spec = pl.BlockSpec((half, block), lambda k, idx: (0, 2 * k + idx[1]))
    return pl.pallas_call(
        product_kernel,
        grid_spec=pltpu.PrefetchScalarGridSpec(
            num_scalar_prefetch=1,
            grid=(HEADS,),
            in_specs=[spec] * 4 + [whole((tok, width))] * 2,
            out_specs=pl.BlockSpec((block, width), lambda k, idx: (k, 0)),
            scratch_shapes=[pltpu.VMEM((block, 4 * half), BF16)],
        ),
        out_shape=jax.ShapeDtypeStruct((HEADS * block, width), BF16),
        compiler_params=params(40),
        cost_estimate=cost(2 * tok * width * dim, 12 * 2**20),
        name="product",
    )(idx, *cols, near, far)


def head_product_kernel(idx, h_ref, dkv_ref, *refs):
    dq_refs, (give_ref, keep_ref, turn_ref) = refs[:HEADS], refs[HEADS:]
    tok = dq_refs[0].shape[0]
    first = (pl.program_id(0) == 0) & (pl.program_id(1) == 0)

    @pl.when(first)
    def _():
        for k, ref in enumerate(dq_refs):
            turn_ref[:HD, k * tok : (k + 1) * tok] = ref[...].astype(F32).T.astype(BF16)
            rows = slice(k * tok, (k + 1) * tok)
            turn_ref[HD:, rows] = dkv_ref[rows, :].astype(F32).T.astype(BF16)

    total = None
    for k in range(HEADS):
        rows = h_ref[pl.ds(pl.multiple_of((idx[0] ^ k) * tok, tok), tok), :]
        term = nn(turn_ref[:, k * tok : (k + 1) * tok], rows)
        total = term if total is None else total + term

    @pl.when(pl.program_id(0) == 0)
    def _():
        give_ref[0] = total.astype(BF16)

    @pl.when(pl.program_id(0) == 1)
    def _():
        keep_ref[0] = total.astype(BF16)


def head_product(idx, h_all, dkv, dq_pieces):
    rows, dim = h_all.shape
    block = dim // (2 * HEADS)
    out = jax.ShapeDtypeStruct((HEADS, 3 * HD, block), BF16)

    def columns(turn, k, idx):
        return (0, (idx[0] ^ k) * 2 + jnp.where(turn == 0, 1 - idx[1], idx[1]))

    return pl.pallas_call(
        head_product_kernel,
        grid_spec=pltpu.PrefetchScalarGridSpec(
            num_scalar_prefetch=1,
            grid=(2, HEADS),
            in_specs=[pl.BlockSpec((rows, block), columns), whole((rows, 2 * HD))]
            + [whole((rows // HEADS, HD))] * HEADS,
            out_specs=[
                pl.BlockSpec(
                    (1, 3 * HD, block),
                    lambda turn, k, idx: (jnp.where(turn == 0, k, HEADS - 1), 0, 0),
                ),
                pl.BlockSpec(
                    (1, 3 * HD, block), lambda turn, k, idx: (jnp.where(turn == 0, 0, k), 0, 0)
                ),
            ],
            scratch_shapes=[pltpu.VMEM((3 * HD, rows), BF16)],
        ),
        out_shape=[out, out],
        compiler_params=params(40),
        cost_estimate=cost(2 * rows * dim * 3 * HD, 12 * 2**20),
        name="head_product",
    )(idx, h_all, dkv, *dq_pieces)


def head_place_kernel(idx, *refs):
    pieces, out_ref = refs[:HEADS], refs[HEADS]
    for k, piece in enumerate(pieces):
        for s in range(3):
            out_ref[s, :, pl.ds(pl.multiple_of((idx[0] ^ k) * HD, HD), HD)] = (
                piece[s * HD : (s + 1) * HD, :].astype(F32).T
            )


def head_place(idx, pieces):
    rows, block = pieces[0].shape
    return pl.pallas_call(
        head_place_kernel,
        out_shape=jax.ShapeDtypeStruct((3, block, HEADS * HD), F32),
        in_specs=[SMEM] + [VMEM] * HEADS,
        out_specs=VMEM,
        compiler_params=params(24),
        cost_estimate=cost(rows * block * 8, 4 * 2**20),
        name="head_place",
    )(idx, *pieces)


def project_back_kernel(idx, w_ref, *refs):
    dq_refs, dkv_refs = refs[:HEADS], refs[HEADS : 2 * HEADS]
    keep_ref, give_ref, flat_ref, acc_ref = refs[2 * HEADS :]
    half = keep_ref.shape[0]
    core = idx[2]
    step = pl.program_id(0)

    for s in range(3):

        @pl.when(step == s)
        def _(s=s):
            for k in range(HEADS):
                lanes = pl.ds(pl.multiple_of((idx[0] ^ k) * HD, HD), HD)
                if s == 0:
                    flat_ref[:, lanes] = dq_refs[k][...]
                else:
                    flat_ref[:, lanes] = dkv_refs[k][:, (s - 1) * HD : s * HD]

    @pl.when(step == 0)
    def _():
        acc_ref[...] = nt(flat_ref[...], w_ref[0])

    @pl.when(step > 0)
    def _():
        acc_ref[...] += nt(flat_ref[...], w_ref[0])

    @pl.when(step == 2)
    def _():
        give_ref[...] = acc_ref[pl.ds(pl.multiple_of((1 - core) * half, half), half), :].astype(BF16)
        keep_ref[...] = acc_ref[pl.ds(pl.multiple_of(core * half, half), half), :].astype(BF16)


def project_back(idx, w_qkv, dq_pieces, dkv_pieces):
    tok = dq_pieces[0].shape[0]
    _, dim, cols = w_qkv.shape
    part = jax.ShapeDtypeStruct((tok // 2, dim), BF16)
    return pl.pallas_call(
        project_back_kernel,
        grid_spec=pltpu.PrefetchScalarGridSpec(
            num_scalar_prefetch=1,
            grid=(3,),
            in_specs=[pl.BlockSpec((1, dim, cols), lambda s, idx: (s, 0, 0))]
            + [whole((tok, HD))] * HEADS
            + [whole((tok, 2 * HD))] * HEADS,
            out_specs=[whole((tok // 2, dim))] * 2,
            scratch_shapes=[pltpu.VMEM((tok, cols), BF16), pltpu.VMEM((tok, dim), F32)],
        ),
        out_shape=[part, part],
        compiler_params=params(40),
        cost_estimate=cost(6 * tok * dim * cols, 12 * 2**20),
        name="project_back",
    )(idx, w_qkv, *dq_pieces, *dkv_pieces)


def join_kernel(idx, mine_ref, other_ref, out_ref):
    half = mine_ref.shape[0]
    core = idx[2]
    out_ref[pl.ds(pl.multiple_of(core * half, half), half), :] = mine_ref[...].astype(out_ref.dtype)
    out_ref[pl.ds(pl.multiple_of((1 - core) * half, half), half), :] = other_ref[...].astype(
        out_ref.dtype
    )


def join(idx, mine, other, dtype):
    half, dim = mine.shape
    return pl.pallas_call(
        join_kernel,
        out_shape=jax.ShapeDtypeStruct((2 * half, dim), dtype),
        in_specs=[SMEM, VMEM, VMEM],
        out_specs=VMEM,
        compiler_params=params(24),
        cost_estimate=cost(half * dim, 8 * half * dim),
        name="join",
    )(idx, mine, other)


def body(
    depth,
    layer_input,
    ln1_gain,
    ln1_bias,
    w_qkv,
    w_out,
    ln2_gain,
    ln2_bias,
    w_up,
    w_down,
    buckets,
    lengths,
    block_order,
    grad_out,
):
    tok, dim = layer_input.shape
    half = tok // 2
    scale = 1.0 / math.sqrt(HD)
    r, h, y, x, c = (lax.axis_index(a) for a in BLK + TP)
    blk = lax.axis_index(BLK)
    tp = lax.axis_index(TP)
    idx = jnp.stack([h, y, c, jnp.zeros_like(c), jnp.ones_like(c)]).astype(jnp.int32)
    idx_rows = jnp.stack([h, y, c, c, 1 - c]).astype(jnp.int32)
    gains = [v.reshape(1, dim) for v in (ln1_gain, ln1_bias, ln2_gain, ln2_bias)]

    def half_of(values, which):
        return lax.dynamic_slice_in_dim(values, which * half, half, 0)

    def regroup(values):
        if depth == 1:
            return values
        rows = values.shape[0]
        split = values.reshape(rows, depth, HEADS, 2, dim // (2 * HEADS * depth))
        return split.transpose(0, 2, 3, 1, 4).reshape(rows, dim)

    def scatter(values):
        if depth > 1:
            split = values.reshape(HEADS, depth, -1, values.shape[1])
            values = split.transpose(1, 0, 2, 3).reshape(values.shape)
        return lax.psum_scatter(values, ("r", "h"), scatter_dimension=0, tiled=True)

    starts = jnp.cumsum(lengths) - lengths

    def firsts_of(places):
        return jnp.max(jnp.where(starts <= places[..., None], starts, 0), axis=-1)

    inside = jnp.arange(half, dtype=jnp.int32)
    own_places = (
        lax.dynamic_slice_in_dim(block_order, 2 * blk, 2, 0)[:, None] * half + inside
    ).reshape(tok)
    cosine, sine = rotary_tables(own_places - firsts_of(own_places))

    grad_mine, grad_other = half_of(grad_out, c), half_of(grad_out, 1 - c)
    far_grad_mine = swap(grad_mine, "y")

    packed = list(project(idx, layer_input, gains[0], gains[1], cosine, sine, w_qkv))
    packed = [packed[0]] + [plane_swap(packed[k], k) for k in range(1, HEADS)]

    relative = h ^ jnp.arange(HEADS, dtype=jnp.int32)
    group_order = lax.dynamic_index_in_dim(
        block_order.reshape(depth, HEADS, 2, 2), r, 0, keepdims=False
    )
    group_order = lax.dynamic_index_in_dim(group_order, y, 1, keepdims=False)
    chosen = relative[:, None] == jnp.arange(HEADS, dtype=jnp.int32)[None, :]
    query_at = jnp.sum(jnp.where(chosen[:, :, None], group_order[None], 0), axis=1).reshape(-1)
    query_places = query_at[:, None] * half + inside
    query_firsts = firsts_of(query_places)
    query_low = query_firsts[:, 0] // half
    block_count = block_order.shape[0]
    slots = jnp.argmax(
        block_order[None, :] == jnp.arange(block_count, dtype=jnp.int32)[:, None], axis=1
    ).astype(jnp.int32)
    slot_dev = slots // 2
    slot_plane = slot_dev // 2
    key_row = (
        jnp.where(slot_dev % 2 == y, 0, block_count // 2)
        + slot_plane // HEADS * (2 * HEADS)
        + ((slot_plane % HEADS) ^ h) * 2
        + slots % 2
    )
    group_cos, group_sin = rotary_tables((query_places - query_firsts).reshape(2 * HEADS * half))
    tables = (query_at, query_low, key_row, query_firsts.reshape(2 * HEADS, 1, half))

    if depth == 1:
        far_a = swap(jnp.concatenate([packed[0][:, HD:], packed[1][:, HD:]]), "y")
        far_b = swap(jnp.concatenate([packed[2][:, HD:], packed[3][:, HD:]]), "y")
        keys_values, lane0s, near_is_q = packed + [far_a, far_b], [HD] * HEADS + [0, 0], True
    else:
        near_kv = lax.all_gather(
            jnp.concatenate([p[:, HD:] for p in packed]), "r", axis=0, tiled=True
        )
        keys_values, lane0s, near_is_q = [near_kv, swap(near_kv, "y")], [0, 0], False

    quarter = lax.dynamic_slice_in_dim(layer_input, tp * (tok // 4), tok // 4, 0)
    quarter, packed[3] = ordered(quarter, packed[3])
    if depth == 1:
        keys_values[3] = packed[3]
    x_all = lax.all_gather(quarter, ("h",) + TP, axis=0, tiled=True)

    far_grad_other = swap(far_grad_mine, "c")
    grad_act = nt(jnp.concatenate([grad_mine, grad_other]), w_down).astype(BF16)
    far_grad_act = nt(jnp.concatenate([far_grad_mine, far_grad_other]), w_down).astype(BF16)
    keep_rows = (buckets >= tp).astype(F32)
    far_keep = swap(keep_rows, "y")
    keep_rows = jnp.concatenate([half_of(keep_rows, c), half_of(keep_rows, 1 - c)])[:, None]
    far_keep = jnp.concatenate([half_of(far_keep, c), half_of(far_keep, 1 - c)])[:, None]
    grad_act, far_grad_act, group_cos, group_sin, keys_values[-1] = ordered(
        grad_act, far_grad_act, group_cos, group_sin, keys_values[-1]
    )

    *attended, lse = attend(half, scale, tables, packed, keys_values, lane0s, near_is_q)
    pieces = [attended[0]] + [plane_swap(attended[k], k) for k in range(1, HEADS)]
    flat, keep, give = out_project(idx, w_out, pieces)

    def chip_sum(keep, give):
        return (keep.astype(F32) + swap(give, "c").astype(F32)).astype(BF16)

    chip = chip_sum(keep, give)
    x_mid, h_mine = norm(half_of(layer_input, c), chip, swap(chip, "x"), gains[2], gains[3])
    h_other = swap(h_mine, "c")
    far_h_mine = swap(h_mine, "y")
    far_flat = swap(flat, "y")
    act, du, keep, give = feed_forward(h_mine, h_other, w_up, grad_act, keep_rows, True)
    chip = chip_sum(keep, give)
    chip_far = swap(chip, "x")

    far_h_other = swap(far_h_mine, "c")
    far_act, far_du = feed_forward(far_h_mine, far_h_other, w_up, far_grad_act, far_keep, False)
    down_part = scatter(
        product(
            idx,
            [regroup(v) for v in (grad_mine, grad_other, far_grad_mine, far_grad_other)],
            act,
            far_act,
        )
    )
    up_part = scatter(
        product(idx, [regroup(v) for v in (h_mine, h_other, far_h_mine, far_h_other)], du, far_du)
    )

    grad_mid, dy_mine, gain_two_grad, bias_two_grad = norm_back(
        chip, chip_far, x_mid, grad_mine, gains[2]
    )
    dy_other = swap(dy_mine, "c")
    grads = list(out_back(idx, w_out, dy_mine, dy_other))
    grads = [grads[0]] + [plane_swap(grads[k], k) for k in range(1, HEADS)]

    far_dy_mine = swap(dy_mine, "y")
    far_dy_other = swap(far_dy_mine, "c")
    wout_part = scatter(
        product(
            idx_rows,
            [regroup(v) for v in (dy_mine, dy_other, far_dy_mine, far_dy_other)],
            flat,
            far_flat,
        )
    )
    feed = [jnp.dot(act[s], w_down, preferred_element_type=F32).astype(BF16) for s in (slice(half), slice(half, tok))]
    feed_chip = chip_sum(feed[0], feed[1])
    out_mine = (
        x_mid + (feed_chip.astype(F32) + swap(feed_chip, "x").astype(F32))
    ).astype(BF16)
    layer_output = join(idx, out_mine, swap(out_mine, "c"), BF16)

    *dq, near, far = attend_back(
        half,
        scale,
        tables,
        lse,
        group_cos,
        group_sin,
        packed,
        keys_values,
        lane0s,
        near_is_q,
        attended,
        grads,
    )
    got = swap(far, "y")
    dq_pieces = [dq[0]] + [plane_swap(dq[k], k) for k in range(1, HEADS)]
    if depth > 1:
        near = lax.psum_scatter(near, "r", scatter_dimension=0, tiled=True)
        got = lax.psum_scatter(got, "r", scatter_dimension=0, tiled=True)
    dkv = settle(near, got, group_cos, group_sin)
    dkv_pieces = [dkv[:tok]] + [
        plane_swap(dkv[k * tok : (k + 1) * tok], k) for k in range(1, HEADS)
    ]
    keep, give = project_back(idx, w_qkv, dq_pieces, dkv_pieces)
    chip = chip_sum(keep, give)
    chip_far = swap(chip, "x")

    h_all = regroup(norm_all(x_all, gains[0], gains[1]))
    head_give, head_keep = head_product(idx, h_all, dkv, dq)
    head_sum = (head_keep.astype(F32) + swap(head_give, "y").astype(F32)).astype(BF16)
    if depth > 1:
        head_sum = lax.psum_scatter(head_sum, "r", scatter_dimension=2, tiled=True)
    head_pieces = [head_sum[0]] + [plane_swap(head_sum[k], k) for k in range(1, HEADS)]
    qkv_part = head_place(idx, head_pieces)

    _, grad_low, gain_one_grad, bias_one_grad = norm_back(
        chip, chip_far, half_of(layer_input, c), grad_mid, gains[0]
    )
    grad_input = join(idx, grad_low, swap(grad_low, "c"), F32)

    counts = jnp.sum(
        (half_of(buckets, c)[:, None] == jnp.arange(NB, dtype=jnp.int32)[None, :]).astype(F32),
        axis=0,
    )
    sums = jnp.concatenate(
        [v.reshape(dim) for v in (gain_one_grad, bias_one_grad, gain_two_grad, bias_two_grad)]
        + [counts]
    )
    if depth > 1:
        sums = lax.psum(sums, "r")
    sums = sums + swap(sums, "c")
    sums = sums + swap(sums, "y")
    one, two, three = (plane_swap(sums, k) for k in range(1, HEADS))
    sums = (sums + one) + (two + three)
    return (
        layer_output,
        grad_input,
        sums[:dim],
        sums[dim : 2 * dim],
        qkv_part,
        wout_part.astype(F32).T,
        sums[2 * dim : 3 * dim],
        sums[3 * dim : 4 * dim],
        up_part.astype(F32),
        down_part.astype(F32).T,
        sums[4 * dim :].astype(jnp.int32),
    )


def solution(mesh):
    depth = mesh.shape["blk"] // (2 * HEADS)
    fine = Mesh(mesh.devices.reshape(depth, HEADS, 2, 2, 2), BLK + TP)
    return jax.shard_map(
        functools.partial(body, depth),
        mesh=fine,
        in_specs=(
            P(BLK, None),
            P(),
            P(),
            P(None, None, TP),
            P(TP, None),
            P(),
            P(),
            P(None, TP),
            P(TP, None),
            P(BLK),
            P(),
            P(),
            P(BLK, None),
        ),
        out_specs=(
            P(BLK, None),
            P(BLK, None),
            P(),
            P(),
            P(None, BLK, TP),
            P(TP, BLK),
            P(),
            P(),
            P(BLK, TP),
            P(TP, BLK),
            P(),
        ),
        check_vma=False,
    )
```

```python
import functools
import math

import jax
import jax.numpy as jnp
from jax import lax
from jax.experimental import pallas as pl
from jax.experimental.pallas import tpu as pltpu
from jax.sharding import Mesh
from jax.sharding import PartitionSpec as P

HD = 128
FF = 8192
NB = 4
HEADS = 4
EPSILON = 1e-05
ROPE_BASE = 10000.0
BLK = ("r", "h", "y")
TP = ("x", "c")
F32 = jnp.float32
BF16 = jnp.bfloat16
SMEM = pl.BlockSpec(memory_space=pltpu.SMEM)
VMEM = pl.BlockSpec(memory_space=pltpu.VMEM)


def swap(value, axis):
    return lax.ppermute(value, axis, [(0, 1), (1, 0)])


def plane_swap(value, k):
    return lax.ppermute(value, "h", [(i, i ^ k) for i in range(HEADS)])


def ordered(*values):
    return lax.optimization_barrier(values)


def nt(lhs, rhs):
    return lax.dot_general(lhs, rhs, (((1,), (1,)), ((), ())), preferred_element_type=F32)


def tn(lhs, rhs):
    return lax.dot_general(lhs, rhs, (((0,), (0,)), ((), ())), preferred_element_type=F32)


def nn(lhs, rhs):
    return lax.dot_general(lhs, rhs, (((1,), (0,)), ((), ())), preferred_element_type=F32)


def params(mib, **more):
    return pltpu.CompilerParams(vmem_limit_bytes=mib * 2**20, **more)


def cost(flops, moved):
    return pl.CostEstimate(flops=int(flops), bytes_accessed=int(moved), transcendentals=0)


def whole(shape):
    return pl.BlockSpec(shape, lambda *_: (0,) * len(shape))


def normalise(values):
    centre = values - jnp.mean(values, axis=-1, keepdims=True)
    inverse = lax.rsqrt(jnp.mean(centre * centre, axis=-1, keepdims=True) + EPSILON)
    return (centre * inverse, inverse)


def rotary_tables(positions):
    freqs = ROPE_BASE ** (-(jnp.arange(HD // 2, dtype=F32) * 2.0 / HD))
    angles = positions.astype(F32)[:, None] * freqs[None, :]
    cosine, sine = jnp.cos(angles), jnp.sin(angles)
    return (
        jnp.concatenate([cosine, cosine], axis=-1),
        jnp.concatenate([-sine, sine], axis=-1),
    )


def rotate(values, cosine, sine):
    return values * cosine + pltpu.roll(values, HD // 2, 1) * sine


def project_kernel(idx, x_ref, gain_ref, bias_ref, cos_ref, sin_ref, w_ref, *refs):
    q_outs, kv_outs, h_ref = refs[:HEADS], refs[HEADS : 2 * HEADS], refs[2 * HEADS]
    step = pl.program_id(0)

    @pl.when(step == 0)
    def _():
        normed, _ = normalise(x_ref[...].astype(F32))
        h_ref[...] = (normed * gain_ref[...] + bias_ref[...]).astype(BF16)

    both = nn(h_ref[...], jnp.concatenate([w_ref[0], w_ref[1]], axis=1))
    cosine, sine = cos_ref[...], sin_ref[...]
    queries = rotate(both[:, :HD], cosine, sine).astype(BF16)
    keys = rotate(both[:, HD:], cosine, sine).astype(BF16)
    values = nn(h_ref[...], w_ref[2]).astype(BF16)
    for k in range(HEADS):

        @pl.when(step == k)
        def _(k=k):
            q_outs[k][...] = queries
            kv_outs[k][:, :HD] = keys
            kv_outs[k][:, HD:] = values


def project(idx, x, gain, bias, cosine, sine, w_qkv):
    tok, dim = x.shape
    return pl.pallas_call(
        project_kernel,
        grid_spec=pltpu.PrefetchScalarGridSpec(
            num_scalar_prefetch=1,
            grid=(HEADS,),
            in_specs=[
                whole((tok, dim)),
                whole((1, dim)),
                whole((1, dim)),
                whole((tok, HD)),
                whole((tok, HD)),
                pl.BlockSpec((3, dim, HD), lambda k, idx: (0, 0, idx[0] ^ k)),
            ],
            out_specs=[whole((tok, HD))] * HEADS + [whole((tok, 2 * HD))] * HEADS,
            scratch_shapes=[pltpu.VMEM((tok, dim), BF16)],
        ),
        out_shape=[jax.ShapeDtypeStruct((tok, HD), BF16)] * HEADS
        + [jax.ShapeDtypeStruct((tok, 2 * HD), BF16)] * HEADS,
        compiler_params=params(40),
        cost_estimate=cost(2 * tok * dim * 12 * HD, 10 * 2**20),
        name="project",
    )(idx, x, gain, bias, cosine, sine, w_qkv)


def visible_of(tile, key_block, query_places, query_firsts):
    key_places = key_block * tile + lax.broadcasted_iota(jnp.int32, (tile, 1), 0)
    return (key_places <= query_places) & (key_places >= query_firsts)


def gather_refs(refs, whole_ref):
    at = 0
    for ref in refs:
        whole_ref[at : at + ref.shape[0], :] = ref[...]
        at += ref.shape[0]


def attend_kernel(tile, scale, n_kv, at_ref, low_ref, row_ref, first_ref, *refs):
    q_refs, kv_refs, refs = refs[:HEADS], refs[HEADS : HEADS + n_kv], refs[HEADS + n_kv :]
    outs, (lse_ref, q_all, kv_all) = refs[:HEADS], refs[HEADS:]
    gather_refs(q_refs, q_all)
    gather_refs(kv_refs, kv_all)
    lanes = lax.broadcasted_iota(jnp.int32, (1, tile), 1)
    per_out = outs[0].shape[0] // tile

    for k, out in enumerate(outs):

        def one_block(j, carry, k=k, out=out):
            i = k * per_out + j
            queries = q_all[pl.ds(pl.multiple_of(i * tile, tile), tile), :]
            firsts = first_ref[i]
            places = at_ref[i] * tile + lanes

            def one_step(b, state):
                run_max, run_sum, run_acc = state
                krows = pl.ds(pl.multiple_of(row_ref[b] * tile, tile), tile)
                scores = nt(kv_all[krows, :HD], queries) * scale
                visible = visible_of(tile, b, places, firsts)
                scores = jnp.where(visible, scores, -1e30)
                new_max = jnp.maximum(run_max, jnp.max(scores, axis=0, keepdims=True))
                factor = jnp.exp(run_max - new_max)
                probs = jnp.where(visible, jnp.exp(scores - new_max), 0.0)
                new_sum = run_sum * factor + jnp.sum(probs, axis=0, keepdims=True)
                new_acc = run_acc * factor + tn(kv_all[krows, HD:], probs.astype(BF16))
                return (new_max, new_sum, new_acc)

            run_max, run_sum, run_acc = lax.fori_loop(
                low_ref[i],
                at_ref[i] + 1,
                one_step,
                (
                    jnp.full((1, tile), -1e30, F32),
                    jnp.zeros((1, tile), F32),
                    jnp.zeros((HD, tile), F32),
                ),
            )
            out[pl.ds(pl.multiple_of(j * tile, tile), tile), :] = (run_acc / run_sum).T.astype(BF16)
            lse_ref[i] = run_max + jnp.log(run_sum)
            return carry

        lax.fori_loop(0, per_out, one_block, 0)


def attend_back_kernel(
    tile, scale, n_kv, at_ref, low_ref, row_ref, first_ref, lse_ref, cos_ref, sin_ref, *refs
):
    q_refs, kv_refs, refs = refs[:HEADS], refs[HEADS : HEADS + n_kv], refs[HEADS + n_kv :]
    o_refs, do_refs, dq_refs = refs[:HEADS], refs[HEADS : 2 * HEADS], refs[2 * HEADS : 3 * HEADS]
    near_ref, far_ref, q_all, kv_all, acc_ref = refs[3 * HEADS :]
    gather_refs(q_refs, q_all)
    gather_refs(kv_refs, kv_all)
    acc_ref[...] = jnp.zeros_like(acc_ref)
    lanes = lax.broadcasted_iota(jnp.int32, (1, tile), 1)
    per_out = dq_refs[0].shape[0] // tile

    for k in range(HEADS):

        def one_block(j, carry, k=k):
            i = k * per_out + j
            rows = pl.ds(pl.multiple_of(i * tile, tile), tile)
            piece = pl.ds(pl.multiple_of(j * tile, tile), tile)
            queries = q_all[rows, :]
            grads = do_refs[k][piece, :]
            firsts = first_ref[i]
            places = at_ref[i] * tile + lanes
            log_sums = lse_ref[i]
            products = grads.astype(F32) * o_refs[k][piece, :].astype(F32)
            deltas = jnp.sum(products.T, axis=0, keepdims=True)

            def one_step(b, grad_q):
                krows = pl.ds(pl.multiple_of(row_ref[b] * tile, tile), tile)
                keys = kv_all[krows, :HD]
                scores = nt(keys, queries) * scale
                visible = visible_of(tile, b, places, firsts)
                probs = jnp.where(visible, jnp.exp(scores - log_sums), 0.0)
                grad_probs = nt(kv_all[krows, HD:], grads)
                grad_scores = (probs * (grad_probs - deltas)).astype(BF16)
                acc_ref[krows, HD:] += nn(probs.astype(BF16), grads)
                acc_ref[krows, :HD] += nn(grad_scores, queries)
                return grad_q + tn(keys, grad_scores)

            grad_q = lax.fori_loop(low_ref[i], at_ref[i] + 1, one_step, jnp.zeros((HD, tile), F32))
            dq_refs[k][piece, :] = rotate(
                (grad_q * scale).T, cos_ref[rows, :], -sin_ref[rows, :]
            ).astype(BF16)
            return carry

        lax.fori_loop(0, per_out, one_block, 0)
    near = near_ref.shape[0]
    near_ref[:, :HD] = (acc_ref[:near, :HD] * scale).astype(BF16)
    near_ref[:, HD:] = acc_ref[:near, HD:].astype(BF16)
    far_ref[:, :HD] = (acc_ref[near:, :HD] * scale).astype(BF16)
    far_ref[:, HD:] = acc_ref[near:, HD:].astype(BF16)


def attend(tile, scale, tables, pieces, keys_values):
    rows = HEADS * pieces[0].shape[0]
    kv_rows = sum(a.shape[0] for a in keys_values)
    operands = pieces + keys_values
    return pl.pallas_call(
        functools.partial(attend_kernel, tile, scale, len(keys_values)),
        out_shape=[jax.ShapeDtypeStruct((rows // HEADS, HD), BF16)] * HEADS
        + [jax.ShapeDtypeStruct((rows // tile, 1, tile), F32)],
        in_specs=[SMEM] * 3 + [VMEM] * (1 + len(operands)),
        out_specs=[VMEM] * (HEADS + 1),
        scratch_shapes=[pltpu.VMEM((rows, HD), BF16), pltpu.VMEM((kv_rows, 2 * HD), BF16)],
        compiler_params=params(50),
        cost_estimate=cost(4 * rows * 1280 * HD, 4 * 2**20),
        name="attend",
    )(*tables, *operands)


def attend_back(tile, scale, tables, lse, cosine, sine, pieces, keys_values, outs, grads):
    rows = HEADS * pieces[0].shape[0]
    kv_rows = sum(a.shape[0] for a in keys_values)
    operands = pieces + keys_values + outs + grads
    return pl.pallas_call(
        functools.partial(attend_back_kernel, tile, scale, len(keys_values)),
        out_shape=[jax.ShapeDtypeStruct((rows // HEADS, HD), BF16)] * HEADS
        + [jax.ShapeDtypeStruct((kv_rows // 2, 2 * HD), BF16)] * 2,
        in_specs=[SMEM] * 3 + [VMEM] * (4 + len(operands)),
        out_specs=[VMEM] * (HEADS + 2),
        scratch_shapes=[
            pltpu.VMEM((rows, HD), BF16),
            pltpu.VMEM((kv_rows, 2 * HD), BF16),
            pltpu.VMEM((kv_rows, 2 * HD), F32),
        ],
        compiler_params=params(56),
        cost_estimate=cost(10 * rows * 1280 * HD, 8 * 2**20),
        name="attend_back",
    )(*tables, lse, cosine, sine, *operands)


def settle_kernel(near_ref, got_ref, cos_ref, sin_ref, out_ref):
    total = near_ref[...].astype(F32) + got_ref[...].astype(F32)
    out_ref[:, :HD] = rotate(total[:, :HD], cos_ref[...], -sin_ref[...]).astype(BF16)
    out_ref[:, HD:] = total[:, HD:].astype(BF16)


def settle(near, got, cosine, sine):
    rows = near.shape[0]
    tile = rows // HEADS
    spec = pl.BlockSpec((tile, 2 * HD), lambda k: (k, 0))
    table = pl.BlockSpec((tile, HD), lambda k: (k, 0))
    return pl.pallas_call(
        settle_kernel,
        grid=(HEADS,),
        out_shape=jax.ShapeDtypeStruct(near.shape, BF16),
        in_specs=[spec, spec, table, table],
        out_specs=spec,
        compiler_params=params(24),
        cost_estimate=cost(rows * 1024, 5 * 2**20),
        name="settle",
    )(near, got, cosine, sine)


def out_project_kernel(idx, w_ref, *refs):
    pieces, (flat_ref, keep_ref, give_ref) = refs[:HEADS], refs[HEADS:]
    for k, piece in enumerate(pieces):
        flat_ref[:, pl.ds(pl.multiple_of((idx[0] ^ k) * HD, HD), HD)] = piece[...]
    half = keep_ref.shape[0]
    core = idx[2]
    mine = flat_ref[pl.ds(pl.multiple_of(core * half, half), half), :]
    other = flat_ref[pl.ds(pl.multiple_of((1 - core) * half, half), half), :]
    give_ref[...] = nn(other, w_ref[...]).astype(BF16)
    keep_ref[...] = nn(mine, w_ref[...]).astype(BF16)


def out_project(idx, w_out, pieces):
    cols, dim = w_out.shape
    tok = pieces[0].shape[0]
    half = jax.ShapeDtypeStruct((tok // 2, dim), BF16)
    return pl.pallas_call(
        out_project_kernel,
        out_shape=[jax.ShapeDtypeStruct((tok, cols), BF16), half, half],
        in_specs=[SMEM] + [VMEM] * (1 + HEADS),
        out_specs=[VMEM] * 3,
        compiler_params=params(40),
        cost_estimate=cost(2 * tok * dim * cols, 6 * 2**20),
        name="out_project",
    )(idx, w_out, *pieces)


def out_back_kernel(idx, w_ref, mine_ref, other_ref, *outs):
    half = mine_ref.shape[0]
    core = idx[2]
    for k, out in enumerate(outs):
        weights = w_ref[pl.ds(pl.multiple_of((idx[0] ^ k) * HD, HD), HD), :]
        out[pl.ds(pl.multiple_of(core * half, half), half), :] = nt(mine_ref[...], weights).astype(BF16)
        out[pl.ds(pl.multiple_of((1 - core) * half, half), half), :] = nt(
            other_ref[...], weights
        ).astype(BF16)


def out_back(idx, w_out, mine, other):
    half, dim = mine.shape
    return pl.pallas_call(
        out_back_kernel,
        out_shape=[jax.ShapeDtypeStruct((2 * half, HD), BF16)] * HEADS,
        in_specs=[SMEM] + [VMEM] * 3,
        out_specs=[VMEM] * HEADS,
        compiler_params=params(40),
        cost_estimate=cost(4 * half * dim * HEADS * HD, 5 * 2**20),
        name="out_back",
    )(idx, w_out, mine, other)


def norm_kernel(x_ref, chip_ref, far_ref, gain_ref, bias_ref, sum_ref, out_ref):
    total = x_ref[...].astype(F32) + (chip_ref[...].astype(F32) + far_ref[...].astype(F32))
    sum_ref[...] = total
    normed, _ = normalise(total)
    out_ref[...] = (normed * gain_ref[...] + bias_ref[...]).astype(BF16)


def norm(x, chip, far, gain, bias):
    rows, dim = x.shape
    tile = rows // 4
    spec = pl.BlockSpec((tile, dim), lambda i: (i, 0))
    return pl.pallas_call(
        norm_kernel,
        grid=(4,),
        out_shape=[jax.ShapeDtypeStruct((rows, dim), F32), jax.ShapeDtypeStruct((rows, dim), BF16)],
        in_specs=[spec, spec, spec, whole((1, dim)), whole((1, dim))],
        out_specs=[spec, spec],
        compiler_params=params(24),
        cost_estimate=cost(16 * rows * dim, 12 * rows * dim),
        name="norm",
    )(x, chip, far, gain, bias)


def norm_all_kernel(x_ref, gain_ref, bias_ref, out_ref):
    normed, _ = normalise(x_ref[...].astype(F32))
    out_ref[...] = (normed * gain_ref[...] + bias_ref[...]).astype(BF16)


def norm_all(x, gain, bias):
    rows, dim = x.shape
    tile = 128
    spec = pl.BlockSpec((tile, dim), lambda i: (i, 0))
    return pl.pallas_call(
        norm_all_kernel,
        grid=(rows // tile,),
        out_shape=jax.ShapeDtypeStruct((rows, dim), BF16),
        in_specs=[spec, whole((1, dim)), whole((1, dim))],
        out_specs=spec,
        compiler_params=params(24),
        cost_estimate=cost(16 * rows * dim, 4 * rows * dim),
        name="norm_all",
    )(x, gain, bias)


def norm_back_kernel(chip_ref, far_ref, x_ref, base_ref, gain_ref, wide_ref, low_ref, dg_ref, db_ref):
    grad = chip_ref[...].astype(F32) + far_ref[...].astype(F32)
    normed, inverse = normalise(x_ref[...].astype(F32))
    scaled = grad * gain_ref[...]
    back = inverse * (
        scaled
        - jnp.mean(scaled, axis=-1, keepdims=True)
        - normed * jnp.mean(scaled * normed, axis=-1, keepdims=True)
    )
    total = base_ref[...].astype(F32) + back
    wide_ref[...] = total
    low_ref[...] = total.astype(BF16)

    @pl.when(pl.program_id(0) == 0)
    def _():
        dg_ref[...] = jnp.zeros_like(dg_ref)
        db_ref[...] = jnp.zeros_like(db_ref)

    dg_ref[...] += jnp.sum(grad * normed, axis=0, keepdims=True)
    db_ref[...] += jnp.sum(grad, axis=0, keepdims=True)


def norm_back(chip, far, x, base, gain):
    rows, dim = chip.shape
    tile = rows // 4
    spec = pl.BlockSpec((tile, dim), lambda i: (i, 0))
    row = whole((1, dim))
    return pl.pallas_call(
        norm_back_kernel,
        grid=(4,),
        out_shape=[
            jax.ShapeDtypeStruct((rows, dim), F32),
            jax.ShapeDtypeStruct((rows, dim), BF16),
            jax.ShapeDtypeStruct((1, dim), F32),
            jax.ShapeDtypeStruct((1, dim), F32),
        ],
        in_specs=[spec] * 4 + [row],
        out_specs=[spec, spec, row, row],
        compiler_params=params(24),
        cost_estimate=cost(30 * rows * dim, 18 * rows * dim),
        name="norm_back",
    )(chip, far, x, base, gain)


def feed_kernel(mine_ref, other_ref, w_ref, gact_ref, keep_ref, act_ref, du_ref, *refs):
    half = mine_ref.shape[0]
    weights = w_ref[...]
    for at, ref in ((0, mine_ref), (half, other_ref)):
        rows = slice(at, at + half)
        relu = jnp.maximum(nn(ref[...], weights), 0.0) * keep_ref[rows, :]
        act_ref[rows, :] = (relu * relu).astype(BF16)
        du_ref[rows, :] = (gact_ref[rows, :].astype(F32) * 2.0 * relu).astype(BF16)
    if refs:
        keep_out, give_out, acc_ref = refs
        step = pl.program_id(0)

        @pl.when(step == 0)
        def _():
            acc_ref[...] = nt(du_ref[...], weights)

        @pl.when(step > 0)
        def _():
            acc_ref[...] += nt(du_ref[...], weights)

        @pl.when(step == pl.num_programs(0) - 1)
        def _():
            keep_out[...] = acc_ref[:half, :].astype(BF16)
            give_out[...] = acc_ref[half:, :].astype(BF16)


def feed_forward(mine, other, w_up, gact, keep, with_back):
    half, dim = mine.shape
    hidden = w_up.shape[1]
    tile = min(hidden, 512)
    tall = jax.ShapeDtypeStruct((2 * half, hidden), BF16)
    part = jax.ShapeDtypeStruct((half, dim), BF16)
    spec = pl.BlockSpec((2 * half, tile), lambda i: (0, i))
    return pl.pallas_call(
        feed_kernel,
        grid=(hidden // tile,),
        out_shape=[tall, tall] + ([part, part] if with_back else []),
        in_specs=[
            whole((half, dim)),
            whole((half, dim)),
            pl.BlockSpec((dim, tile), lambda i: (0, i)),
            spec,
            whole((2 * half, 1)),
        ],
        out_specs=[spec, spec] + ([whole((half, dim))] * 2 if with_back else []),
        scratch_shapes=[pltpu.VMEM((2 * half, dim), F32)] if with_back else [],
        compiler_params=params(48),
        cost_estimate=cost((8 if with_back else 4) * half * dim * hidden, 16 * 2**20),
        name="feed_own" if with_back else "feed_far",
    )(mine, other, w_up, gact, keep)


def back_act_kernel(mine_ref, other_ref, w_ref, out_ref):
    half = mine_ref.shape[0]
    out_ref[:half, :] = nt(mine_ref[...], w_ref[...]).astype(BF16)
    out_ref[half:, :] = nt(other_ref[...], w_ref[...]).astype(BF16)


def back_act(mine, other, w_down):
    half, dim = mine.shape
    hidden = w_down.shape[0]
    tile = min(hidden, 512)
    return pl.pallas_call(
        back_act_kernel,
        grid=(hidden // tile,),
        out_shape=jax.ShapeDtypeStruct((2 * half, hidden), BF16),
        in_specs=[
            whole((half, dim)),
            whole((half, dim)),
            pl.BlockSpec((tile, dim), lambda i: (i, 0)),
        ],
        out_specs=pl.BlockSpec((2 * half, tile), lambda i: (0, i)),
        compiler_params=params(40),
        cost_estimate=cost(4 * half * dim * hidden, 12 * 2**20),
        name="back_act",
    )(mine, other, w_down)


def quad_product_kernel(idx, *refs):
    cols, rows, (give_ref, keep_ref, turn_ref) = refs[:16], refs[16:20], refs[20:]
    block = give_ref.shape[0]
    half = cols[0].shape[0]

    @pl.when(pl.program_id(0) == 0)
    def _():
        for j in range(2):
            for k in range(8):
                turn_ref[j * block : (j + 1) * block, k * half : (k + 1) * half] = (
                    cols[8 * j + k][...].astype(F32).T.astype(BF16)
                )

    tok = 2 * half
    for j, out in ((0, give_ref), (1, keep_ref)):
        total = None
        for k, ref in enumerate(rows):
            term = nn(turn_ref[j * block : (j + 1) * block, k * tok : (k + 1) * tok], ref[...])
            total = term if total is None else total + term
        out[...] = total.astype(out.dtype)


def quad_product(idx, cols, rows):
    half, dim = cols[0].shape
    tok, width = rows[0].shape
    block = dim // (2 * HEADS)
    tile = min(width, 512)
    give = pl.BlockSpec((half, block), lambda i, idx: (0, 2 * (idx[0] ^ 2) + idx[1]))
    keep = pl.BlockSpec((half, block), lambda i, idx: (0, 2 * idx[0] + idx[1]))
    out = pl.BlockSpec((block, tile), lambda i, idx: (0, i))
    return pl.pallas_call(
        quad_product_kernel,
        grid_spec=pltpu.PrefetchScalarGridSpec(
            num_scalar_prefetch=1,
            grid=(width // tile,),
            in_specs=[give] * 8
            + [keep] * 8
            + [pl.BlockSpec((tok, tile), lambda i, idx: (0, i))] * 4,
            out_specs=[out, out],
            scratch_shapes=[pltpu.VMEM((2 * block, 8 * half), BF16)],
        ),
        out_shape=[
            jax.ShapeDtypeStruct((block, width), BF16),
            jax.ShapeDtypeStruct((block, width), F32),
        ],
        compiler_params=params(40),
        cost_estimate=cost(16 * half * block * width * 2, 16 * 2**20),
        name="quad_product",
    )(idx, *cols, *cols, *rows)


def product_kernel(idx, *refs):
    cols, near_ref, far_ref, out_ref, turn_ref = refs[:4], refs[4], refs[5], refs[6], refs[7]
    half = cols[0].shape[0]
    for k, ref in enumerate(cols):
        turn_ref[:, k * half : (k + 1) * half] = ref[...].astype(F32).T.astype(BF16)
    width = out_ref.shape[1]
    tile = min(width, 512)
    starts = [pl.multiple_of(idx[3 + j] * half, half) for j in range(2)]
    for at in range(0, width, tile):
        lanes = slice(at, at + tile)
        total = None
        for k in range(4):
            rows = (near_ref, far_ref)[k // 2][pl.ds(starts[k % 2], half), lanes]
            term = nn(turn_ref[:, k * half : (k + 1) * half], rows)
            total = term if total is None else total + term
        out_ref[:, lanes] = total.astype(BF16)


def product(idx, cols, near, far):
    half, dim = cols[0].shape
    tok, width = near.shape
    block = dim // (2 * HEADS)
    spec = pl.BlockSpec((half, block), lambda k, idx: (0, 2 * k + idx[1]))
    return pl.pallas_call(
        product_kernel,
        grid_spec=pltpu.PrefetchScalarGridSpec(
            num_scalar_prefetch=1,
            grid=(HEADS,),
            in_specs=[spec] * 4 + [whole((tok, width))] * 2,
            out_specs=pl.BlockSpec((block, width), lambda k, idx: (k, 0)),
            scratch_shapes=[pltpu.VMEM((block, 4 * half), BF16)],
        ),
        out_shape=jax.ShapeDtypeStruct((HEADS * block, width), BF16),
        compiler_params=params(40),
        cost_estimate=cost(2 * tok * width * dim, 12 * 2**20),
        name="product",
    )(idx, *cols, near, far)


def head_product_kernel(idx, h_ref, dkv_ref, *refs):
    dq_refs, (give_ref, keep_ref, turn_ref) = refs[:HEADS], refs[HEADS:]
    tok = dq_refs[0].shape[0]
    first = (pl.program_id(0) == 0) & (pl.program_id(1) == 0)

    @pl.when(first)
    def _():
        for k, ref in enumerate(dq_refs):
            turn_ref[:HD, k * tok : (k + 1) * tok] = ref[...].astype(F32).T.astype(BF16)
            rows = slice(k * tok, (k + 1) * tok)
            turn_ref[HD:, rows] = dkv_ref[rows, :].astype(F32).T.astype(BF16)

    total = None
    for k in range(HEADS):
        rows = h_ref[pl.ds(pl.multiple_of((idx[0] ^ k) * tok, tok), tok), :]
        term = nn(turn_ref[:, k * tok : (k + 1) * tok], rows)
        total = term if total is None else total + term

    @pl.when(pl.program_id(0) == 0)
    def _():
        give_ref[0] = total.astype(BF16)

    @pl.when(pl.program_id(0) == 1)
    def _():
        keep_ref[0] = total.astype(BF16)


def head_product(idx, h_all, dkv, dq_pieces):
    rows, dim = h_all.shape
    block = dim // (2 * HEADS)
    out = jax.ShapeDtypeStruct((HEADS, 3 * HD, block), BF16)

    def columns(turn, k, idx):
        return (0, (idx[0] ^ k) * 2 + jnp.where(turn == 0, 1 - idx[1], idx[1]))

    return pl.pallas_call(
        head_product_kernel,
        grid_spec=pltpu.PrefetchScalarGridSpec(
            num_scalar_prefetch=1,
            grid=(2, HEADS),
            in_specs=[pl.BlockSpec((rows, block), columns), whole((rows, 2 * HD))]
            + [whole((rows // HEADS, HD))] * HEADS,
            out_specs=[
                pl.BlockSpec(
                    (1, 3 * HD, block),
                    lambda turn, k, idx: (jnp.where(turn == 0, k, HEADS - 1), 0, 0),
                ),
                pl.BlockSpec(
                    (1, 3 * HD, block), lambda turn, k, idx: (jnp.where(turn == 0, 0, k), 0, 0)
                ),
            ],
            scratch_shapes=[pltpu.VMEM((3 * HD, rows), BF16)],
        ),
        out_shape=[out, out],
        compiler_params=params(40),
        cost_estimate=cost(2 * rows * dim * 3 * HD, 12 * 2**20),
        name="head_product",
    )(idx, h_all, dkv, *dq_pieces)


def head_place_kernel(idx, *refs):
    pieces, out_ref = refs[:HEADS], refs[HEADS]
    for k, piece in enumerate(pieces):
        for s in range(3):
            out_ref[s, :, pl.ds(pl.multiple_of((idx[0] ^ k) * HD, HD), HD)] = (
                piece[s * HD : (s + 1) * HD, :].astype(F32).T
            )


def head_place(idx, pieces):
    rows, block = pieces[0].shape
    return pl.pallas_call(
        head_place_kernel,
        out_shape=jax.ShapeDtypeStruct((3, block, HEADS * HD), F32),
        in_specs=[SMEM] + [VMEM] * HEADS,
        out_specs=VMEM,
        compiler_params=params(24),
        cost_estimate=cost(rows * block * 8, 4 * 2**20),
        name="head_place",
    )(idx, *pieces)


def project_back_kernel(idx, w_ref, *refs):
    dq_refs, dkv_refs = refs[:HEADS], refs[HEADS : 2 * HEADS]
    keep_ref, give_ref, flat_ref, acc_ref = refs[2 * HEADS :]
    half = keep_ref.shape[0]
    core = idx[2]
    step = pl.program_id(0)

    for s in range(3):

        @pl.when(step == s)
        def _(s=s):
            for k in range(HEADS):
                lanes = pl.ds(pl.multiple_of((idx[0] ^ k) * HD, HD), HD)
                if s == 0:
                    flat_ref[:, lanes] = dq_refs[k][...]
                else:
                    flat_ref[:, lanes] = dkv_refs[k][:, (s - 1) * HD : s * HD]

    @pl.when(step == 0)
    def _():
        acc_ref[...] = nt(flat_ref[...], w_ref[0])

    @pl.when(step > 0)
    def _():
        acc_ref[...] += nt(flat_ref[...], w_ref[0])

    @pl.when(step == 2)
    def _():
        give_ref[...] = acc_ref[pl.ds(pl.multiple_of((1 - core) * half, half), half), :].astype(BF16)
        keep_ref[...] = acc_ref[pl.ds(pl.multiple_of(core * half, half), half), :].astype(BF16)


def project_back(idx, w_qkv, dq_pieces, dkv_pieces):
    tok = dq_pieces[0].shape[0]
    _, dim, cols = w_qkv.shape
    part = jax.ShapeDtypeStruct((tok // 2, dim), BF16)
    return pl.pallas_call(
        project_back_kernel,
        grid_spec=pltpu.PrefetchScalarGridSpec(
            num_scalar_prefetch=1,
            grid=(3,),
            in_specs=[pl.BlockSpec((1, dim, cols), lambda s, idx: (s, 0, 0))]
            + [whole((tok, HD))] * HEADS
            + [whole((tok, 2 * HD))] * HEADS,
            out_specs=[whole((tok // 2, dim))] * 2,
            scratch_shapes=[pltpu.VMEM((tok, cols), BF16), pltpu.VMEM((tok, dim), F32)],
        ),
        out_shape=[part, part],
        compiler_params=params(40),
        cost_estimate=cost(6 * tok * dim * cols, 12 * 2**20),
        name="project_back",
    )(idx, w_qkv, *dq_pieces, *dkv_pieces)


def join_kernel(idx, mine_ref, other_ref, out_ref):
    half = mine_ref.shape[0]
    core = idx[2]
    out_ref[pl.ds(pl.multiple_of(core * half, half), half), :] = mine_ref[...].astype(out_ref.dtype)
    out_ref[pl.ds(pl.multiple_of((1 - core) * half, half), half), :] = other_ref[...].astype(
        out_ref.dtype
    )


def join(idx, mine, other, dtype):
    half, dim = mine.shape
    return pl.pallas_call(
        join_kernel,
        out_shape=jax.ShapeDtypeStruct((2 * half, dim), dtype),
        in_specs=[SMEM, VMEM, VMEM],
        out_specs=VMEM,
        compiler_params=params(24),
        cost_estimate=cost(half * dim, 8 * half * dim),
        name="join",
    )(idx, mine, other)


def body(
    depth,
    layer_input,
    ln1_gain,
    ln1_bias,
    w_qkv,
    w_out,
    ln2_gain,
    ln2_bias,
    w_up,
    w_down,
    buckets,
    lengths,
    block_order,
    grad_out,
):
    tok, dim = layer_input.shape
    half = tok // 2
    scale = 1.0 / math.sqrt(HD)
    r, h, y, x, c = (lax.axis_index(a) for a in BLK + TP)
    blk = lax.axis_index(BLK)
    tp = lax.axis_index(TP)
    idx = jnp.stack([h, y, c, jnp.zeros_like(c), jnp.ones_like(c)]).astype(jnp.int32)
    idx_rows = jnp.stack([h, y, c, c, 1 - c]).astype(jnp.int32)
    gains = [v.reshape(1, dim) for v in (ln1_gain, ln1_bias, ln2_gain, ln2_bias)]

    def half_of(values, which):
        return lax.dynamic_slice_in_dim(values, which * half, half, 0)

    def regroup(values):
        if depth == 1:
            return values
        rows = values.shape[0]
        split = values.reshape(rows, depth, HEADS, 2, dim // (2 * HEADS * depth))
        return split.transpose(0, 2, 3, 1, 4).reshape(rows, dim)

    def scatter(values):
        if depth > 1:
            split = values.reshape(HEADS, depth, -1, values.shape[1])
            values = split.transpose(1, 0, 2, 3).reshape(values.shape)
        return lax.psum_scatter(values, ("r", "h"), scatter_dimension=0, tiled=True)

    starts = jnp.cumsum(lengths) - lengths

    def firsts_of(places):
        return jnp.max(jnp.where(starts <= places[..., None], starts, 0), axis=-1)

    inside = jnp.arange(half, dtype=jnp.int32)
    own_places = (
        lax.dynamic_slice_in_dim(block_order, 2 * blk, 2, 0)[:, None] * half + inside
    ).reshape(tok)
    cosine, sine = rotary_tables(own_places - firsts_of(own_places))

    group_buckets = lax.all_gather(buckets, ("h", "y"), axis=0, tiled=True)
    group_buckets = group_buckets.reshape(HEADS, 2, 2, half)

    def row_mask(plane, parity):
        chosen = lax.dynamic_slice(group_buckets, (plane, parity, 0, 0), (1, 1, 2, half))
        kept = (chosen.reshape(2, half) >= tp).astype(F32)
        return jnp.where(c == 0, kept, kept[::-1]).reshape(tok, 1)

    grad_mine, grad_other = half_of(grad_out, c), half_of(grad_out, 1 - c)
    y_grad = swap(grad_mine, "y")

    projected = project(idx, layer_input, gains[0], gains[1], cosine, sine, w_qkv)
    queries, near_kv = list(projected[:HEADS]), list(projected[HEADS:])
    near_kv = [near_kv[0]] + [plane_swap(near_kv[k], k) for k in range(1, HEADS)]
    queries = [queries[0]] + [plane_swap(queries[k], k) for k in range(1, HEADS)]

    relative = h ^ jnp.arange(HEADS, dtype=jnp.int32)
    group_order = lax.dynamic_index_in_dim(
        block_order.reshape(depth, HEADS, 2, 2), r, 0, keepdims=False
    )
    group_order = lax.dynamic_index_in_dim(group_order, y, 1, keepdims=False)
    chosen = relative[:, None] == jnp.arange(HEADS, dtype=jnp.int32)[None, :]
    query_at = jnp.sum(jnp.where(chosen[:, :, None], group_order[None], 0), axis=1).reshape(-1)
    query_places = query_at[:, None] * half + inside
    query_firsts = firsts_of(query_places)
    query_low = query_firsts[:, 0] // half
    block_count = block_order.shape[0]
    slots = jnp.argmax(
        block_order[None, :] == jnp.arange(block_count, dtype=jnp.int32)[:, None], axis=1
    ).astype(jnp.int32)
    slot_dev = slots // 2
    slot_plane = slot_dev // 2
    key_row = (
        jnp.where(slot_dev % 2 == y, 0, block_count // 2)
        + slot_plane // HEADS * (2 * HEADS)
        + ((slot_plane % HEADS) ^ h) * 2
        + slots % 2
    )
    group_cos, group_sin = rotary_tables((query_places - query_firsts).reshape(2 * HEADS * half))
    tables = (query_at, query_low, key_row, query_firsts.reshape(2 * HEADS, 1, half))

    quarter = lax.dynamic_slice_in_dim(layer_input, tp * (tok // 4), tok // 4, 0)
    quarter, near_kv[3] = ordered(quarter, near_kv[3])
    x_all = lax.all_gather(quarter, ("h",) + TP, axis=0, tiled=True)

    if depth == 1:
        keys_values = near_kv + [swap(v, "y") for v in near_kv]
    else:
        near_all = lax.all_gather(jnp.concatenate(near_kv), "r", axis=0, tiled=True)
        keys_values = [near_all, swap(near_all, "y")]
    for_plane, queries[3] = ordered(grad_mine, queries[3])
    z_grad = plane_swap(for_plane, 1)

    y_grad_other = swap(y_grad, "c")
    grad_act = back_act(grad_mine, grad_other, w_down)
    y_grad_act = back_act(y_grad, y_grad_other, w_down)
    masks = [row_mask(h ^ kz, y ^ ky) for kz in range(2) for ky in range(2)]
    grad_act, y_grad_act, group_cos, group_sin, keys_values[-1], *masks = ordered(
        grad_act, y_grad_act, group_cos, group_sin, keys_values[-1], *masks
    )

    *attended, lse = attend(half, scale, tables, queries, keys_values)
    z_grad, attended[1] = ordered(z_grad, attended[1])
    zy_grad = swap(z_grad, "y")
    pieces = [attended[0]] + [plane_swap(attended[k], k) for k in range(1, HEADS)]
    flat, keep, give = out_project(idx, w_out, pieces)

    def chip_sum(keep, give):
        return (keep.astype(F32) + swap(give, "c").astype(F32)).astype(BF16)

    chip = chip_sum(keep, give)
    chip_far = swap(chip, "x")
    z_grad_other, zy_grad_other = swap(z_grad, "c"), swap(zy_grad, "c")
    z_grad_act = back_act(z_grad, z_grad_other, w_down)
    zy_grad_act = back_act(zy_grad, zy_grad_other, w_down)
    h_all = regroup(norm_all(x_all, gains[0], gains[1]))
    z_grad_act, zy_grad_act, h_all, chip_far = ordered(z_grad_act, zy_grad_act, h_all, chip_far)

    x_mid, h_mine = norm(half_of(layer_input, c), chip, chip_far, gains[2], gains[3])
    h_other = swap(h_mine, "c")
    y_h = swap(h_mine, "y")
    z_h = plane_swap(h_mine, 1)
    act, du, keep, give = feed_forward(h_mine, h_other, w_up, grad_act, masks[0], True)
    chip = chip_sum(keep, give)
    chip_far = swap(chip, "x")

    y_h_other = swap(y_h, "c")
    y_act, y_du = feed_forward(y_h, y_h_other, w_up, y_grad_act, masks[1], False)
    zy_h = swap(z_h, "y")
    z_h_other = swap(z_h, "c")
    z_act, z_du = feed_forward(z_h, z_h_other, w_up, z_grad_act, masks[2], False)
    y_act, z_act, chip_far = ordered(y_act, z_act, chip_far)

    grad_mid, dy_mine, gain_two_grad, bias_two_grad = norm_back(
        chip, chip_far, x_mid, grad_mine, gains[2]
    )
    dy_other = swap(dy_mine, "c")
    grads = list(out_back(idx, w_out, dy_mine, dy_other))
    grads = [grads[0]] + [plane_swap(grads[k], k) for k in range(1, HEADS)]
    y_dy = swap(dy_mine, "y")
    y_flat = swap(flat, "y")

    zy_h_other = swap(zy_h, "c")
    zy_act, zy_du = feed_forward(zy_h, zy_h_other, w_up, zy_grad_act, masks[3], False)
    quad_grads = [grad_mine, grad_other, y_grad, y_grad_other, z_grad, z_grad_other, zy_grad, zy_grad_other]
    down_give, down_keep = quad_product(
        idx, [regroup(v) for v in quad_grads], [act, y_act, z_act, zy_act]
    )
    down_give, grads[3] = ordered(down_give, grads[3])
    down_got = plane_swap(down_give, 2)

    *dq, near, far = attend_back(
        half, scale, tables, lse, group_cos, group_sin, queries, keys_values, attended, grads
    )
    got = swap(far, "y")
    dq_pieces = [dq[0]] + [plane_swap(dq[k], k) for k in range(1, HEADS)]

    quad_rows = [h_mine, h_other, y_h, y_h_other, z_h, z_h_other, zy_h, zy_h_other]
    first_row, near = ordered(quad_rows[0], near)
    quad_rows[0] = first_row
    up_give, up_keep = quad_product(
        idx, [regroup(v) for v in quad_rows], [du, y_du, z_du, zy_du]
    )
    feed_act, near = ordered(act, near)
    feed = [
        jnp.dot(feed_act[s], w_down, preferred_element_type=F32).astype(BF16)
        for s in (slice(half), slice(half, tok))
    ]
    up_give, feed[0], feed[1], got = ordered(up_give, feed[0], feed[1], got)
    up_got = plane_swap(up_give, 2)
    feed_chip = chip_sum(feed[0], feed[1])
    feed_far = swap(feed_chip, "x")

    if depth > 1:
        near = lax.psum_scatter(near, "r", scatter_dimension=0, tiled=True)
        got = lax.psum_scatter(got, "r", scatter_dimension=0, tiled=True)
    dkv = settle(near, got, group_cos, group_sin)
    dkv_pieces = [dkv[:tok]] + [
        plane_swap(dkv[k * tok : (k + 1) * tok], k) for k in range(1, HEADS)
    ]

    head_give, head_keep = head_product(idx, h_all, dkv, dq)
    y_dy_other = swap(y_dy, "c")
    wout_cols = [regroup(v) for v in (dy_mine, dy_other, y_dy, y_dy_other)]
    wout_cols[0], dkv_pieces[0] = ordered(wout_cols[0], dkv_pieces[0])
    wout_sum = product(idx_rows, wout_cols, flat, y_flat)
    head_give, wout_sum, dkv_pieces[3] = ordered(head_give, wout_sum, dkv_pieces[3])
    wout_part = scatter(wout_sum)
    keep, give = project_back(idx, w_qkv, dq_pieces, dkv_pieces)
    head_got = swap(head_give, "y")
    chip = chip_sum(keep, give)
    chip_far = swap(chip, "x")

    head_sum = (head_keep.astype(F32) + head_got.astype(F32)).astype(BF16)
    if depth > 1:
        head_sum = lax.psum_scatter(head_sum, "r", scatter_dimension=2, tiled=True)
    head_pieces = [head_sum[0]] + [plane_swap(head_sum[k], k) for k in range(1, HEADS)]
    down_part = down_keep + down_got.astype(F32)
    up_part = up_keep + up_got.astype(F32)
    if depth > 1:
        down_part, up_part = (
            lax.psum_scatter(v, "r", scatter_dimension=0, tiled=True) for v in (down_part, up_part)
        )
    out_mine = (x_mid + (feed_chip.astype(F32) + feed_far.astype(F32))).astype(BF16)
    out_other = swap(out_mine, "c")
    layer_output = join(idx, out_mine, out_other, BF16)
    layer_output, chip_far = ordered(layer_output, chip_far)

    _, grad_low, gain_one_grad, bias_one_grad = norm_back(
        chip, chip_far, half_of(layer_input, c), grad_mid, gains[0]
    )
    grad_input = join(idx, grad_low, swap(grad_low, "c"), F32)
    qkv_part = head_place(idx, head_pieces)

    counts = jnp.sum(
        (half_of(buckets, c)[:, None] == jnp.arange(NB, dtype=jnp.int32)[None, :]).astype(F32),
        axis=0,
    )
    sums = jnp.concatenate(
        [v.reshape(dim) for v in (gain_one_grad, bias_one_grad, gain_two_grad, bias_two_grad)]
        + [counts]
    )
    if depth > 1:
        sums = lax.psum(sums, "r")
    sums = sums + swap(sums, "c")
    sums = sums + swap(sums, "y")
    one, two, three = (plane_swap(sums, k) for k in range(1, HEADS))
    sums = (sums + one) + (two + three)
    return (
        layer_output,
        grad_input,
        sums[:dim],
        sums[dim : 2 * dim],
        qkv_part,
        wout_part.astype(F32).T,
        sums[2 * dim : 3 * dim],
        sums[3 * dim : 4 * dim],
        up_part,
        down_part.T,
        sums[4 * dim :].astype(jnp.int32),
    )


def solution(mesh):
    depth = mesh.shape["blk"] // (2 * HEADS)
    fine = Mesh(mesh.devices.reshape(depth, HEADS, 2, 2, 2), BLK + TP)
    return jax.shard_map(
        functools.partial(body, depth),
        mesh=fine,
        in_specs=(
            P(BLK, None),
            P(),
            P(),
            P(None, None, TP),
            P(TP, None),
            P(),
            P(),
            P(None, TP),
            P(TP, None),
            P(BLK),
            P(),
            P(),
            P(BLK, None),
        ),
        out_specs=(
            P(BLK, None),
            P(BLK, None),
            P(),
            P(),
            P(None, BLK, TP),
            P(TP, BLK),
            P(),
            P(),
            P(BLK, TP),
            P(TP, BLK),
            P(),
        ),
        check_vma=False,
    )
```

```python
import functools
import math

import jax
import jax.numpy as jnp
from jax import lax
from jax.experimental import pallas as pl
from jax.experimental.pallas import tpu as pltpu
from jax.sharding import Mesh
from jax.sharding import PartitionSpec as P

HD = 128
FF = 8192
NB = 4
HEADS = 4
EPSILON = 1e-05
ROPE_BASE = 10000.0
PLANE = ("hh", "hl")
BLK = ("r", "hh", "hl", "y")
TP = ("x", "c")
F32 = jnp.float32
BF16 = jnp.bfloat16
SMEM = pl.BlockSpec(memory_space=pltpu.SMEM)
VMEM = pl.BlockSpec(memory_space=pltpu.VMEM)
ANY = pl.BlockSpec(memory_space=pl.ANY)


def swap(value, axis):
    return lax.ppermute(value, axis, [(0, 1), (1, 0)])


def plane_swap(value, k):
    return lax.ppermute(value, PLANE, [(i, i ^ k) for i in range(HEADS)])


def ordered(*values):
    return lax.optimization_barrier(values)


def nt(lhs, rhs):
    return lax.dot_general(lhs, rhs, (((1,), (1,)), ((), ())), preferred_element_type=F32)


def tn(lhs, rhs):
    return lax.dot_general(lhs, rhs, (((0,), (0,)), ((), ())), preferred_element_type=F32)


def nn(lhs, rhs):
    return lax.dot_general(lhs, rhs, (((1,), (0,)), ((), ())), preferred_element_type=F32)


def params(mib):
    return pltpu.CompilerParams(vmem_limit_bytes=60 * 2**20)


def cost(flops, moved):
    return pl.CostEstimate(
        flops=int(flops) // 10**6, bytes_accessed=int(moved) // 10**6, transcendentals=0
    )


def whole(shape):
    return pl.BlockSpec(shape, lambda *_: (0,) * len(shape))


def normalise(values):
    centre = values - jnp.mean(values, axis=-1, keepdims=True)
    inverse = lax.rsqrt(jnp.mean(centre * centre, axis=-1, keepdims=True) + EPSILON)
    return (centre * inverse, inverse)


def rotary_tables(positions):
    freqs = ROPE_BASE ** (-(jnp.arange(HD // 2, dtype=F32) * 2.0 / HD))
    angles = positions.astype(F32)[:, None] * freqs[None, :]
    cosine, sine = jnp.cos(angles), jnp.sin(angles)
    return (
        jnp.concatenate([cosine, cosine], axis=-1),
        jnp.concatenate([-sine, sine], axis=-1),
    )


def rotate(values, cosine, sine):
    return values * cosine + pltpu.roll(values, HD // 2, 1) * sine


def project_kernel(idx, x_ref, gain_ref, bias_ref, cos_ref, sin_ref, w_ref, *refs):
    h_ref, q_outs, kv_outs = refs[0], refs[1 : 1 + HEADS], refs[1 + HEADS :]
    step = pl.program_id(0)

    @pl.when(step == 0)
    def _():
        normed, _ = normalise(x_ref[...].astype(F32))
        h_ref[...] = (normed * gain_ref[...] + bias_ref[...]).astype(BF16)

    both = nn(h_ref[...], jnp.concatenate([w_ref[0], w_ref[1]], axis=1))
    cosine, sine = cos_ref[...], sin_ref[...]
    queries = rotate(both[:, :HD], cosine, sine).astype(BF16)
    keys = rotate(both[:, HD:], cosine, sine).astype(BF16)
    values = nn(h_ref[...], w_ref[2]).astype(BF16)
    for k in range(HEADS):

        @pl.when(step == k)
        def _(k=k):
            q_outs[k][...] = queries
            kv_outs[k][:, :HD] = keys
            kv_outs[k][:, HD:] = values


def project(idx, x, gain, bias, cosine, sine, w_qkv):
    tok, dim = x.shape
    return pl.pallas_call(
        project_kernel,
        grid_spec=pltpu.PrefetchScalarGridSpec(
            num_scalar_prefetch=1,
            grid=(HEADS,),
            in_specs=[
                whole((tok, dim)),
                whole((1, dim)),
                whole((1, dim)),
                whole((tok, HD)),
                whole((tok, HD)),
                pl.BlockSpec((3, dim, HD), lambda k, idx: (0, 0, idx[0] ^ k)),
            ],
            out_specs=[whole((tok, dim))]
            + [whole((tok, HD))] * HEADS
            + [whole((tok, 2 * HD))] * HEADS,
        ),
        out_shape=[jax.ShapeDtypeStruct((tok, dim), BF16)]
        + [jax.ShapeDtypeStruct((tok, HD), BF16)] * HEADS
        + [jax.ShapeDtypeStruct((tok, 2 * HD), BF16)] * HEADS,
        compiler_params=params(40),
        cost_estimate=cost(2 * tok * dim * 12 * HD, 10 * 2**20),
        name="project",
    )(idx, x, gain, bias, cosine, sine, w_qkv)


def visible_of(tile, key_block, query_places, query_firsts):
    key_places = key_block * tile + lax.broadcasted_iota(jnp.int32, (tile, 1), 0)
    return (key_places <= query_places) & (key_places >= query_firsts)


def gather_refs(refs, whole_ref):
    at = 0
    for ref in refs:
        whole_ref[at : at + ref.shape[0], :] = ref[...]
        at += ref.shape[0]


def attend_kernel(tile, scale, n_kv, at_ref, low_ref, row_ref, first_ref, *refs):
    q_refs, kv_refs, refs = refs[:HEADS], refs[HEADS : HEADS + n_kv], refs[HEADS + n_kv :]
    outs, (lse_ref, q_all, kv_all) = refs[:HEADS], refs[HEADS:]
    gather_refs(q_refs, q_all)
    gather_refs(kv_refs, kv_all)
    lanes = lax.broadcasted_iota(jnp.int32, (1, tile), 1)
    per_out = outs[0].shape[0] // tile

    for k, out in enumerate(outs):

        def one_block(j, carry, k=k, out=out):
            i = k * per_out + j
            queries = q_all[pl.ds(pl.multiple_of(i * tile, tile), tile), :]
            firsts = first_ref[i]
            places = at_ref[i] * tile + lanes

            def one_step(b, state):
                run_max, run_sum, run_acc = state
                krows = pl.ds(pl.multiple_of(row_ref[b] * tile, tile), tile)
                scores = nt(kv_all[krows, :HD], queries) * scale
                visible = visible_of(tile, b, places, firsts)
                scores = jnp.where(visible, scores, -1e30)
                new_max = jnp.maximum(run_max, jnp.max(scores, axis=0, keepdims=True))
                factor = jnp.exp(run_max - new_max)
                probs = jnp.where(visible, jnp.exp(scores - new_max), 0.0)
                new_sum = run_sum * factor + jnp.sum(probs, axis=0, keepdims=True)
                new_acc = run_acc * factor + tn(kv_all[krows, HD:], probs.astype(BF16))
                return (new_max, new_sum, new_acc)

            run_max, run_sum, run_acc = lax.fori_loop(
                low_ref[i],
                at_ref[i] + 1,
                one_step,
                (
                    jnp.full((1, tile), -1e30, F32),
                    jnp.zeros((1, tile), F32),
                    jnp.zeros((HD, tile), F32),
                ),
            )
            out[pl.ds(pl.multiple_of(j * tile, tile), tile), :] = (run_acc / run_sum).T.astype(BF16)
            lse_ref[i] = run_max + jnp.log(run_sum)
            return carry

        lax.fori_loop(0, per_out, one_block, 0)


def attend_back_kernel(
    tile, scale, n_kv, at_ref, low_ref, row_ref, first_ref, lse_ref, cos_ref, sin_ref, *refs
):
    q_refs, kv_refs, refs = refs[:HEADS], refs[HEADS : HEADS + n_kv], refs[HEADS + n_kv :]
    o_refs, do_refs, dq_refs = refs[:HEADS], refs[HEADS : 2 * HEADS], refs[2 * HEADS : 3 * HEADS]
    near_ref, far_ref, q_all, kv_all, acc_ref = refs[3 * HEADS :]
    gather_refs(q_refs, q_all)
    gather_refs(kv_refs, kv_all)
    acc_ref[...] = jnp.zeros_like(acc_ref)
    lanes = lax.broadcasted_iota(jnp.int32, (1, tile), 1)
    per_out = dq_refs[0].shape[0] // tile

    for k in range(HEADS):

        def one_block(j, carry, k=k):
            i = k * per_out + j
            rows = pl.ds(pl.multiple_of(i * tile, tile), tile)
            piece = pl.ds(pl.multiple_of(j * tile, tile), tile)
            queries = q_all[rows, :]
            grads = do_refs[k][piece, :]
            firsts = first_ref[i]
            places = at_ref[i] * tile + lanes
            log_sums = lse_ref[i]
            products = grads.astype(F32) * o_refs[k][piece, :].astype(F32)
            deltas = jnp.sum(products.T, axis=0, keepdims=True)

            def one_step(b, grad_q):
                krows = pl.ds(pl.multiple_of(row_ref[b] * tile, tile), tile)
                keys = kv_all[krows, :HD]
                scores = nt(keys, queries) * scale
                visible = visible_of(tile, b, places, firsts)
                probs = jnp.where(visible, jnp.exp(scores - log_sums), 0.0)
                grad_probs = nt(kv_all[krows, HD:], grads)
                grad_scores = (probs * (grad_probs - deltas)).astype(BF16)
                acc_ref[krows, HD:] += nn(probs.astype(BF16), grads)
                acc_ref[krows, :HD] += nn(grad_scores, queries)
                return grad_q + tn(keys, grad_scores)

            grad_q = lax.fori_loop(low_ref[i], at_ref[i] + 1, one_step, jnp.zeros((HD, tile), F32))
            dq_refs[k][piece, :] = rotate(
                (grad_q * scale).T, cos_ref[rows, :], -sin_ref[rows, :]
            ).astype(BF16)
            return carry

        lax.fori_loop(0, per_out, one_block, 0)
    near = near_ref.shape[0]
    near_ref[:, :HD] = (acc_ref[:near, :HD] * scale).astype(BF16)
    near_ref[:, HD:] = acc_ref[:near, HD:].astype(BF16)
    far_ref[:, :HD] = (acc_ref[near:, :HD] * scale).astype(BF16)
    far_ref[:, HD:] = acc_ref[near:, HD:].astype(BF16)


def attend(tile, scale, tables, pieces, keys_values):
    rows = HEADS * pieces[0].shape[0]
    kv_rows = sum(a.shape[0] for a in keys_values)
    operands = pieces + keys_values
    return pl.pallas_call(
        functools.partial(attend_kernel, tile, scale, len(keys_values)),
        out_shape=[jax.ShapeDtypeStruct((rows // HEADS, HD), BF16)] * HEADS
        + [jax.ShapeDtypeStruct((rows // tile, 1, tile), F32)],
        in_specs=[SMEM] * 3 + [VMEM] * (1 + len(operands)),
        out_specs=[VMEM] * (HEADS + 1),
        scratch_shapes=[pltpu.VMEM((rows, HD), BF16), pltpu.VMEM((kv_rows, 2 * HD), BF16)],
        compiler_params=params(50),
        cost_estimate=cost(4 * rows * 1280 * HD, 4 * 2**20),
        name="attend",
    )(*tables, *operands)


def attend_back(tile, scale, tables, lse, cosine, sine, pieces, keys_values, outs, grads):
    rows = HEADS * pieces[0].shape[0]
    kv_rows = sum(a.shape[0] for a in keys_values)
    operands = pieces + keys_values + outs + grads
    return pl.pallas_call(
        functools.partial(attend_back_kernel, tile, scale, len(keys_values)),
        out_shape=[jax.ShapeDtypeStruct((rows // HEADS, HD), BF16)] * HEADS
        + [jax.ShapeDtypeStruct((kv_rows // 2, 2 * HD), BF16)] * 2,
        in_specs=[SMEM] * 3 + [VMEM] * (4 + len(operands)),
        out_specs=[VMEM] * (HEADS + 2),
        scratch_shapes=[
            pltpu.VMEM((rows, HD), BF16),
            pltpu.VMEM((kv_rows, 2 * HD), BF16),
            pltpu.VMEM((kv_rows, 2 * HD), F32),
        ],
        compiler_params=params(56),
        cost_estimate=cost(10 * rows * 1280 * HD, 8 * 2**20),
        name="attend_back",
    )(*tables, lse, cosine, sine, *operands)


def settle_kernel(near_ref, got_ref, cos_ref, sin_ref, *outs):
    total = near_ref[...].astype(F32) + got_ref[...].astype(F32)
    for k, out in enumerate(outs):

        @pl.when(pl.program_id(0) == k)
        def _(out=out):
            out[:, :HD] = rotate(total[:, :HD], cos_ref[...], -sin_ref[...]).astype(BF16)
            out[:, HD:] = total[:, HD:].astype(BF16)


def settle(near, got, cosine, sine):
    rows = near.shape[0]
    tile = rows // HEADS
    spec = pl.BlockSpec((tile, 2 * HD), lambda k: (k, 0))
    table = pl.BlockSpec((tile, HD), lambda k: (k, 0))
    return pl.pallas_call(
        settle_kernel,
        grid=(HEADS,),
        out_shape=[jax.ShapeDtypeStruct((tile, 2 * HD), BF16)] * HEADS,
        in_specs=[spec, spec, table, table],
        out_specs=[whole((tile, 2 * HD))] * HEADS,
        compiler_params=params(24),
        cost_estimate=cost(4 * 10**15, 0),
        name="settle",
    )(near, got, cosine, sine)


def out_project_kernel(idx, w_ref, *refs):
    pieces, (flat_ref, keep_ref, give_ref) = refs[:HEADS], refs[HEADS:]
    for k, piece in enumerate(pieces):
        flat_ref[:, pl.ds(pl.multiple_of((idx[0] ^ k) * HD, HD), HD)] = piece[...]
    half = keep_ref.shape[0]
    core = idx[2]
    mine = flat_ref[pl.ds(pl.multiple_of(core * half, half), half), :]
    other = flat_ref[pl.ds(pl.multiple_of((1 - core) * half, half), half), :]
    give_ref[...] = nn(other, w_ref[...]).astype(BF16)
    keep_ref[...] = nn(mine, w_ref[...]).astype(BF16)


def out_project(idx, w_out, pieces):
    cols, dim = w_out.shape
    tok = pieces[0].shape[0]
    half = jax.ShapeDtypeStruct((tok // 2, dim), BF16)
    return pl.pallas_call(
        out_project_kernel,
        out_shape=[jax.ShapeDtypeStruct((tok, cols), BF16), half, half],
        in_specs=[SMEM] + [VMEM] * (1 + HEADS),
        out_specs=[VMEM] * 3,
        compiler_params=params(40),
        cost_estimate=cost(2 * tok * dim * cols, 6 * 2**20),
        name="out_project",
    )(idx, w_out, *pieces)


def out_back_kernel(idx, w_ref, mine_ref, other_ref, *outs):
    half = mine_ref.shape[0]
    core = idx[2]
    for k, out in enumerate(outs):
        weights = w_ref[pl.ds(pl.multiple_of((idx[0] ^ k) * HD, HD), HD), :]
        out[pl.ds(pl.multiple_of(core * half, half), half), :] = nt(mine_ref[...], weights).astype(BF16)
        out[pl.ds(pl.multiple_of((1 - core) * half, half), half), :] = nt(
            other_ref[...], weights
        ).astype(BF16)


def out_back(idx, w_out, mine, other):
    half, dim = mine.shape
    return pl.pallas_call(
        out_back_kernel,
        out_shape=[jax.ShapeDtypeStruct((2 * half, HD), BF16)] * HEADS,
        in_specs=[SMEM] + [VMEM] * 3,
        out_specs=[VMEM] * HEADS,
        compiler_params=params(40),
        cost_estimate=cost(4 * half * dim * HEADS * HD, 5 * 2**20),
        name="out_back",
    )(idx, w_out, mine, other)


def norm_kernel(x_ref, chip_ref, far_ref, gain_ref, bias_ref, bucket_ref, sum_ref, out_ref):
    dim = x_ref.shape[1]
    total = x_ref[...].astype(F32) + (chip_ref[...].astype(F32) + far_ref[...].astype(F32))
    sum_ref[...] = total
    normed, _ = normalise(total)
    out_ref[:, :dim] = (normed * gain_ref[...] + bias_ref[...]).astype(BF16)
    out_ref[:, dim:] = jnp.broadcast_to(bucket_ref[...], (total.shape[0], HD)).astype(BF16)


def norm(x, chip, far, gain, bias, buckets):
    rows, dim = x.shape
    tile = rows // 4
    spec = pl.BlockSpec((tile, dim), lambda i: (i, 0))
    wide = pl.BlockSpec((tile, dim + HD), lambda i: (i, 0))
    return pl.pallas_call(
        norm_kernel,
        grid=(4,),
        out_shape=[
            jax.ShapeDtypeStruct((rows, dim), F32),
            jax.ShapeDtypeStruct((rows, dim + HD), BF16),
        ],
        in_specs=[spec, spec, spec, whole((1, dim)), whole((1, dim))]
        + [pl.BlockSpec((tile, 1), lambda i: (i, 0))],
        out_specs=[spec, wide],
        compiler_params=params(24),
        cost_estimate=cost(16 * rows * dim, 12 * rows * dim),
        name="norm",
    )(x, chip, far, gain, bias, buckets)


def norm_back_kernel(chip_ref, far_ref, x_ref, base_ref, gain_ref, wide_ref, low_ref, dg_ref, db_ref):
    grad = chip_ref[...].astype(F32) + far_ref[...].astype(F32)
    normed, inverse = normalise(x_ref[...].astype(F32))
    scaled = grad * gain_ref[...]
    back = inverse * (
        scaled
        - jnp.mean(scaled, axis=-1, keepdims=True)
        - normed * jnp.mean(scaled * normed, axis=-1, keepdims=True)
    )
    total = base_ref[...].astype(F32) + back
    wide_ref[...] = total
    low_ref[...] = total.astype(BF16)

    @pl.when(pl.program_id(0) == 0)
    def _():
        dg_ref[...] = jnp.zeros_like(dg_ref)
        db_ref[...] = jnp.zeros_like(db_ref)

    dg_ref[...] += jnp.sum(grad * normed, axis=0, keepdims=True)
    db_ref[...] += jnp.sum(grad, axis=0, keepdims=True)


def norm_back(chip, far, x, base, gain):
    rows, dim = chip.shape
    tile = rows // 4
    spec = pl.BlockSpec((tile, dim), lambda i: (i, 0))
    row = whole((1, dim))
    return pl.pallas_call(
        norm_back_kernel,
        grid=(4,),
        out_shape=[
            jax.ShapeDtypeStruct((rows, dim), F32),
            jax.ShapeDtypeStruct((rows, dim), BF16),
            jax.ShapeDtypeStruct((1, dim), F32),
            jax.ShapeDtypeStruct((1, dim), F32),
        ],
        in_specs=[spec] * 4 + [row],
        out_specs=[spec, spec, row, row],
        compiler_params=params(24),
        cost_estimate=cost(30 * rows * dim, 18 * rows * dim),
        name="norm_back",
    )(chip, far, x, base, gain)


def feed_kernel(idx, mine_ref, other_ref, w_ref, gact_ref, act_ref, du_ref, *refs):
    half = mine_ref.shape[0]
    weights = w_ref[...]
    dim = weights.shape[0]
    for at, ref in ((0, mine_ref), (half, other_ref)):
        rows = slice(at, at + half)
        kept = ref[:, dim : dim + 1].astype(F32) >= idx[5].astype(F32)
        relu = jnp.where(kept, jnp.maximum(nn(ref[:, :dim], weights), 0.0), 0.0)
        act_ref[rows, :] = (relu * relu).astype(BF16)
        du_ref[rows, :] = (gact_ref[rows, :].astype(F32) * 2.0 * relu).astype(BF16)
    if refs:
        keep_out, give_out, acc_ref = refs
        step = pl.program_id(0)

        @pl.when(step == 0)
        def _():
            acc_ref[...] = nt(du_ref[...], weights)

        @pl.when(step > 0)
        def _():
            acc_ref[...] += nt(du_ref[...], weights)

        @pl.when(step == pl.num_programs(0) - 1)
        def _():
            keep_out[...] = acc_ref[:half, :].astype(BF16)
            give_out[...] = acc_ref[half:, :].astype(BF16)


def feed_forward(idx, mine, other, w_up, gact, with_back):
    half, wide = mine.shape
    dim, hidden = w_up.shape
    tile = min(hidden, 512)
    tall = jax.ShapeDtypeStruct((2 * half, hidden), BF16)
    part = jax.ShapeDtypeStruct((half, dim), BF16)
    spec = pl.BlockSpec((2 * half, tile), lambda i, idx: (0, i))
    return pl.pallas_call(
        feed_kernel,
        grid_spec=pltpu.PrefetchScalarGridSpec(
            num_scalar_prefetch=1,
            grid=(hidden // tile,),
            in_specs=[
                whole((half, wide)),
                whole((half, wide)),
                pl.BlockSpec((dim, tile), lambda i, idx: (0, i)),
                spec,
            ],
            out_specs=[spec, spec] + ([whole((half, dim))] * 2 if with_back else []),
            scratch_shapes=[pltpu.VMEM((2 * half, dim), F32)] if with_back else [],
        ),
        out_shape=[tall, tall] + ([part, part] if with_back else []),
        compiler_params=params(48),
        cost_estimate=cost((8 if with_back else 4) * half * dim * hidden, 16 * 2**20),
        name="feed_own" if with_back else "feed_far",
    )(idx, mine, other, w_up, gact)


def feed_down_kernel(act_ref, w_ref, *refs):
    outs, acc_ref = refs[:4], refs[4]
    step = pl.program_id(0)

    @pl.when(step == 0)
    def _():
        acc_ref[...] = nn(act_ref[...], w_ref[...])

    @pl.when(step > 0)
    def _():
        acc_ref[...] += nn(act_ref[...], w_ref[...])

    @pl.when(step == pl.num_programs(0) - 1)
    def _():
        rows = outs[0].shape[0]
        for k, out in enumerate(outs):
            out[...] = acc_ref[k * rows : (k + 1) * rows, :].astype(BF16)


def feed_down(act, w_down):
    tok, hidden = act.shape
    dim = w_down.shape[1]
    tile = min(hidden, 1024)
    part = (tok // 4, dim)
    return pl.pallas_call(
        feed_down_kernel,
        grid=(hidden // tile,),
        out_shape=[jax.ShapeDtypeStruct(part, BF16)] * 4,
        in_specs=[
            pl.BlockSpec((tok, tile), lambda i: (0, i)),
            pl.BlockSpec((tile, dim), lambda i: (i, 0)),
        ],
        out_specs=[whole(part)] * 4,
        scratch_shapes=[pltpu.VMEM((tok, dim), F32)],
        compiler_params=params(40),
        cost_estimate=cost(2 * tok * dim * hidden, 12 * 2**20),
        name="feed_down",
    )(act, w_down)


def back_act_kernel(mine_ref, other_ref, w_ref, out_ref):
    half = mine_ref.shape[0]
    out_ref[:half, :] = nt(mine_ref[...], w_ref[...]).astype(BF16)
    out_ref[half:, :] = nt(other_ref[...], w_ref[...]).astype(BF16)


def back_act(mine, other, w_down):
    half, dim = mine.shape
    hidden = w_down.shape[0]
    tile = min(hidden, 512)
    return pl.pallas_call(
        back_act_kernel,
        grid=(hidden // tile,),
        out_shape=jax.ShapeDtypeStruct((2 * half, hidden), BF16),
        in_specs=[
            whole((half, dim)),
            whole((half, dim)),
            pl.BlockSpec((tile, dim), lambda i: (i, 0)),
        ],
        out_specs=pl.BlockSpec((2 * half, tile), lambda i: (0, i)),
        compiler_params=params(40),
        cost_estimate=cost(4 * half * dim * hidden, 12 * 2**20),
        name="back_act",
    )(mine, other, w_down)


def product_kernel(idx, *refs):
    cols, near_ref, far_ref, out_ref, turn_ref = refs[:4], refs[4], refs[5], refs[6], refs[7]
    half = cols[0].shape[0]
    for k, ref in enumerate(cols):
        turn_ref[:, k * half : (k + 1) * half] = ref[...].astype(F32).T.astype(BF16)
    width = out_ref.shape[1]
    tile = min(width, 512)
    starts = [pl.multiple_of(idx[3 + j] * half, half) for j in range(2)]
    for at in range(0, width, tile):
        lanes = slice(at, at + tile)
        total = None
        for k in range(4):
            rows = (near_ref, far_ref)[k // 2][pl.ds(starts[k % 2], half), lanes]
            term = nn(turn_ref[:, k * half : (k + 1) * half], rows)
            total = term if total is None else total + term
        out_ref[:, lanes] = total.astype(BF16)


def product(idx, cols, near, far, dim):
    half = cols[0].shape[0]
    tok, width = near.shape
    block = dim // (2 * HEADS)
    spec = pl.BlockSpec((half, block), lambda k, idx: (0, 2 * k + idx[1]))
    return pl.pallas_call(
        product_kernel,
        grid_spec=pltpu.PrefetchScalarGridSpec(
            num_scalar_prefetch=1,
            grid=(HEADS,),
            in_specs=[spec] * 4 + [whole((tok, width))] * 2,
            out_specs=pl.BlockSpec((block, width), lambda k, idx: (k, 0)),
            scratch_shapes=[pltpu.VMEM((block, 4 * half), BF16)],
        ),
        out_shape=jax.ShapeDtypeStruct((HEADS * block, width), BF16),
        compiler_params=params(40),
        cost_estimate=cost(2 * tok * width * dim, 12 * 2**20),
        name="product",
    )(idx, *cols, near, far)


def head_product_kernel(idx, h_ref, *refs):
    dq_refs, dkv_refs = refs[:HEADS], refs[HEADS : 2 * HEADS]
    give_ref, keep_ref, turn_ref = refs[2 * HEADS :]
    tok = dq_refs[0].shape[0]
    first = (pl.program_id(0) == 0) & (pl.program_id(1) == 0)

    @pl.when(first)
    def _():
        for k, ref in enumerate(dq_refs):
            turn_ref[:HD, k * tok : (k + 1) * tok] = ref[...].astype(F32).T.astype(BF16)
            turn_ref[HD:, k * tok : (k + 1) * tok] = dkv_refs[k][...].astype(F32).T.astype(BF16)

    total = None
    for k in range(HEADS):
        rows = h_ref[pl.ds(pl.multiple_of((idx[0] ^ k) * tok, tok), tok), :]
        term = nn(turn_ref[:, k * tok : (k + 1) * tok], rows)
        total = term if total is None else total + term

    @pl.when(pl.program_id(0) == 0)
    def _():
        give_ref[0] = total.astype(BF16)

    @pl.when(pl.program_id(0) == 1)
    def _():
        keep_ref[0] = total.astype(BF16)


def head_product(idx, h_all, dq_pieces, dkv_pieces):
    rows, dim = h_all.shape
    block = dim // (2 * HEADS)
    out = jax.ShapeDtypeStruct((HEADS, 3 * HD, block), BF16)

    def columns(turn, k, idx):
        return (0, (idx[0] ^ k) * 2 + jnp.where(turn == 0, 1 - idx[1], idx[1]))

    return pl.pallas_call(
        head_product_kernel,
        grid_spec=pltpu.PrefetchScalarGridSpec(
            num_scalar_prefetch=1,
            grid=(2, HEADS),
            in_specs=[pl.BlockSpec((rows, block), columns)]
            + [whole((rows // HEADS, HD))] * HEADS
            + [whole((rows // HEADS, 2 * HD))] * HEADS,
            out_specs=[
                pl.BlockSpec(
                    (1, 3 * HD, block),
                    lambda turn, k, idx: (jnp.where(turn == 0, k, HEADS - 1), 0, 0),
                ),
                pl.BlockSpec(
                    (1, 3 * HD, block), lambda turn, k, idx: (jnp.where(turn == 0, 0, k), 0, 0)
                ),
            ],
            scratch_shapes=[pltpu.VMEM((3 * HD, rows), BF16)],
        ),
        out_shape=[out, out],
        compiler_params=params(40),
        cost_estimate=cost(2 * rows * dim * 3 * HD, 12 * 2**20),
        name="head_product",
    )(idx, h_all, *dq_pieces, *dkv_pieces)


def head_add_kernel(keep_ref, got_ref, after_ref, *outs):
    del after_ref
    for k, out in enumerate(outs):
        out[...] = (keep_ref[k].astype(F32) + got_ref[k].astype(F32)).astype(BF16)


def head_add(keep, got, after):
    return pl.pallas_call(
        head_add_kernel,
        out_shape=[jax.ShapeDtypeStruct(keep.shape[1:], BF16)] * HEADS,
        in_specs=[VMEM, VMEM, ANY],
        out_specs=[VMEM] * HEADS,
        compiler_params=params(24),
        cost_estimate=cost(keep.size, 6 * keep.size),
        name="head_add",
    )(keep, got, after)


def head_place_kernel(idx, *refs):
    pieces, out_ref = refs[:HEADS], refs[HEADS]
    for k, piece in enumerate(pieces):
        for s in range(3):
            out_ref[s, :, pl.ds(pl.multiple_of((idx[0] ^ k) * HD, HD), HD)] = (
                piece[s * HD : (s + 1) * HD, :].astype(F32).T
            )


def head_place(idx, pieces):
    rows, block = pieces[0].shape
    return pl.pallas_call(
        head_place_kernel,
        out_shape=jax.ShapeDtypeStruct((3, block, HEADS * HD), F32),
        in_specs=[SMEM] + [VMEM] * HEADS,
        out_specs=VMEM,
        compiler_params=params(24),
        cost_estimate=cost(rows * block * 8, 4 * 2**20),
        name="head_place",
    )(idx, *pieces)


def project_back_kernel(idx, w_ref, *refs):
    dq_refs, dkv_refs = refs[:HEADS], refs[HEADS : 2 * HEADS]
    keep_ref, give_a_ref, give_b_ref, flat_ref, acc_ref = refs[2 * HEADS :]
    half = keep_ref.shape[0]
    core = idx[2]
    step = pl.program_id(0)

    for s in range(3):

        @pl.when(step == s)
        def _(s=s):
            for k in range(HEADS):
                lanes = pl.ds(pl.multiple_of((idx[0] ^ k) * HD, HD), HD)
                if s == 0:
                    flat_ref[:, lanes] = dq_refs[k][...]
                else:
                    flat_ref[:, lanes] = dkv_refs[k][:, (s - 1) * HD : s * HD]

    @pl.when(step == 0)
    def _():
        acc_ref[...] = nt(flat_ref[...], w_ref[0])

    @pl.when(step > 0)
    def _():
        acc_ref[...] += nt(flat_ref[...], w_ref[0])

    @pl.when(step == 2)
    def _():
        part = half // 2
        for k, out in enumerate((give_a_ref, give_b_ref)):
            start = pl.multiple_of((1 - core) * half + k * part, part)
            out[...] = acc_ref[pl.ds(start, part), :].astype(BF16)
        keep_ref[...] = acc_ref[pl.ds(pl.multiple_of(core * half, half), half), :].astype(BF16)


def project_back(idx, w_qkv, dq_pieces, dkv_pieces):
    tok = dq_pieces[0].shape[0]
    _, dim, cols = w_qkv.shape
    return pl.pallas_call(
        project_back_kernel,
        grid_spec=pltpu.PrefetchScalarGridSpec(
            num_scalar_prefetch=1,
            grid=(3,),
            in_specs=[pl.BlockSpec((1, dim, cols), lambda s, idx: (s, 0, 0))]
            + [whole((tok, HD))] * HEADS
            + [whole((tok, 2 * HD))] * HEADS,
            out_specs=[whole((tok // 2, dim))] + [whole((tok // 4, dim))] * 2,
            scratch_shapes=[pltpu.VMEM((tok, cols), BF16), pltpu.VMEM((tok, dim), F32)],
        ),
        out_shape=[jax.ShapeDtypeStruct((tok // 2, dim), BF16)]
        + [jax.ShapeDtypeStruct((tok // 4, dim), BF16)] * 2,
        compiler_params=params(40),
        cost_estimate=cost(6 * tok * dim * cols, 12 * 2**20),
        name="project_back",
    )(idx, w_qkv, *dq_pieces, *dkv_pieces)


def join_kernel(idx, mine_ref, other_ref, out_ref):
    half = mine_ref.shape[0]
    core = idx[2]
    out_ref[pl.ds(pl.multiple_of(core * half, half), half), :] = mine_ref[...].astype(out_ref.dtype)
    out_ref[pl.ds(pl.multiple_of((1 - core) * half, half), half), :] = other_ref[...].astype(
        out_ref.dtype
    )


def join(idx, mine, other, dtype):
    half, dim = mine.shape
    return pl.pallas_call(
        join_kernel,
        out_shape=jax.ShapeDtypeStruct((2 * half, dim), dtype),
        in_specs=[SMEM, VMEM, VMEM],
        out_specs=VMEM,
        compiler_params=params(24),
        cost_estimate=cost(half * dim, 8 * half * dim),
        name="join",
    )(idx, mine, other)


def body(
    depth,
    layer_input,
    ln1_gain,
    ln1_bias,
    w_qkv,
    w_out,
    ln2_gain,
    ln2_bias,
    w_up,
    w_down,
    buckets,
    lengths,
    block_order,
    grad_out,
):
    tok, dim = layer_input.shape
    half = tok // 2
    scale = 1.0 / math.sqrt(HD)
    r, h, y, x, c = (lax.axis_index(a) for a in ("r", PLANE, "y") + TP)
    blk = lax.axis_index(BLK)
    tp = lax.axis_index(TP)
    idx = jnp.stack([h, y, c, jnp.zeros_like(c), jnp.ones_like(c), tp]).astype(jnp.int32)
    idx_rows = jnp.stack([h, y, c, c, 1 - c]).astype(jnp.int32)
    gains = [v.reshape(1, dim) for v in (ln1_gain, ln1_bias, ln2_gain, ln2_bias)]

    def half_of(values, which):
        return lax.dynamic_slice_in_dim(values, which * half, half, 0)

    def regroup(values):
        if depth == 1:
            return values
        rows = values.shape[0]
        split = values[:, :dim].reshape(rows, depth, HEADS, 2, dim // (2 * HEADS * depth))
        return split.transpose(0, 2, 3, 1, 4).reshape(rows, dim)

    def scatter(values):
        if depth > 1:
            split = values.reshape(HEADS, depth, -1, values.shape[1])
            values = split.transpose(1, 0, 2, 3).reshape(values.shape)
        return lax.psum_scatter(values, ("r",) + PLANE, scatter_dimension=0, tiled=True)

    starts = jnp.cumsum(lengths) - lengths

    def firsts_of(places):
        return jnp.max(jnp.where(starts <= places[..., None], starts, 0), axis=-1)

    inside = jnp.arange(half, dtype=jnp.int32)
    own_places = (
        lax.dynamic_slice_in_dim(block_order, 2 * blk, 2, 0)[:, None] * half + inside
    ).reshape(tok)
    cosine, sine = rotary_tables(own_places - firsts_of(own_places))

    def chip_sum(keep, give):
        return (keep.astype(F32) + swap(give, "c").astype(F32)).astype(BF16)

    grad_mine, grad_other = half_of(grad_out, c), half_of(grad_out, 1 - c)
    h_one, *projected = project(idx, layer_input, gains[0], gains[1], cosine, sine, w_qkv)
    queries, near_kv = list(projected[:HEADS]), list(projected[HEADS:])
    near_kv = [near_kv[0]] + [plane_swap(near_kv[k], k) for k in range(1, HEADS)]
    *queries[1:], near_kv[2] = ordered(*queries[1:], near_kv[2])
    queries = [queries[0]] + [plane_swap(queries[k], k) for k in range(1, HEADS)]
    y_grad = swap(grad_mine, "y")

    relative = h ^ jnp.arange(HEADS, dtype=jnp.int32)
    group_order = lax.dynamic_index_in_dim(
        block_order.reshape(depth, HEADS, 2, 2), r, 0, keepdims=False
    )
    group_order = lax.dynamic_index_in_dim(group_order, y, 1, keepdims=False)
    chosen = relative[:, None] == jnp.arange(HEADS, dtype=jnp.int32)[None, :]
    query_at = jnp.sum(jnp.where(chosen[:, :, None], group_order[None], 0), axis=1).reshape(-1)
    query_places = query_at[:, None] * half + inside
    query_firsts = firsts_of(query_places)
    query_low = query_firsts[:, 0] // half
    block_count = block_order.shape[0]
    slots = jnp.argmax(
        block_order[None, :] == jnp.arange(block_count, dtype=jnp.int32)[:, None], axis=1
    ).astype(jnp.int32)
    slot_dev = slots // 2
    slot_plane = slot_dev // 2
    key_row = (
        jnp.where(slot_dev % 2 == y, 0, block_count // 2)
        + slot_plane // HEADS * (2 * HEADS)
        + ((slot_plane % HEADS) ^ h) * 2
        + slots % 2
    )
    group_cos, group_sin = rotary_tables((query_places - query_firsts).reshape(2 * HEADS * half))
    tables = (query_at, query_low, key_row, query_firsts.reshape(2 * HEADS, 1, half))

    grad_act = back_act(grad_mine, grad_other, w_down)
    far_first = swap(near_kv[0], "y")
    far_first, y_grad, grad_act, group_cos, group_sin, *near_kv[1:] = ordered(
        far_first, y_grad, grad_act, group_cos, group_sin, *near_kv[1:]
    )
    if depth == 1:
        keys_values = near_kv + [far_first, swap(jnp.concatenate(near_kv[1:]), "y")]
    else:
        near_all = lax.all_gather(jnp.concatenate(near_kv), "r", axis=0, tiled=True)
        keys_values = [near_all, swap(near_all, "y")]
    y_grad_other = swap(y_grad, "c")
    y_grad_other, *queries[1:], keys_values[-1] = ordered(
        y_grad_other, *queries[1:], keys_values[-1]
    )

    *attended, lse = attend(half, scale, tables, queries, keys_values)
    pieces = [attended[0]] + [plane_swap(attended[k], k) for k in range(1, HEADS)]
    y_grad, lse = ordered(y_grad, lse)
    y_grad_act = back_act(y_grad, y_grad_other, w_down)
    y_grad_act, *pieces[1:] = ordered(y_grad_act, *pieces[1:])
    flat, keep, give = out_project(idx, w_out, pieces)
    chip = chip_sum(keep, give)
    chip_far = swap(chip, "x")
    quarter = lax.dynamic_slice_in_dim(h_one, tp * (tok // 4), tok // 4, 0)
    quarter, flat = ordered(quarter, flat)
    h_all = lax.all_gather(quarter, PLANE + TP, axis=0, tiled=True)
    y_flat = swap(flat, "y")
    y_flat, chip_far = ordered(y_flat, chip_far)

    my_buckets = half_of(buckets, c).reshape(half, 1)
    x_mid, h_mine = norm(
        half_of(layer_input, c), chip, chip_far, gains[2], gains[3], my_buckets
    )
    h_other = swap(h_mine, "c")
    y_h = swap(h_mine, "y")
    act, du, keep, give = feed_forward(idx, h_mine, h_other, w_up, grad_act, True)
    chip = chip_sum(keep, give)
    chip_far = swap(chip, "x")

    y_h_other = swap(y_h, "c")
    y_act, y_du = feed_forward(idx, y_h, y_h_other, w_up, y_grad_act, False)
    pair_grads = [regroup(v) for v in (grad_mine, grad_other, y_grad, y_grad_other)]
    down_sum = product(idx, pair_grads, act, y_act, dim)
    down_sum, h_all, chip_far = ordered(down_sum, h_all, chip_far)
    down_part = scatter(down_sum)

    grad_mid, dy_mine, gain_two_grad, bias_two_grad = norm_back(
        chip, chip_far, x_mid, grad_mine, gains[2]
    )
    dy_other = swap(dy_mine, "c")
    grads = list(out_back(idx, w_out, dy_mine, dy_other))
    for_pair, for_product, grads[0] = ordered(dy_mine, h_mine, grads[0])
    grads = [grads[0]] + [plane_swap(grads[k], k) for k in range(1, HEADS)]
    y_dy = swap(for_pair, "y")

    pair_rows = [regroup(v) for v in (for_product, h_other, y_h, y_h_other)]
    up_sum = product(idx, pair_rows, du, y_du, dim)
    up_sum, y_dy, *grads[1:] = ordered(up_sum, y_dy, *grads[1:])

    *dq, near, far = attend_back(
        half, scale, tables, lse, group_cos, group_sin, queries, keys_values, attended, grads
    )
    got = swap(far, "y")
    dq_pieces = [dq[0]] + [plane_swap(dq[k], k) for k in range(1, HEADS)]

    feed_act, near = ordered(act, near)
    feed = list(feed_down(feed_act, w_down))
    y_dy_other = swap(y_dy, "c")
    wout_cols = [regroup(v) for v in (dy_mine, dy_other, y_dy, y_dy_other)]
    wout_cols[0], near = ordered(wout_cols[0], near)
    wout_sum = product(idx_rows, wout_cols, flat, y_flat, dim)
    wout_sum, feed[1], down_part, got, *dq_pieces[1:] = ordered(
        wout_sum, feed[1], down_part, got, *dq_pieces[1:]
    )
    up_part = scatter(up_sum)

    if depth > 1:
        near = lax.psum_scatter(near, "r", scatter_dimension=0, tiled=True)
        got = lax.psum_scatter(got, "r", scatter_dimension=0, tiled=True)
    dkv = list(settle(near, got, group_cos, group_sin))
    dkv_pieces = [dkv[0]] + [plane_swap(dkv[k], k) for k in range(1, HEADS)]
    feed_chip = [chip_sum(feed[k], feed[k + 2]) for k in range(2)]
    feed_far = [swap(v, "x") for v in feed_chip]

    head_give, head_keep = head_product(idx, regroup(h_all), dq, dkv)
    head_give, *feed_far, dkv_pieces[1], dkv_pieces[2], dkv_pieces[3] = ordered(
        head_give, *feed_far, *dkv_pieces[1:]
    )
    keep, *gives = project_back(idx, w_qkv, dq_pieces, dkv_pieces)
    chip = jnp.concatenate([swap(v, "c") for v in gives])
    chip = (keep.astype(F32) + chip.astype(F32)).astype(BF16)
    chip_far = swap(chip, "x")

    head_got = swap(head_give, "y")
    feed_chip, feed_far = jnp.concatenate(feed_chip), jnp.concatenate(feed_far)
    out_mine = (x_mid + (feed_chip.astype(F32) + feed_far.astype(F32))).astype(BF16)
    out_mine, chip = ordered(out_mine, chip)
    out_other = swap(out_mine, "c")
    layer_output = join(idx, out_mine, out_other, BF16)
    layer_output, head_got, chip_far = ordered(layer_output, head_got, chip_far)
    wout_part = scatter(wout_sum)

    _, grad_low, gain_one_grad, bias_one_grad = norm_back(
        chip, chip_far, half_of(layer_input, c), grad_mid, gains[0]
    )
    head_sum = list(head_add(head_keep, head_got, grad_low))
    if depth > 1:
        head_sum = [lax.psum_scatter(v, "r", scatter_dimension=1, tiled=True) for v in head_sum]
    head_pieces = [head_sum[0]] + [plane_swap(head_sum[k], k) for k in range(1, HEADS)]
    grad_input = join(idx, grad_low, swap(grad_low, "c"), F32)

    counts = jnp.sum(
        (half_of(buckets, c)[:, None] == jnp.arange(NB, dtype=jnp.int32)[None, :]).astype(F32),
        axis=0,
    )
    sums = jnp.concatenate(
        [v.reshape(dim) for v in (gain_one_grad, bias_one_grad, gain_two_grad, bias_two_grad)]
        + [counts]
    )
    if depth > 1:
        sums = lax.psum(sums, "r")
    sums = sums + swap(sums, "c")
    sums, up_part = ordered(sums, up_part)
    sums = sums + swap(sums, "y")
    sums, *head_pieces[1:] = ordered(sums, *head_pieces[1:])
    qkv_part = head_place(idx, head_pieces)
    one, two, three = (plane_swap(sums, k) for k in range(1, HEADS))
    sums = (sums + one) + (two + three)
    return (
        layer_output,
        grad_input,
        sums[:dim],
        sums[dim : 2 * dim],
        qkv_part,
        wout_part.astype(F32).T,
        sums[2 * dim : 3 * dim],
        sums[3 * dim : 4 * dim],
        up_part.astype(F32),
        down_part.astype(F32).T,
        sums[4 * dim :].astype(jnp.int32),
    )


def solution(mesh):
    depth = mesh.shape["blk"] // (2 * HEADS)
    fine = Mesh(mesh.devices.reshape(depth, 2, 2, 2, 2, 2), BLK + TP)
    return jax.shard_map(
        functools.partial(body, depth),
        mesh=fine,
        in_specs=(
            P(BLK, None),
            P(),
            P(),
            P(None, None, TP),
            P(TP, None),
            P(),
            P(),
            P(None, TP),
            P(TP, None),
            P(BLK),
            P(),
            P(),
            P(BLK, None),
        ),
        out_specs=(
            P(BLK, None),
            P(BLK, None),
            P(),
            P(),
            P(None, BLK, TP),
            P(TP, BLK),
            P(),
            P(),
            P(BLK, TP),
            P(TP, BLK),
            P(),
        ),
        check_vma=False,
    )
```

```python
import functools
import math

import jax
import jax.numpy as jnp
from jax import lax
from jax.experimental import pallas as pl
from jax.experimental.pallas import tpu as pltpu
from jax.sharding import Mesh
from jax.sharding import PartitionSpec as P

HD = 128
FF = 8192
NB = 4
HEADS = 4
EPSILON = 1e-05
ROPE_BASE = 10000.0
PLANE = ("hh", "hl")
LOG_E = math.log2(math.e)
HIDDEN = -1e30
BLK = ("r", "hh", "hl", "y")
TP = ("x", "c")
F32 = jnp.float32
BF16 = jnp.bfloat16
SMEM = pl.BlockSpec(memory_space=pltpu.SMEM)
VMEM = pl.BlockSpec(memory_space=pltpu.VMEM)
ANY = pl.BlockSpec(memory_space=pl.ANY)


def swap(value, axis):
    return lax.ppermute(value, axis, [(0, 1), (1, 0)])


def plane_swap(value, k):
    return lax.ppermute(value, PLANE, [(i, i ^ k) for i in range(HEADS)])


def ordered(*values):
    return lax.optimization_barrier(values)


def nt(lhs, rhs):
    return lax.dot_general(lhs, rhs, (((1,), (1,)), ((), ())), preferred_element_type=F32)


def tn(lhs, rhs):
    return lax.dot_general(lhs, rhs, (((0,), (0,)), ((), ())), preferred_element_type=F32)


def nn(lhs, rhs):
    return lax.dot_general(lhs, rhs, (((1,), (0,)), ((), ())), preferred_element_type=F32)


def params(mib):
    return pltpu.CompilerParams(vmem_limit_bytes=60 * 2**20)


def cost(on_path):
    return pl.CostEstimate(flops=10**9 if on_path else 1, bytes_accessed=1, transcendentals=0)


def whole(shape):
    return pl.BlockSpec(shape, lambda *_: (0,) * len(shape))


def normalise(values):
    centre = values - jnp.mean(values, axis=-1, keepdims=True)
    inverse = lax.rsqrt(jnp.mean(centre * centre, axis=-1, keepdims=True) + EPSILON)
    return (centre * inverse, inverse)


def rotary_tables(positions):
    freqs = ROPE_BASE ** (-(jnp.arange(HD // 2, dtype=F32) * 2.0 / HD))
    angles = positions.astype(F32)[:, None] * freqs[None, :]
    cosine, sine = jnp.cos(angles), jnp.sin(angles)
    return (
        jnp.concatenate([cosine, cosine], axis=-1),
        jnp.concatenate([-sine, sine], axis=-1),
    )


def rotate(values, cosine, sine):
    return values * cosine + pltpu.roll(values, HD // 2, 1) * sine


def project_kernel(idx, x_ref, gain_ref, bias_ref, cos_ref, sin_ref, w_ref, *refs):
    part_ref, q_outs, kv_outs = refs[0], refs[1 : 1 + HEADS], refs[1 + HEADS : 1 + 2 * HEADS]
    h_ref = refs[1 + 2 * HEADS]
    step = pl.program_id(0)

    @pl.when(step == 0)
    def _():
        normed, _ = normalise(x_ref[...].astype(F32))
        h_ref[...] = (normed * gain_ref[...] + bias_ref[...]).astype(BF16)
        rows = part_ref.shape[0]
        part_ref[...] = h_ref[pl.ds(pl.multiple_of(idx[2] * rows, rows), rows), :]

    both = nn(h_ref[...], jnp.concatenate([w_ref[0], w_ref[1]], axis=1))
    cosine, sine = cos_ref[...], sin_ref[...]
    queries = rotate(both[:, :HD], cosine, sine).astype(BF16)
    keys = rotate(both[:, HD:], cosine, sine).astype(BF16)
    values = nn(h_ref[...], w_ref[2]).astype(BF16)
    for k in range(HEADS):

        @pl.when(step == k)
        def _(k=k):
            q_outs[k][...] = queries
            kv_outs[k][:, :HD] = keys
            kv_outs[k][:, HD:] = values


def project(idx, x, gain, bias, cosine, sine, w_qkv):
    tok, dim = x.shape
    return pl.pallas_call(
        project_kernel,
        grid_spec=pltpu.PrefetchScalarGridSpec(
            num_scalar_prefetch=1,
            grid=(HEADS,),
            in_specs=[
                whole((tok, dim)),
                whole((1, dim)),
                whole((1, dim)),
                whole((tok, HD)),
                whole((tok, HD)),
                pl.BlockSpec((3, dim, HD), lambda k, idx: (0, 0, idx[0] ^ k)),
            ],
            out_specs=[whole((tok // 2, dim))]
            + [whole((tok, HD))] * HEADS
            + [whole((tok, 2 * HD))] * HEADS,
            scratch_shapes=[pltpu.VMEM((tok, dim), BF16)],
        ),
        out_shape=[jax.ShapeDtypeStruct((tok // 2, dim), BF16)]
        + [jax.ShapeDtypeStruct((tok, HD), BF16)] * HEADS
        + [jax.ShapeDtypeStruct((tok, 2 * HD), BF16)] * HEADS,
        compiler_params=params(40),
        cost_estimate=cost(True),
        name="project",
    )(idx, x, gain, bias, cosine, sine, w_qkv)


def visible_of(tile, key_block, query_places, query_firsts):
    key_places = key_block * tile + lax.broadcasted_iota(jnp.int32, (tile, 1), 0)
    return (key_places <= query_places) & (key_places >= query_firsts)


def gather_refs(refs, whole_ref):
    at = 0
    for ref in refs:
        whole_ref[at : at + ref.shape[0], :] = ref[...]
        at += ref.shape[0]


def over_blocks(low, full, at, masked, open_pair, state):
    pairs = lax.div(at - full, 2)
    middle = full + 2 * pairs
    state = lax.fori_loop(low, full, masked, state)
    state = lax.fori_loop(0, pairs, lambda j, st: open_pair(full + 2 * j, st), state)
    return lax.fori_loop(middle, at + 1, masked, state)


def attend_kernel(tile, scale, n_kv, at_ref, low_ref, full_ref, row_ref, first_ref, *refs):
    q_refs, kv_refs, refs = refs[:HEADS], refs[HEADS : HEADS + n_kv], refs[HEADS + n_kv :]
    outs, (lse_ref, q_all, kv_all) = refs[:HEADS], refs[HEADS:]
    gather_refs(q_refs, q_all)
    gather_refs(kv_refs, kv_all)
    lanes = lax.broadcasted_iota(jnp.int32, (1, tile), 1)
    per_out = outs[0].shape[0] // tile
    scale_two = scale * LOG_E

    def one_block(i, carry):
        rows = pl.ds(pl.multiple_of(i * tile, tile), tile)
        queries = q_all[rows, :]
        firsts = first_ref[i]
        places = at_ref[i] * tile + lanes

        def key_rows(b):
            return pl.ds(pl.multiple_of(row_ref[b] * tile, tile), tile)

        def absorb(state, scores, values):
            run_max, run_sum, run_acc = state
            new_max = run_max
            for part in scores:
                new_max = jnp.maximum(new_max, jnp.max(part, axis=0, keepdims=True))
            factor = jnp.exp2(run_max - new_max)
            new_sum = run_sum * factor
            new_acc = run_acc * factor
            for part, rows in zip(scores, values, strict=True):
                probs = jnp.exp2(part - new_max)
                new_sum = new_sum + jnp.sum(probs, axis=0, keepdims=True)
                new_acc = new_acc + tn(rows, probs.astype(BF16))
            return (new_max, new_sum, new_acc)

        def masked(b, state):
            krows = key_rows(b)
            scores = nt(kv_all[krows, :HD], queries) * scale_two
            scores = jnp.where(visible_of(tile, b, places, firsts), scores, HIDDEN)
            return absorb(state, [scores], [kv_all[krows, HD:]])

        def open_pair(b, state):
            one, two = key_rows(b), key_rows(b + 1)
            scores = [nt(kv_all[k, :HD], queries) * scale_two for k in (one, two)]
            return absorb(state, scores, [kv_all[one, HD:], kv_all[two, HD:]])

        run_max, run_sum, run_acc = over_blocks(
            low_ref[i],
            full_ref[i],
            at_ref[i],
            masked,
            open_pair,
            (
                jnp.full((1, tile), HIDDEN / 10, F32),
                jnp.zeros((1, tile), F32),
                jnp.zeros((HD, tile), F32),
            ),
        )
        q_all[rows, :] = (run_acc / run_sum).T.astype(BF16)
        lse_ref[i] = run_max + jnp.log2(run_sum)
        return carry

    lax.fori_loop(0, HEADS * per_out, one_block, 0)
    for k, out in enumerate(outs):
        out[...] = q_all[k * per_out * tile : (k + 1) * per_out * tile, :]


def attend_back_kernel(
    tile,
    scale,
    n_kv,
    at_ref,
    low_ref,
    full_ref,
    row_ref,
    first_ref,
    lse_ref,
    cos_ref,
    sin_ref,
    *refs,
):
    q_refs, kv_refs, refs = refs[:HEADS], refs[HEADS : HEADS + n_kv], refs[HEADS + n_kv :]
    o_refs, do_refs, dq_refs = refs[:HEADS], refs[HEADS : 2 * HEADS], refs[2 * HEADS : 3 * HEADS]
    near_ref, far_ref, q_all, kv_all, do_all, dot_all, acc_ref = refs[3 * HEADS :]
    gather_refs(q_refs, q_all)
    gather_refs(kv_refs, kv_all)
    gather_refs(do_refs, do_all)
    acc_ref[...] = jnp.zeros_like(acc_ref)
    lanes = lax.broadcasted_iota(jnp.int32, (1, tile), 1)
    per_out = dq_refs[0].shape[0] // tile
    scale_two = scale * LOG_E
    for k in range(HEADS):
        for j in range(per_out):
            piece = slice(j * tile, (j + 1) * tile)
            products = do_refs[k][piece, :].astype(F32) * o_refs[k][piece, :].astype(F32)
            dot_all[k * per_out + j] = jnp.sum(products.T, axis=0, keepdims=True)

    def one_block(i, carry):
        rows = pl.ds(pl.multiple_of(i * tile, tile), tile)
        queries = q_all[rows, :]
        grads = do_all[rows, :]
        firsts = first_ref[i]
        places = at_ref[i] * tile + lanes
        log_sums = lse_ref[i]
        deltas = dot_all[i]

        def one(b, grad_q, hide):
            krows = pl.ds(pl.multiple_of(row_ref[b] * tile, tile), tile)
            keys = kv_all[krows, :HD]
            probs = jnp.exp2(nt(keys, queries) * scale_two - log_sums)
            if hide:
                probs = jnp.where(visible_of(tile, b, places, firsts), probs, 0.0)
            grad_probs = nt(kv_all[krows, HD:], grads)
            grad_scores = (probs * (grad_probs - deltas)).astype(BF16)
            acc_ref[krows, HD:] += nn(probs.astype(BF16), grads)
            acc_ref[krows, :HD] += nn(grad_scores, queries)
            return grad_q + tn(keys, grad_scores)

        def open_pair(b, grad_q):
            return one(b + 1, one(b, grad_q, False), False)

        grad_q = over_blocks(
            low_ref[i],
            full_ref[i],
            at_ref[i],
            lambda b, grad_q: one(b, grad_q, True),
            open_pair,
            jnp.zeros((HD, tile), F32),
        )
        do_all[rows, :] = rotate((grad_q * scale).T, cos_ref[rows, :], -sin_ref[rows, :]).astype(BF16)
        return carry

    lax.fori_loop(0, HEADS * per_out, one_block, 0)
    for k, out in enumerate(dq_refs):
        out[...] = do_all[k * per_out * tile : (k + 1) * per_out * tile, :]
    near = near_ref.shape[0]
    near_ref[:, :HD] = (acc_ref[:near, :HD] * scale).astype(BF16)
    near_ref[:, HD:] = acc_ref[:near, HD:].astype(BF16)
    far_ref[:, :HD] = (acc_ref[near:, :HD] * scale).astype(BF16)
    far_ref[:, HD:] = acc_ref[near:, HD:].astype(BF16)


def attend(tile, scale, tables, pieces, keys_values):
    rows = HEADS * pieces[0].shape[0]
    kv_rows = sum(a.shape[0] for a in keys_values)
    operands = pieces + keys_values
    return pl.pallas_call(
        functools.partial(attend_kernel, tile, scale, len(keys_values)),
        out_shape=[jax.ShapeDtypeStruct((rows // HEADS, HD), BF16)] * HEADS
        + [jax.ShapeDtypeStruct((rows // tile, 1, tile), F32)],
        in_specs=[SMEM] * 4 + [VMEM] * (1 + len(operands)),
        out_specs=[VMEM] * (HEADS + 1),
        scratch_shapes=[pltpu.VMEM((rows, HD), BF16), pltpu.VMEM((kv_rows, 2 * HD), BF16)],
        compiler_params=params(50),
        cost_estimate=cost(True),
        name="attend",
    )(*tables, *operands)


def attend_back(tile, scale, tables, lse, cosine, sine, pieces, keys_values, outs, grads):
    rows = HEADS * pieces[0].shape[0]
    kv_rows = sum(a.shape[0] for a in keys_values)
    operands = pieces + keys_values + outs + grads
    return pl.pallas_call(
        functools.partial(attend_back_kernel, tile, scale, len(keys_values)),
        out_shape=[jax.ShapeDtypeStruct((rows // HEADS, HD), BF16)] * HEADS
        + [jax.ShapeDtypeStruct((kv_rows // 2, 2 * HD), BF16)] * 2,
        in_specs=[SMEM] * 4 + [VMEM] * (4 + len(operands)),
        out_specs=[VMEM] * (HEADS + 2),
        scratch_shapes=[
            pltpu.VMEM((rows, HD), BF16),
            pltpu.VMEM((kv_rows, 2 * HD), BF16),
            pltpu.VMEM((rows, HD), BF16),
            pltpu.VMEM((rows // tile, 1, tile), F32),
            pltpu.VMEM((kv_rows, 2 * HD), F32),
        ],
        compiler_params=params(56),
        cost_estimate=cost(True),
        name="attend_back",
    )(*tables, lse, cosine, sine, *operands)


def settle_kernel(near_ref, got_ref, cos_ref, sin_ref, *refs):
    dq_refs, outs = refs[:HEADS], refs[HEADS:]
    total = near_ref[...].astype(F32) + got_ref[...].astype(F32)
    for k, out in enumerate(outs):

        @pl.when(pl.program_id(0) == k)
        def _(k=k, out=out):
            out[:, :HD] = dq_refs[k][...]
            out[:, HD : 2 * HD] = rotate(total[:, :HD], cos_ref[...], -sin_ref[...]).astype(BF16)
            out[:, 2 * HD :] = total[:, HD:].astype(BF16)


def settle(near, got, cosine, sine, dq_pieces):
    rows = near.shape[0]
    tile = rows // HEADS
    spec = pl.BlockSpec((tile, 2 * HD), lambda k: (k, 0))
    table = pl.BlockSpec((tile, HD), lambda k: (k, 0))
    return pl.pallas_call(
        settle_kernel,
        grid=(HEADS,),
        out_shape=[jax.ShapeDtypeStruct((tile, 3 * HD), BF16)] * HEADS,
        in_specs=[spec, spec, table, table] + [whole((tile, HD))] * HEADS,
        out_specs=[whole((tile, 3 * HD))] * HEADS,
        compiler_params=params(24),
        cost_estimate=cost(True),
        name="settle",
    )(near, got, cosine, sine, *dq_pieces)


def out_project_kernel(idx, w_ref, *refs):
    pieces, (flat_ref, keep_ref, give_ref) = refs[:HEADS], refs[HEADS:]
    for k, piece in enumerate(pieces):
        flat_ref[:, pl.ds(pl.multiple_of((idx[0] ^ k) * HD, HD), HD)] = piece[...]
    half = keep_ref.shape[0]
    core = idx[2]
    mine = flat_ref[pl.ds(pl.multiple_of(core * half, half), half), :]
    other = flat_ref[pl.ds(pl.multiple_of((1 - core) * half, half), half), :]
    give_ref[...] = nn(other, w_ref[...]).astype(BF16)
    keep_ref[...] = nn(mine, w_ref[...]).astype(BF16)


def out_project(idx, w_out, pieces):
    cols, dim = w_out.shape
    tok = pieces[0].shape[0]
    half = jax.ShapeDtypeStruct((tok // 2, dim), BF16)
    return pl.pallas_call(
        out_project_kernel,
        out_shape=[jax.ShapeDtypeStruct((tok, cols), BF16), half, half],
        in_specs=[SMEM] + [VMEM] * (1 + HEADS),
        out_specs=[VMEM] * 3,
        compiler_params=params(40),
        cost_estimate=cost(True),
        name="out_project",
    )(idx, w_out, *pieces)


def out_back_kernel(idx, w_ref, mine_ref, other_ref, *outs):
    half = mine_ref.shape[0]
    core = idx[2]
    for k, out in enumerate(outs):
        weights = w_ref[pl.ds(pl.multiple_of((idx[0] ^ k) * HD, HD), HD), :]
        out[pl.ds(pl.multiple_of(core * half, half), half), :] = nt(mine_ref[...], weights).astype(BF16)
        out[pl.ds(pl.multiple_of((1 - core) * half, half), half), :] = nt(
            other_ref[...], weights
        ).astype(BF16)


def out_back(idx, w_out, mine, other):
    half, dim = mine.shape
    return pl.pallas_call(
        out_back_kernel,
        out_shape=[jax.ShapeDtypeStruct((2 * half, HD), BF16)] * HEADS,
        in_specs=[SMEM] + [VMEM] * 3,
        out_specs=[VMEM] * HEADS,
        compiler_params=params(40),
        cost_estimate=cost(True),
        name="out_back",
    )(idx, w_out, mine, other)


def norm_kernel(x_ref, chip_ref, far_ref, gain_ref, bias_ref, bucket_ref, sum_ref, out_ref):
    dim = x_ref.shape[1]
    total = x_ref[...].astype(F32) + (chip_ref[...].astype(F32) + far_ref[...].astype(F32))
    sum_ref[...] = total
    normed, _ = normalise(total)
    out_ref[:, :dim] = (normed * gain_ref[...] + bias_ref[...]).astype(BF16)
    out_ref[:, dim:] = jnp.broadcast_to(bucket_ref[...], (total.shape[0], HD)).astype(BF16)


def norm(x, chip, far, gain, bias, buckets):
    rows, dim = x.shape
    tile = rows // 4
    spec = pl.BlockSpec((tile, dim), lambda i: (i, 0))
    wide = pl.BlockSpec((tile, dim + HD), lambda i: (i, 0))
    return pl.pallas_call(
        norm_kernel,
        grid=(4,),
        out_shape=[
            jax.ShapeDtypeStruct((rows, dim), F32),
            jax.ShapeDtypeStruct((rows, dim + HD), BF16),
        ],
        in_specs=[spec, spec, spec, whole((1, dim)), whole((1, dim))]
        + [pl.BlockSpec((tile, 1), lambda i: (i, 0))],
        out_specs=[spec, wide],
        compiler_params=params(24),
        cost_estimate=cost(True),
        name="norm",
    )(x, chip, far, gain, bias, buckets)


def norm_back_kernel(chip_ref, far_ref, x_ref, base_ref, gain_ref, wide_ref, low_ref, dg_ref, db_ref):
    grad = chip_ref[...].astype(F32) + far_ref[...].astype(F32)
    normed, inverse = normalise(x_ref[...].astype(F32))
    scaled = grad * gain_ref[...]
    back = inverse * (
        scaled
        - jnp.mean(scaled, axis=-1, keepdims=True)
        - normed * jnp.mean(scaled * normed, axis=-1, keepdims=True)
    )
    total = base_ref[...].astype(F32) + back
    wide_ref[...] = total
    low_ref[...] = total.astype(BF16)

    @pl.when(pl.program_id(0) == 0)
    def _():
        dg_ref[...] = jnp.zeros_like(dg_ref)
        db_ref[...] = jnp.zeros_like(db_ref)

    dg_ref[...] += jnp.sum(grad * normed, axis=0, keepdims=True)
    db_ref[...] += jnp.sum(grad, axis=0, keepdims=True)


def norm_back(chip, far, x, base, gain):
    rows, dim = chip.shape
    tile = rows // 4
    spec = pl.BlockSpec((tile, dim), lambda i: (i, 0))
    row = whole((1, dim))
    return pl.pallas_call(
        norm_back_kernel,
        grid=(4,),
        out_shape=[
            jax.ShapeDtypeStruct((rows, dim), F32),
            jax.ShapeDtypeStruct((rows, dim), BF16),
            jax.ShapeDtypeStruct((1, dim), F32),
            jax.ShapeDtypeStruct((1, dim), F32),
        ],
        in_specs=[spec] * 4 + [row],
        out_specs=[spec, spec, row, row],
        compiler_params=params(24),
        cost_estimate=cost(True),
        name="norm_back",
    )(chip, far, x, base, gain)


def relu_of(idx, ref, weights):
    dim = weights.shape[0]
    kept = ref[:, dim : dim + 1].astype(F32) >= idx[5].astype(F32)
    return jnp.where(kept, jnp.maximum(nn(ref[:, :dim], weights), 0.0), 0.0)


def feed_kernel(with_act, with_back, idx, mine_ref, other_ref, w_ref, gact_ref, *refs):
    half = mine_ref.shape[0]
    weights = w_ref[...]
    act_ref = refs[0] if with_act else None
    du_ref = refs[1 if with_act else 0]
    for at, ref in ((0, mine_ref), (half, other_ref)):
        rows = slice(at, at + half)
        relu = relu_of(idx, ref, weights)
        if with_act:
            act_ref[rows, :] = (relu * relu).astype(BF16)
        du_ref[rows, :] = (gact_ref[rows, :].astype(F32) * 2.0 * relu).astype(BF16)
    if with_back:
        keep_out, give_out, acc_ref = refs[2:]
        step = pl.program_id(0)

        @pl.when(step == 0)
        def _():
            acc_ref[...] = nt(du_ref[...], weights)

        @pl.when(step > 0)
        def _():
            acc_ref[...] += nt(du_ref[...], weights)

        @pl.when(step == pl.num_programs(0) - 1)
        def _():
            keep_out[...] = acc_ref[:half, :].astype(BF16)
            give_out[...] = acc_ref[half:, :].astype(BF16)


def feed_forward(idx, mine, other, w_up, gact, with_act, with_back):
    half, wide = mine.shape
    dim, hidden = w_up.shape
    tile = min(hidden, 512)
    tall = jax.ShapeDtypeStruct((2 * half, hidden), BF16)
    part = jax.ShapeDtypeStruct((half, dim), BF16)
    spec = pl.BlockSpec((2 * half, tile), lambda i, idx: (0, i))
    n_tall = 2 if with_act else 1
    return pl.pallas_call(
        functools.partial(feed_kernel, with_act, with_back),
        grid_spec=pltpu.PrefetchScalarGridSpec(
            num_scalar_prefetch=1,
            grid=(hidden // tile,),
            in_specs=[
                whole((half, wide)),
                whole((half, wide)),
                pl.BlockSpec((dim, tile), lambda i, idx: (0, i)),
                spec,
            ],
            out_specs=[spec] * n_tall + ([whole((half, dim))] * 2 if with_back else []),
            scratch_shapes=[pltpu.VMEM((2 * half, dim), F32)] if with_back else [],
        ),
        out_shape=[tall] * n_tall + ([part, part] if with_back else []),
        compiler_params=params(48),
        cost_estimate=cost(with_back),
        name="feed_own" if with_back else "feed_far",
    )(idx, mine, other, w_up, gact)


def feed_down_kernel(act_ref, w_ref, *refs):
    outs, acc_ref = refs[:4], refs[4]
    step = pl.program_id(0)

    @pl.when(step == 0)
    def _():
        acc_ref[...] = nn(act_ref[...], w_ref[...])

    @pl.when(step > 0)
    def _():
        acc_ref[...] += nn(act_ref[...], w_ref[...])

    @pl.when(step == pl.num_programs(0) - 1)
    def _():
        rows = outs[0].shape[0]
        for k, out in enumerate(outs):
            out[...] = acc_ref[k * rows : (k + 1) * rows, :].astype(BF16)


def feed_down(act, w_down):
    tok, hidden = act.shape
    dim = w_down.shape[1]
    tile = min(hidden, 1024)
    part = (tok // 4, dim)
    return pl.pallas_call(
        feed_down_kernel,
        grid=(hidden // tile,),
        out_shape=[jax.ShapeDtypeStruct(part, BF16)] * 4,
        in_specs=[
            pl.BlockSpec((tok, tile), lambda i: (0, i)),
            pl.BlockSpec((tile, dim), lambda i: (i, 0)),
        ],
        out_specs=[whole(part)] * 4,
        scratch_shapes=[pltpu.VMEM((tok, dim), F32)],
        compiler_params=params(40),
        cost_estimate=cost(False),
        name="feed_down",
    )(act, w_down)


def back_act_kernel(mine_ref, other_ref, w_ref, out_ref):
    half = mine_ref.shape[0]
    out_ref[:half, :] = nt(mine_ref[...], w_ref[...]).astype(BF16)
    out_ref[half:, :] = nt(other_ref[...], w_ref[...]).astype(BF16)


def back_act(mine, other, w_down):
    half, dim = mine.shape
    hidden = w_down.shape[0]
    tile = min(hidden, 512)
    return pl.pallas_call(
        back_act_kernel,
        grid=(hidden // tile,),
        out_shape=jax.ShapeDtypeStruct((2 * half, hidden), BF16),
        in_specs=[
            whole((half, dim)),
            whole((half, dim)),
            pl.BlockSpec((tile, dim), lambda i: (i, 0)),
        ],
        out_specs=pl.BlockSpec((2 * half, tile), lambda i: (0, i)),
        compiler_params=params(40),
        cost_estimate=cost(False),
        name="back_act",
    )(mine, other, w_down)


def product_kernel(idx, *refs):
    cols, near_ref, far_ref, out_ref, turn_ref = refs[:4], refs[4], refs[5], refs[6], refs[7]
    half = cols[0].shape[0]
    for k, ref in enumerate(cols):
        turn_ref[:, k * half : (k + 1) * half] = ref[...].astype(F32).T.astype(BF16)
    width = out_ref.shape[1]
    tile = min(width, 512)
    starts = [pl.multiple_of(idx[3 + j] * half, half) for j in range(2)]
    for at in range(0, width, tile):
        lanes = slice(at, at + tile)
        total = None
        for k in range(4):
            rows = (near_ref, far_ref)[k // 2][pl.ds(starts[k % 2], half), lanes]
            term = nn(turn_ref[:, k * half : (k + 1) * half], rows)
            total = term if total is None else total + term
        out_ref[:, lanes] = total.astype(BF16)


def product(idx, cols, near, far, dim):
    half = cols[0].shape[0]
    tok, width = near.shape
    block = dim // (2 * HEADS)
    spec = pl.BlockSpec((half, block), lambda k, idx: (0, 2 * k + idx[1]))
    return pl.pallas_call(
        product_kernel,
        grid_spec=pltpu.PrefetchScalarGridSpec(
            num_scalar_prefetch=1,
            grid=(HEADS,),
            in_specs=[spec] * 4 + [whole((tok, width))] * 2,
            out_specs=pl.BlockSpec((block, width), lambda k, idx: (k, 0)),
            scratch_shapes=[pltpu.VMEM((block, 4 * half), BF16)],
        ),
        out_shape=jax.ShapeDtypeStruct((HEADS * block, width), BF16),
        compiler_params=params(40),
        cost_estimate=cost(False),
        name="product",
    )(idx, *cols, near, far)


def head_product_kernel(idx, h_ref, *refs):
    pieces, (give_ref, keep_ref, turn_ref) = refs[:HEADS], refs[HEADS:]
    tok = pieces[0].shape[0]
    block = h_ref.shape[1] // 2

    @pl.when(pl.program_id(0) == 0)
    def _():
        for k in range(HEADS):
            turn_ref[:, k * tok : (k + 1) * tok] = pieces[k][...].astype(F32).T.astype(BF16)

    total = None
    for k in range(HEADS):
        rows = h_ref[pl.ds(pl.multiple_of((idx[0] ^ k) * tok, tok), tok), :]
        term = nn(turn_ref[:, k * tok : (k + 1) * tok], rows)
        total = term if total is None else total + term
    first, second = total[:, :block], total[:, block:]
    odd = idx[1] == 1
    give_ref[0] = jnp.where(odd, first, second).astype(BF16)
    keep_ref[0] = jnp.where(odd, second, first).astype(BF16)


def head_product(idx, h_all, pieces):
    rows, dim = h_all.shape
    block = dim // (2 * HEADS)
    out = jax.ShapeDtypeStruct((HEADS, 3 * HD, block), BF16)
    spec = pl.BlockSpec((1, 3 * HD, block), lambda k, idx: (k, 0, 0))
    return pl.pallas_call(
        head_product_kernel,
        grid_spec=pltpu.PrefetchScalarGridSpec(
            num_scalar_prefetch=1,
            grid=(HEADS,),
            in_specs=[pl.BlockSpec((rows, 2 * block), lambda k, idx: (0, idx[0] ^ k))]
            + [whole((rows // HEADS, 3 * HD))] * HEADS,
            out_specs=[spec, spec],
            scratch_shapes=[pltpu.VMEM((3 * HD, rows), BF16)],
        ),
        out_shape=[out, out],
        compiler_params=params(40),
        cost_estimate=cost(False),
        name="head_product",
    )(idx, h_all, *pieces)


def head_add_kernel(keep_ref, got_ref, after_ref, *outs):
    del after_ref
    for k, out in enumerate(outs):
        out[...] = (keep_ref[k].astype(F32) + got_ref[k].astype(F32)).astype(BF16)


def head_add(keep, got, after):
    return pl.pallas_call(
        head_add_kernel,
        out_shape=[jax.ShapeDtypeStruct(keep.shape[1:], BF16)] * HEADS,
        in_specs=[VMEM, VMEM, ANY],
        out_specs=[VMEM] * HEADS,
        compiler_params=params(24),
        cost_estimate=cost(False),
        name="head_add",
    )(keep, got, after)


def head_place_kernel(idx, *refs):
    pieces, out_ref = refs[:HEADS], refs[HEADS]
    for k, piece in enumerate(pieces):
        for s in range(3):
            out_ref[s, :, pl.ds(pl.multiple_of((idx[0] ^ k) * HD, HD), HD)] = (
                piece[s * HD : (s + 1) * HD, :].astype(F32).T
            )


def head_place(idx, pieces):
    rows, block = pieces[0].shape
    return pl.pallas_call(
        head_place_kernel,
        out_shape=jax.ShapeDtypeStruct((3, block, HEADS * HD), F32),
        in_specs=[SMEM] + [VMEM] * HEADS,
        out_specs=VMEM,
        compiler_params=params(24),
        cost_estimate=cost(False),
        name="head_place",
    )(idx, *pieces)


def project_back_kernel(idx, w_ref, *refs):
    pieces, (keep_ref, give_a_ref, give_b_ref, flat_ref, acc_ref) = refs[:HEADS], refs[HEADS:]
    half = keep_ref.shape[0]
    core = idx[2]
    step = pl.program_id(0)

    for s in range(3):

        @pl.when(step == s)
        def _(s=s):
            for k in range(HEADS):
                lanes = pl.ds(pl.multiple_of((idx[0] ^ k) * HD, HD), HD)
                flat_ref[:, lanes] = pieces[k][:, s * HD : (s + 1) * HD]

    @pl.when(step == 0)
    def _():
        acc_ref[...] = nt(flat_ref[...], w_ref[0])

    @pl.when(step > 0)
    def _():
        acc_ref[...] += nt(flat_ref[...], w_ref[0])

    @pl.when(step == 2)
    def _():
        part = half // 2
        for k, out in enumerate((give_a_ref, give_b_ref)):
            start = pl.multiple_of((1 - core) * half + k * part, part)
            out[...] = acc_ref[pl.ds(start, part), :].astype(BF16)
        keep_ref[...] = acc_ref[pl.ds(pl.multiple_of(core * half, half), half), :].astype(BF16)


def project_back(idx, w_qkv, pieces):
    tok = pieces[0].shape[0]
    _, dim, cols = w_qkv.shape
    return pl.pallas_call(
        project_back_kernel,
        grid_spec=pltpu.PrefetchScalarGridSpec(
            num_scalar_prefetch=1,
            grid=(3,),
            in_specs=[pl.BlockSpec((1, dim, cols), lambda s, idx: (s, 0, 0))]
            + [whole((tok, 3 * HD))] * HEADS,
            out_specs=[whole((tok // 2, dim))] + [whole((tok // 4, dim))] * 2,
            scratch_shapes=[pltpu.VMEM((tok, cols), BF16), pltpu.VMEM((tok, dim), F32)],
        ),
        out_shape=[jax.ShapeDtypeStruct((tok // 2, dim), BF16)]
        + [jax.ShapeDtypeStruct((tok // 4, dim), BF16)] * 2,
        compiler_params=params(40),
        cost_estimate=cost(True),
        name="project_back",
    )(idx, w_qkv, *pieces)


def join_kernel(idx, mine_ref, other_ref, out_ref):
    half = mine_ref.shape[0]
    core = idx[2]
    out_ref[pl.ds(pl.multiple_of(core * half, half), half), :] = mine_ref[...].astype(out_ref.dtype)
    out_ref[pl.ds(pl.multiple_of((1 - core) * half, half), half), :] = other_ref[...].astype(
        out_ref.dtype
    )


def join(idx, mine, other, dtype):
    half, dim = mine.shape
    return pl.pallas_call(
        join_kernel,
        out_shape=jax.ShapeDtypeStruct((2 * half, dim), dtype),
        in_specs=[SMEM, VMEM, VMEM],
        out_specs=VMEM,
        compiler_params=params(24),
        cost_estimate=cost(False),
        name="join",
    )(idx, mine, other)


def body(
    depth,
    layer_input,
    ln1_gain,
    ln1_bias,
    w_qkv,
    w_out,
    ln2_gain,
    ln2_bias,
    w_up,
    w_down,
    buckets,
    lengths,
    block_order,
    grad_out,
):
    tok, dim = layer_input.shape
    half = tok // 2
    scale = 1.0 / math.sqrt(HD)
    r, h, y, x, c = (lax.axis_index(a) for a in ("r", PLANE, "y") + TP)
    blk = lax.axis_index(BLK)
    tp = lax.axis_index(TP)
    idx_rows = jnp.stack([h, y, c, c, 1 - c]).astype(jnp.int32)
    idx = jnp.stack([h, y, c, jnp.zeros_like(c), jnp.ones_like(c), tp]).astype(jnp.int32)
    gains = [v.reshape(1, dim) for v in (ln1_gain, ln1_bias, ln2_gain, ln2_bias)]

    def half_of(values, which):
        return lax.dynamic_slice_in_dim(values, which * half, half, 0)

    def regroup(values):
        if depth == 1:
            return values
        rows = values.shape[0]
        split = values[:, :dim].reshape(rows, depth, HEADS, 2, dim // (2 * HEADS * depth))
        return split.transpose(0, 2, 3, 1, 4).reshape(rows, dim)

    def scatter(values):
        if depth > 1:
            split = values.reshape(HEADS, depth, -1, values.shape[1])
            values = split.transpose(1, 0, 2, 3).reshape(values.shape)
        return lax.psum_scatter(values, ("r",) + PLANE, scatter_dimension=0, tiled=True)

    starts = jnp.cumsum(lengths) - lengths

    def firsts_of(places):
        return jnp.max(jnp.where(starts <= places[..., None], starts, 0), axis=-1)

    inside = jnp.arange(half, dtype=jnp.int32)
    own_places = (
        lax.dynamic_slice_in_dim(block_order, 2 * blk, 2, 0)[:, None] * half + inside
    ).reshape(tok)
    cosine, sine = rotary_tables(own_places - firsts_of(own_places))

    def chip_sum(keep, give):
        return (keep.astype(F32) + swap(give, "c").astype(F32)).astype(BF16)

    grad_mine, grad_other = half_of(grad_out, c), half_of(grad_out, 1 - c)
    own_rows, *projected = project(idx, layer_input, gains[0], gains[1], cosine, sine, w_qkv)
    queries, near_kv = list(projected[:HEADS]), list(projected[HEADS:])
    near_kv = [near_kv[0]] + [plane_swap(near_kv[k], k) for k in range(1, HEADS)]
    *queries[1:], near_kv[2] = ordered(*queries[1:], near_kv[2])
    queries = [queries[0]] + [plane_swap(queries[k], k) for k in range(1, HEADS)]
    y_grad = swap(grad_mine, "y")

    relative = h ^ jnp.arange(HEADS, dtype=jnp.int32)
    group_order = lax.dynamic_index_in_dim(
        block_order.reshape(depth, HEADS, 2, 2), r, 0, keepdims=False
    )
    group_order = lax.dynamic_index_in_dim(group_order, y, 1, keepdims=False)
    chosen = relative[:, None] == jnp.arange(HEADS, dtype=jnp.int32)[None, :]
    query_at = jnp.sum(jnp.where(chosen[:, :, None], group_order[None], 0), axis=1).reshape(-1)
    query_places = query_at[:, None] * half + inside
    query_firsts = firsts_of(query_places)
    query_low = query_firsts[:, 0] // half
    query_full = jnp.minimum((query_firsts[:, -1] + half - 1) // half, query_at)
    block_count = block_order.shape[0]
    slots = jnp.argmax(
        block_order[None, :] == jnp.arange(block_count, dtype=jnp.int32)[:, None], axis=1
    ).astype(jnp.int32)
    slot_dev = slots // 2
    slot_plane = slot_dev // 2
    key_row = (
        jnp.where(slot_dev % 2 == y, 0, block_count // 2)
        + slot_plane // HEADS * (2 * HEADS)
        + ((slot_plane % HEADS) ^ h) * 2
        + slots % 2
    )
    group_cos, group_sin = rotary_tables((query_places - query_firsts).reshape(2 * HEADS * half))
    tables = (query_at, query_low, query_full, key_row, query_firsts.reshape(2 * HEADS, 1, half))

    grad_act = back_act(grad_mine, grad_other, w_down)
    far_first = swap(near_kv[0], "y")
    far_first, y_grad, grad_act, group_cos, group_sin, *near_kv[1:] = ordered(
        far_first, y_grad, grad_act, group_cos, group_sin, *near_kv[1:]
    )
    if depth == 1:
        keys_values = near_kv + [far_first, swap(jnp.concatenate(near_kv[1:]), "y")]
    else:
        near_all = lax.all_gather(jnp.concatenate(near_kv), "r", axis=0, tiled=True)
        keys_values = [near_all, swap(near_all, "y")]
    y_grad_other = swap(y_grad, "c")
    y_grad_other, *queries[1:], keys_values[-1] = ordered(
        y_grad_other, *queries[1:], keys_values[-1]
    )

    *attended, lse = attend(half, scale, tables, queries, keys_values)
    pieces = [attended[0]] + [plane_swap(attended[k], k) for k in range(1, HEADS)]
    flat, keep, give = out_project(idx, w_out, pieces)
    chip = chip_sum(keep, give)
    chip_far = swap(chip, "x")
    y_grad, flat = ordered(y_grad, flat)
    y_grad_act = back_act(y_grad, y_grad_other, w_down)
    y_grad_act, chip_far = ordered(y_grad_act, chip_far)

    own_rows, flat = ordered(own_rows, flat)
    h_all = lax.all_gather(own_rows, PLANE + ("c",), axis=0, tiled=True)
    y_flat = swap(flat, "y")
    y_flat, chip_far = ordered(y_flat, chip_far)
    my_buckets = half_of(buckets, c).reshape(half, 1)
    x_mid, h_mine = norm(
        half_of(layer_input, c), chip, chip_far, gains[2], gains[3], my_buckets
    )
    h_other = swap(h_mine, "c")
    y_h = swap(h_mine, "y")
    act, du, keep, give = feed_forward(
        idx, h_mine, h_other, w_up, grad_act, True, True
    )
    chip = chip_sum(keep, give)
    chip_far = swap(chip, "x")

    y_h_other = swap(y_h, "c")
    y_act, y_du = feed_forward(idx, y_h, y_h_other, w_up, y_grad_act, True, False)
    pair_grads = [regroup(v) for v in (grad_mine, grad_other, y_grad, y_grad_other)]
    down_sum = product(idx, pair_grads, act, y_act, dim)
    down_sum, h_all, chip_far = ordered(down_sum, h_all, chip_far)
    down_part = scatter(down_sum)

    grad_mid, dy_mine, gain_two_grad, bias_two_grad = norm_back(
        chip, chip_far, x_mid, grad_mine, gains[2]
    )
    dy_other = swap(dy_mine, "c")
    grads = list(out_back(idx, w_out, dy_mine, dy_other))
    grads = [grads[0]] + [plane_swap(grads[k], k) for k in range(1, HEADS)]

    y_dy = swap(dy_mine, "y")
    for_up, dy_other = ordered(h_mine, dy_other)
    up_sum = product(idx, [regroup(v) for v in (for_up, h_other, y_h, y_h_other)], du, y_du, dim)
    up_sum, y_dy, *grads[1:] = ordered(up_sum, y_dy, *grads[1:])
    y_dy_other = swap(y_dy, "c")

    *dq, near, far = attend_back(
        half, scale, tables, lse, group_cos, group_sin, queries, keys_values, attended, grads
    )
    got = swap(far, "y")

    for_feed, near = ordered(act, near)
    feed = list(feed_down(for_feed, w_down))
    wout_cols = [regroup(v) for v in (dy_mine, dy_other, y_dy, y_dy_other)]
    wout_cols[0], near = ordered(wout_cols[0], near)
    wout_sum = product(idx_rows, wout_cols, flat, y_flat, dim)
    wout_sum, down_part, feed[1], got = ordered(wout_sum, down_part, feed[1], got)
    if depth > 1:
        near = lax.psum_scatter(near, "r", scatter_dimension=0, tiled=True)
        got = lax.psum_scatter(got, "r", scatter_dimension=0, tiled=True)
    mixed = list(settle(near, got, group_cos, group_sin, dq))
    pieces = [mixed[0]] + [plane_swap(mixed[k], k) for k in range(1, HEADS)]
    feed_chip = [chip_sum(feed[k], feed[k + 2]) for k in range(2)]
    feed_far = [swap(v, "x") for v in feed_chip]

    head_give, head_keep = head_product(idx, regroup(h_all), mixed)
    wout_sum, up_sum, mixed[1] = ordered(wout_sum, up_sum, mixed[1])
    late_sum = jnp.concatenate([up_sum, wout_sum], axis=1)
    feed_far[0], feed_far[1], head_give, late_sum, *pieces[1:] = ordered(
        *feed_far, head_give, late_sum, *pieces[1:]
    )
    late_part = scatter(late_sum)
    keep, *gives = project_back(idx, w_qkv, pieces)
    chip = jnp.concatenate([swap(v, "c") for v in gives])
    chip = (keep.astype(F32) + chip.astype(F32)).astype(BF16)
    chip_far = swap(chip, "x")

    head_got = swap(head_give, "y")
    feed_chip, feed_far = jnp.concatenate(feed_chip), jnp.concatenate(feed_far)
    out_mine = (x_mid + (feed_chip.astype(F32) + feed_far.astype(F32))).astype(BF16)
    out_mine, chip = ordered(out_mine, chip)
    out_other = swap(out_mine, "c")
    out_other, chip_far = ordered(out_other, chip_far)
    layer_output = join(idx, out_mine, out_other, BF16)
    head_got, chip_far = ordered(head_got, chip_far)

    _, grad_low, gain_one_grad, bias_one_grad = norm_back(
        chip, chip_far, half_of(layer_input, c), grad_mid, gains[0]
    )
    head_sum = list(head_add(head_keep, head_got, grad_low))
    if depth > 1:
        head_sum = [lax.psum_scatter(v, "r", scatter_dimension=1, tiled=True) for v in head_sum]
    head_pieces = [head_sum[0]] + [plane_swap(head_sum[k], k) for k in range(1, HEADS)]
    grad_input = join(idx, grad_low, swap(grad_low, "c"), F32)

    counts = jnp.sum(
        (half_of(buckets, c)[:, None] == jnp.arange(NB, dtype=jnp.int32)[None, :]).astype(F32),
        axis=0,
    )
    sums = jnp.concatenate(
        [v.reshape(dim) for v in (gain_one_grad, bias_one_grad, gain_two_grad, bias_two_grad)]
        + [counts]
    )
    if depth > 1:
        sums = lax.psum(sums, "r")
    one, two, three = (plane_swap(sums, k) for k in range(1, HEADS))
    sums = (sums + one) + (two + three)
    sums = sums + swap(sums, "y")
    qkv_part = head_place(idx, head_pieces)
    sums, late_part, grad_input, layer_output, qkv_part = ordered(
        sums, late_part, grad_input, layer_output, qkv_part
    )
    hidden = w_up.shape[1]
    up_part, wout_part = late_part[:, :hidden], late_part[:, hidden:]
    sums = sums + swap(sums, "c")
    return (
        layer_output,
        grad_input,
        sums[:dim],
        sums[dim : 2 * dim],
        qkv_part,
        wout_part.astype(F32).T,
        sums[2 * dim : 3 * dim],
        sums[3 * dim : 4 * dim],
        up_part.astype(F32),
        down_part.astype(F32).T,
        sums[4 * dim :].astype(jnp.int32),
    )


def solution(mesh):
    depth = mesh.shape["blk"] // (2 * HEADS)
    fine = Mesh(mesh.devices.reshape(depth, 2, 2, 2, 2, 2), BLK + TP)
    return jax.shard_map(
        functools.partial(body, depth),
        mesh=fine,
        in_specs=(
            P(BLK, None),
            P(),
            P(),
            P(None, None, TP),
            P(TP, None),
            P(),
            P(),
            P(None, TP),
            P(TP, None),
            P(BLK),
            P(),
            P(),
            P(BLK, None),
        ),
        out_specs=(
            P(BLK, None),
            P(BLK, None),
            P(),
            P(),
            P(None, BLK, TP),
            P(TP, BLK),
            P(),
            P(),
            P(BLK, TP),
            P(TP, BLK),
            P(),
        ),
        check_vma=False,
    )
```

```python
import functools
import math

import jax
import jax.numpy as jnp
from jax import lax
from jax.experimental import pallas as pl
from jax.experimental.pallas import tpu as pltpu
from jax.sharding import Mesh
from jax.sharding import PartitionSpec as P

HD = 128
FF = 8192
NB = 4
HEADS = 4
EPSILON = 1e-05
ROPE_BASE = 10000.0
PLANE = ("hh", "hl")
LOG_E = math.log2(math.e)
HIDDEN = -1e30
GROUPS = (4, 2)
BLK = ("r", "hh", "hl", "y")
TP = ("x", "c")
F32 = jnp.float32
BF16 = jnp.bfloat16
SMEM = pl.BlockSpec(memory_space=pltpu.SMEM)
VMEM = pl.BlockSpec(memory_space=pltpu.VMEM)
ANY = pl.BlockSpec(memory_space=pl.ANY)


def swap(value, axis):
    return lax.ppermute(value, axis, [(0, 1), (1, 0)])


def plane_swap(value, k):
    return lax.ppermute(value, PLANE, [(i, i ^ k) for i in range(HEADS)])


def ordered(*values):
    return lax.optimization_barrier(values)


def nt(lhs, rhs):
    return lax.dot_general(lhs, rhs, (((1,), (1,)), ((), ())), preferred_element_type=F32)


def tn(lhs, rhs):
    return lax.dot_general(lhs, rhs, (((0,), (0,)), ((), ())), preferred_element_type=F32)


def nn(lhs, rhs):
    return lax.dot_general(lhs, rhs, (((1,), (0,)), ((), ())), preferred_element_type=F32)


def params(mib):
    return pltpu.CompilerParams(vmem_limit_bytes=60 * 2**20)


def cost(on_path):
    return pl.CostEstimate(flops=10**9 if on_path else 1, bytes_accessed=1, transcendentals=0)


def whole(shape):
    return pl.BlockSpec(shape, lambda *_: (0,) * len(shape))


def normalise(values):
    centre = values - jnp.mean(values, axis=-1, keepdims=True)
    inverse = lax.rsqrt(jnp.mean(centre * centre, axis=-1, keepdims=True) + EPSILON)
    return (centre * inverse, inverse)


def rotary_tables(positions):
    freqs = ROPE_BASE ** (-(jnp.arange(HD // 2, dtype=F32) * 2.0 / HD))
    angles = positions.astype(F32)[:, None] * freqs[None, :]
    cosine, sine = jnp.cos(angles), jnp.sin(angles)
    return (
        jnp.concatenate([cosine, cosine], axis=-1),
        jnp.concatenate([-sine, sine], axis=-1),
    )


def rotate(values, cosine, sine):
    return values * cosine + pltpu.roll(values, HD // 2, 1) * sine


def project_kernel(idx, x_ref, gain_ref, bias_ref, cos_ref, sin_ref, w_ref, *refs):
    part_ref, q_outs, kv_outs = refs[0], refs[1 : 1 + HEADS], refs[1 + HEADS : 1 + 2 * HEADS]
    h_ref = refs[1 + 2 * HEADS]
    step = pl.program_id(0)

    @pl.when(step == 0)
    def _():
        normed, _ = normalise(x_ref[...].astype(F32))
        h_ref[...] = (normed * gain_ref[...] + bias_ref[...]).astype(BF16)
        rows = part_ref.shape[0]
        part_ref[...] = h_ref[pl.ds(pl.multiple_of(idx[2] * rows, rows), rows), :]

    both = nn(h_ref[...], jnp.concatenate([w_ref[0], w_ref[1]], axis=1))
    cosine, sine = cos_ref[...], sin_ref[...]
    queries = rotate(both[:, :HD], cosine, sine).astype(BF16)
    keys = rotate(both[:, HD:], cosine, sine).astype(BF16)
    values = nn(h_ref[...], w_ref[2]).astype(BF16)
    for k in range(HEADS):

        @pl.when(step == k)
        def _(k=k):
            q_outs[k][...] = queries
            kv_outs[k][:, :HD] = keys
            kv_outs[k][:, HD:] = values


def project(idx, x, gain, bias, cosine, sine, w_qkv):
    tok, dim = x.shape
    return pl.pallas_call(
        project_kernel,
        grid_spec=pltpu.PrefetchScalarGridSpec(
            num_scalar_prefetch=1,
            grid=(HEADS,),
            in_specs=[
                whole((tok, dim)),
                whole((1, dim)),
                whole((1, dim)),
                whole((tok, HD)),
                whole((tok, HD)),
                pl.BlockSpec((3, dim, HD), lambda k, idx: (0, 0, idx[0] ^ k)),
            ],
            out_specs=[whole((tok // 2, dim))]
            + [whole((tok, HD))] * HEADS
            + [whole((tok, 2 * HD))] * HEADS,
            scratch_shapes=[pltpu.VMEM((tok, dim), BF16)],
        ),
        out_shape=[jax.ShapeDtypeStruct((tok // 2, dim), BF16)]
        + [jax.ShapeDtypeStruct((tok, HD), BF16)] * HEADS
        + [jax.ShapeDtypeStruct((tok, 2 * HD), BF16)] * HEADS,
        compiler_params=params(40),
        cost_estimate=cost(True),
        name="project",
    )(idx, x, gain, bias, cosine, sine, w_qkv)


def visible_of(tile, key_block, query_places, query_firsts):
    key_places = key_block * tile + lax.broadcasted_iota(jnp.int32, (tile, 1), 0)
    return (key_places <= query_places) & (key_places >= query_firsts)


def gather_refs(refs, whole_ref):
    at = 0
    for ref in refs:
        whole_ref[at : at + ref.shape[0], :] = ref[...]
        at += ref.shape[0]


def over_blocks(low, full, at, masked, group, state):
    state = lax.fori_loop(low, full, masked, state)
    for size in GROUPS:
        count = lax.div(at - full, size)
        start = full
        state = lax.fori_loop(
            0, count, lambda j, st, s=size, a=start: group(a + s * j, s, st), state
        )
        full = full + size * count
    return lax.fori_loop(full, at + 1, masked, state)


def attend_kernel(tile, scale, n_kv, at_ref, low_ref, full_ref, row_ref, first_ref, *refs):
    q_refs, kv_refs, refs = refs[:HEADS], refs[HEADS : HEADS + n_kv], refs[HEADS + n_kv :]
    outs, (lse_ref, q_all, kv_all) = refs[:HEADS], refs[HEADS:]
    gather_refs(q_refs, q_all)
    gather_refs(kv_refs, kv_all)
    lanes = lax.broadcasted_iota(jnp.int32, (1, tile), 1)
    per_out = outs[0].shape[0] // tile
    scale_two = scale * LOG_E

    def one_block(i, carry):
        rows = pl.ds(pl.multiple_of(i * tile, tile), tile)
        queries = q_all[rows, :]
        firsts = first_ref[i]
        places = at_ref[i] * tile + lanes

        def key_rows(b):
            return pl.ds(pl.multiple_of(row_ref[b] * tile, tile), tile)

        def absorb(state, scores, values):
            run_max, run_sum, run_acc = state
            new_max = run_max
            for part in scores:
                new_max = jnp.maximum(new_max, jnp.max(part, axis=0, keepdims=True))
            factor = jnp.exp2(run_max - new_max)
            new_sum = run_sum * factor
            new_acc = run_acc * factor
            for part, rows in zip(scores, values, strict=True):
                probs = jnp.exp2(part - new_max)
                new_sum = new_sum + jnp.sum(probs, axis=0, keepdims=True)
                new_acc = new_acc + tn(rows, probs.astype(BF16))
            return (new_max, new_sum, new_acc)

        def masked(b, state):
            krows = key_rows(b)
            scores = nt(kv_all[krows, :HD], queries) * scale_two
            scores = jnp.where(visible_of(tile, b, places, firsts), scores, HIDDEN)
            return absorb(state, [scores], [kv_all[krows, HD:]])

        def group(b, size, state):
            rows = [key_rows(b + k) for k in range(size)]
            scores = [nt(kv_all[k, :HD], queries) * scale_two for k in rows]
            return absorb(state, scores, [kv_all[k, HD:] for k in rows])

        run_max, run_sum, run_acc = over_blocks(
            low_ref[i],
            full_ref[i],
            at_ref[i],
            masked,
            group,
            (
                jnp.full((1, tile), HIDDEN / 10, F32),
                jnp.zeros((1, tile), F32),
                jnp.zeros((HD, tile), F32),
            ),
        )
        q_all[rows, :] = (run_acc / run_sum).T.astype(BF16)
        lse_ref[i] = run_max + jnp.log2(run_sum)
        return carry

    lax.fori_loop(0, HEADS * per_out, one_block, 0)
    for k, out in enumerate(outs):
        out[...] = q_all[k * per_out * tile : (k + 1) * per_out * tile, :]


def attend_back_kernel(
    tile,
    scale,
    n_kv,
    at_ref,
    low_ref,
    full_ref,
    row_ref,
    first_ref,
    lse_ref,
    *refs,
):
    q_refs, kv_refs, refs = refs[:HEADS], refs[HEADS : HEADS + n_kv], refs[HEADS + n_kv :]
    o_refs, do_refs, dq_refs = refs[:HEADS], refs[HEADS : 2 * HEADS], refs[2 * HEADS : 3 * HEADS]
    near_ref, far_ref, q_all, kv_all, do_all, dot_all, acc_ref = refs[3 * HEADS :]
    gather_refs(q_refs, q_all)
    gather_refs(kv_refs, kv_all)
    gather_refs(do_refs, do_all)
    acc_ref[...] = jnp.zeros_like(acc_ref)
    lanes = lax.broadcasted_iota(jnp.int32, (1, tile), 1)
    per_out = dq_refs[0].shape[0] // tile
    scale_two = scale * LOG_E
    for k in range(HEADS):
        for j in range(per_out):
            piece = slice(j * tile, (j + 1) * tile)
            products = do_refs[k][piece, :].astype(F32) * o_refs[k][piece, :].astype(F32)
            dot_all[k * per_out + j] = jnp.sum(products.T, axis=0, keepdims=True)

    def one_block(i, carry):
        rows = pl.ds(pl.multiple_of(i * tile, tile), tile)
        queries = q_all[rows, :]
        grads = do_all[rows, :]
        firsts = first_ref[i]
        places = at_ref[i] * tile + lanes
        log_sums = lse_ref[i]
        deltas = dot_all[i]

        def one(b, grad_q, hide):
            krows = pl.ds(pl.multiple_of(row_ref[b] * tile, tile), tile)
            keys = kv_all[krows, :HD]
            probs = jnp.exp2(nt(keys, queries) * scale_two - log_sums)
            if hide:
                probs = jnp.where(visible_of(tile, b, places, firsts), probs, 0.0)
            grad_probs = nt(kv_all[krows, HD:], grads)
            grad_scores = (probs * (grad_probs - deltas)).astype(BF16)
            acc_ref[krows, HD:] += nn(probs.astype(BF16), grads)
            acc_ref[krows, :HD] += nn(grad_scores, queries)
            return grad_q + tn(keys, grad_scores)

        def group(b, size, grad_q):
            for k in range(size):
                grad_q = one(b + k, grad_q, False)
            return grad_q

        grad_q = over_blocks(
            low_ref[i],
            full_ref[i],
            at_ref[i],
            lambda b, grad_q: one(b, grad_q, True),
            group,
            jnp.zeros((HD, tile), F32),
        )
        do_all[rows, :] = (grad_q * scale).T.astype(BF16)
        return carry

    lax.fori_loop(0, HEADS * per_out, one_block, 0)
    for k, out in enumerate(dq_refs):
        out[...] = do_all[k * per_out * tile : (k + 1) * per_out * tile, :]
    near = near_ref.shape[0]
    near_ref[:, :HD] = (acc_ref[:near, :HD] * scale).astype(BF16)
    near_ref[:, HD:] = acc_ref[:near, HD:].astype(BF16)
    far_ref[:, :HD] = (acc_ref[near:, :HD] * scale).astype(BF16)
    far_ref[:, HD:] = acc_ref[near:, HD:].astype(BF16)


def attend(tile, scale, tables, pieces, keys_values):
    rows = HEADS * pieces[0].shape[0]
    kv_rows = sum(a.shape[0] for a in keys_values)
    operands = pieces + keys_values
    return pl.pallas_call(
        functools.partial(attend_kernel, tile, scale, len(keys_values)),
        out_shape=[jax.ShapeDtypeStruct((rows // HEADS, HD), BF16)] * HEADS
        + [jax.ShapeDtypeStruct((rows // tile, 1, tile), F32)],
        in_specs=[SMEM] * 4 + [VMEM] * (1 + len(operands)),
        out_specs=[VMEM] * (HEADS + 1),
        scratch_shapes=[pltpu.VMEM((rows, HD), BF16), pltpu.VMEM((kv_rows, 2 * HD), BF16)],
        compiler_params=params(50),
        cost_estimate=cost(True),
        name="attend",
    )(*tables, *operands)


def attend_back(tile, scale, tables, lse, pieces, keys_values, outs, grads):
    rows = HEADS * pieces[0].shape[0]
    kv_rows = sum(a.shape[0] for a in keys_values)
    operands = pieces + keys_values + outs + grads
    return pl.pallas_call(
        functools.partial(attend_back_kernel, tile, scale, len(keys_values)),
        out_shape=[jax.ShapeDtypeStruct((rows // HEADS, HD), BF16)] * HEADS
        + [jax.ShapeDtypeStruct((kv_rows // 2, 2 * HD), BF16)] * 2,
        in_specs=[SMEM] * 4 + [VMEM] * (2 + len(operands)),
        out_specs=[VMEM] * (HEADS + 2),
        scratch_shapes=[
            pltpu.VMEM((rows, HD), BF16),
            pltpu.VMEM((kv_rows, 2 * HD), BF16),
            pltpu.VMEM((rows, HD), BF16),
            pltpu.VMEM((rows // tile, 1, tile), F32),
            pltpu.VMEM((kv_rows, 2 * HD), F32),
        ],
        compiler_params=params(56),
        cost_estimate=cost(True),
        name="attend_back",
    )(*tables, lse, *operands)


def settle_kernel(near_ref, got_ref, cos_ref, sin_ref, *refs):
    dq_refs, outs = refs[:HEADS], refs[HEADS:]
    total = near_ref[...].astype(F32) + got_ref[...].astype(F32)
    for k, out in enumerate(outs):

        @pl.when(pl.program_id(0) == k)
        def _(k=k, out=out):
            cosine, sine = cos_ref[...], -sin_ref[...]
            out[:, :HD] = rotate(dq_refs[k][...].astype(F32), cosine, sine).astype(BF16)
            out[:, HD : 2 * HD] = rotate(total[:, :HD], cosine, sine).astype(BF16)
            out[:, 2 * HD :] = total[:, HD:].astype(BF16)


def settle(near, got, cosine, sine, dq_pieces):
    rows = near.shape[0]
    tile = rows // HEADS
    spec = pl.BlockSpec((tile, 2 * HD), lambda k: (k, 0))
    table = pl.BlockSpec((tile, HD), lambda k: (k, 0))
    return pl.pallas_call(
        settle_kernel,
        grid=(HEADS,),
        out_shape=[jax.ShapeDtypeStruct((tile, 3 * HD), BF16)] * HEADS,
        in_specs=[spec, spec, table, table] + [whole((tile, HD))] * HEADS,
        out_specs=[whole((tile, 3 * HD))] * HEADS,
        compiler_params=params(24),
        cost_estimate=cost(True),
        name="settle",
    )(near, got, cosine, sine, *dq_pieces)


def out_project_kernel(idx, w_ref, *refs):
    pieces, (flat_ref, keep_ref, give_ref) = refs[:HEADS], refs[HEADS:]
    for k, piece in enumerate(pieces):
        flat_ref[:, pl.ds(pl.multiple_of((idx[0] ^ k) * HD, HD), HD)] = piece[...]
    half = keep_ref.shape[0]
    core = idx[2]
    mine = flat_ref[pl.ds(pl.multiple_of(core * half, half), half), :]
    other = flat_ref[pl.ds(pl.multiple_of((1 - core) * half, half), half), :]
    give_ref[...] = nn(other, w_ref[...]).astype(BF16)
    keep_ref[...] = nn(mine, w_ref[...]).astype(BF16)


def out_project(idx, w_out, pieces):
    cols, dim = w_out.shape
    tok = pieces[0].shape[0]
    half = jax.ShapeDtypeStruct((tok // 2, dim), BF16)
    return pl.pallas_call(
        out_project_kernel,
        out_shape=[jax.ShapeDtypeStruct((tok, cols), BF16), half, half],
        in_specs=[SMEM] + [VMEM] * (1 + HEADS),
        out_specs=[VMEM] * 3,
        compiler_params=params(40),
        cost_estimate=cost(True),
        name="out_project",
    )(idx, w_out, *pieces)


def out_back_kernel(idx, w_ref, mine_ref, other_ref, *outs):
    half = mine_ref.shape[0]
    core = idx[2]
    for k, out in enumerate(outs):
        weights = w_ref[pl.ds(pl.multiple_of((idx[0] ^ k) * HD, HD), HD), :]
        out[pl.ds(pl.multiple_of(core * half, half), half), :] = nt(mine_ref[...], weights).astype(BF16)
        out[pl.ds(pl.multiple_of((1 - core) * half, half), half), :] = nt(
            other_ref[...], weights
        ).astype(BF16)


def out_back(idx, w_out, mine, other):
    half, dim = mine.shape
    return pl.pallas_call(
        out_back_kernel,
        out_shape=[jax.ShapeDtypeStruct((2 * half, HD), BF16)] * HEADS,
        in_specs=[SMEM] + [VMEM] * 3,
        out_specs=[VMEM] * HEADS,
        compiler_params=params(40),
        cost_estimate=cost(True),
        name="out_back",
    )(idx, w_out, mine, other)


def norm_kernel(x_ref, chip_ref, far_ref, gain_ref, bias_ref, bucket_ref, sum_ref, out_ref):
    dim = x_ref.shape[1]
    total = x_ref[...].astype(F32) + (chip_ref[...].astype(F32) + far_ref[...].astype(F32))
    sum_ref[...] = total
    normed, _ = normalise(total)
    out_ref[:, :dim] = (normed * gain_ref[...] + bias_ref[...]).astype(BF16)
    out_ref[:, dim:] = jnp.broadcast_to(bucket_ref[...], (total.shape[0], HD)).astype(BF16)


def norm(x, chip, far, gain, bias, buckets):
    rows, dim = x.shape
    tile = rows // 4
    spec = pl.BlockSpec((tile, dim), lambda i: (i, 0))
    wide = pl.BlockSpec((tile, dim + HD), lambda i: (i, 0))
    return pl.pallas_call(
        norm_kernel,
        grid=(4,),
        out_shape=[
            jax.ShapeDtypeStruct((rows, dim), F32),
            jax.ShapeDtypeStruct((rows, dim + HD), BF16),
        ],
        in_specs=[spec, spec, spec, whole((1, dim)), whole((1, dim))]
        + [pl.BlockSpec((tile, 1), lambda i: (i, 0))],
        out_specs=[spec, wide],
        compiler_params=params(24),
        cost_estimate=cost(True),
        name="norm",
    )(x, chip, far, gain, bias, buckets)


def norm_back_kernel(chip_ref, far_ref, x_ref, base_ref, gain_ref, wide_ref, low_ref, dg_ref, db_ref):
    grad = chip_ref[...].astype(F32) + far_ref[...].astype(F32)
    normed, inverse = normalise(x_ref[...].astype(F32))
    scaled = grad * gain_ref[...]
    back = inverse * (
        scaled
        - jnp.mean(scaled, axis=-1, keepdims=True)
        - normed * jnp.mean(scaled * normed, axis=-1, keepdims=True)
    )
    total = base_ref[...].astype(F32) + back
    wide_ref[...] = total
    low_ref[...] = total.astype(BF16)

    @pl.when(pl.program_id(0) == 0)
    def _():
        dg_ref[...] = jnp.zeros_like(dg_ref)
        db_ref[...] = jnp.zeros_like(db_ref)

    dg_ref[...] += jnp.sum(grad * normed, axis=0, keepdims=True)
    db_ref[...] += jnp.sum(grad, axis=0, keepdims=True)


def norm_back(chip, far, x, base, gain):
    rows, dim = chip.shape
    tile = rows // 4
    spec = pl.BlockSpec((tile, dim), lambda i: (i, 0))
    row = whole((1, dim))
    return pl.pallas_call(
        norm_back_kernel,
        grid=(4,),
        out_shape=[
            jax.ShapeDtypeStruct((rows, dim), F32),
            jax.ShapeDtypeStruct((rows, dim), BF16),
            jax.ShapeDtypeStruct((1, dim), F32),
            jax.ShapeDtypeStruct((1, dim), F32),
        ],
        in_specs=[spec] * 4 + [row],
        out_specs=[spec, spec, row, row],
        compiler_params=params(24),
        cost_estimate=cost(True),
        name="norm_back",
    )(chip, far, x, base, gain)


def relu_of(idx, ref, weights):
    dim = weights.shape[0]
    kept = ref[:, dim : dim + 1].astype(F32) >= idx[5].astype(F32)
    return jnp.where(kept, jnp.maximum(nn(ref[:, :dim], weights), 0.0), 0.0)


def feed_kernel(with_act, with_back, idx, mine_ref, other_ref, w_ref, gact_ref, *refs):
    half = mine_ref.shape[0]
    weights = w_ref[...]
    act_ref = refs[0] if with_act else None
    du_ref = refs[1 if with_act else 0]
    for at, ref in ((0, mine_ref), (half, other_ref)):
        rows = slice(at, at + half)
        relu = relu_of(idx, ref, weights)
        if with_act:
            act_ref[rows, :] = (relu * relu).astype(BF16)
        du_ref[rows, :] = (gact_ref[rows, :].astype(F32) * 2.0 * relu).astype(BF16)
    if with_back:
        keep_out, give_out, acc_ref = refs[2:]
        step = pl.program_id(0)

        @pl.when(step == 0)
        def _():
            acc_ref[...] = nt(du_ref[...], weights)

        @pl.when(step > 0)
        def _():
            acc_ref[...] += nt(du_ref[...], weights)

        @pl.when(step == pl.num_programs(0) - 1)
        def _():
            keep_out[...] = acc_ref[:half, :].astype(BF16)
            give_out[...] = acc_ref[half:, :].astype(BF16)


def feed_forward(idx, mine, other, w_up, gact, with_act, with_back):
    half, wide = mine.shape
    dim, hidden = w_up.shape
    tile = min(hidden, 512)
    tall = jax.ShapeDtypeStruct((2 * half, hidden), BF16)
    part = jax.ShapeDtypeStruct((half, dim), BF16)
    spec = pl.BlockSpec((2 * half, tile), lambda i, idx: (0, i))
    n_tall = 2 if with_act else 1
    return pl.pallas_call(
        functools.partial(feed_kernel, with_act, with_back),
        grid_spec=pltpu.PrefetchScalarGridSpec(
            num_scalar_prefetch=1,
            grid=(hidden // tile,),
            in_specs=[
                whole((half, wide)),
                whole((half, wide)),
                pl.BlockSpec((dim, tile), lambda i, idx: (0, i)),
                spec,
            ],
            out_specs=[spec] * n_tall + ([whole((half, dim))] * 2 if with_back else []),
            scratch_shapes=[pltpu.VMEM((2 * half, dim), F32)] if with_back else [],
        ),
        out_shape=[tall] * n_tall + ([part, part] if with_back else []),
        compiler_params=params(48),
        cost_estimate=cost(with_back),
        name="feed_own" if with_back else "feed_far",
    )(idx, mine, other, w_up, gact)


def feed_down_kernel(act_ref, w_ref, *refs):
    outs, acc_ref = refs[:4], refs[4]
    step = pl.program_id(0)

    @pl.when(step == 0)
    def _():
        acc_ref[...] = nn(act_ref[...], w_ref[...])

    @pl.when(step > 0)
    def _():
        acc_ref[...] += nn(act_ref[...], w_ref[...])

    @pl.when(step == pl.num_programs(0) - 1)
    def _():
        rows = outs[0].shape[0]
        for k, out in enumerate(outs):
            out[...] = acc_ref[k * rows : (k + 1) * rows, :].astype(BF16)


def feed_down(act, w_down):
    tok, hidden = act.shape
    dim = w_down.shape[1]
    tile = min(hidden, 1024)
    part = (tok // 4, dim)
    return pl.pallas_call(
        feed_down_kernel,
        grid=(hidden // tile,),
        out_shape=[jax.ShapeDtypeStruct(part, BF16)] * 4,
        in_specs=[
            pl.BlockSpec((tok, tile), lambda i: (0, i)),
            pl.BlockSpec((tile, dim), lambda i: (i, 0)),
        ],
        out_specs=[whole(part)] * 4,
        scratch_shapes=[pltpu.VMEM((tok, dim), F32)],
        compiler_params=params(40),
        cost_estimate=cost(False),
        name="feed_down",
    )(act, w_down)


def back_act_kernel(mine_ref, other_ref, w_ref, out_ref):
    half = mine_ref.shape[0]
    out_ref[:half, :] = nt(mine_ref[...], w_ref[...]).astype(BF16)
    out_ref[half:, :] = nt(other_ref[...], w_ref[...]).astype(BF16)


def back_act(mine, other, w_down):
    half, dim = mine.shape
    hidden = w_down.shape[0]
    tile = min(hidden, 512)
    return pl.pallas_call(
        back_act_kernel,
        grid=(hidden // tile,),
        out_shape=jax.ShapeDtypeStruct((2 * half, hidden), BF16),
        in_specs=[
            whole((half, dim)),
            whole((half, dim)),
            pl.BlockSpec((tile, dim), lambda i: (i, 0)),
        ],
        out_specs=pl.BlockSpec((2 * half, tile), lambda i: (0, i)),
        compiler_params=params(40),
        cost_estimate=cost(False),
        name="back_act",
    )(mine, other, w_down)


def product_kernel(idx, *refs):
    cols, near_ref, far_ref, out_ref, turn_ref = refs[:4], refs[4], refs[5], refs[6], refs[7]
    half = cols[0].shape[0]
    for k, ref in enumerate(cols):
        turn_ref[:, k * half : (k + 1) * half] = ref[...].astype(F32).T.astype(BF16)
    width = out_ref.shape[1]
    tile = min(width, 512)
    starts = [pl.multiple_of(idx[3 + j] * half, half) for j in range(2)]
    for at in range(0, width, tile):
        lanes = slice(at, at + tile)
        total = None
        for k in range(4):
            rows = (near_ref, far_ref)[k // 2][pl.ds(starts[k % 2], half), lanes]
            term = nn(turn_ref[:, k * half : (k + 1) * half], rows)
            total = term if total is None else total + term
        out_ref[:, lanes] = total.astype(BF16)


def product(idx, cols, near, far, dim):
    half = cols[0].shape[0]
    tok, width = near.shape
    block = dim // (2 * HEADS)
    spec = pl.BlockSpec((half, block), lambda k, idx: (0, 2 * k + idx[1]))
    return pl.pallas_call(
        product_kernel,
        grid_spec=pltpu.PrefetchScalarGridSpec(
            num_scalar_prefetch=1,
            grid=(HEADS,),
            in_specs=[spec] * 4 + [whole((tok, width))] * 2,
            out_specs=pl.BlockSpec((block, width), lambda k, idx: (k, 0)),
            scratch_shapes=[pltpu.VMEM((block, 4 * half), BF16)],
        ),
        out_shape=jax.ShapeDtypeStruct((HEADS * block, width), BF16),
        compiler_params=params(40),
        cost_estimate=cost(False),
        name="product",
    )(idx, *cols, near, far)


def head_product_kernel(idx, h_ref, *refs):
    pieces, (give_ref, keep_ref, turn_ref) = refs[:HEADS], refs[HEADS:]
    tok = pieces[0].shape[0]
    block = h_ref.shape[1] // 2

    @pl.when(pl.program_id(0) == 0)
    def _():
        for k in range(HEADS):
            turn_ref[:, k * tok : (k + 1) * tok] = pieces[k][...].astype(F32).T.astype(BF16)

    total = None
    for k in range(HEADS):
        rows = h_ref[pl.ds(pl.multiple_of((idx[0] ^ k) * tok, tok), tok), :]
        term = nn(turn_ref[:, k * tok : (k + 1) * tok], rows)
        total = term if total is None else total + term
    first, second = total[:, :block], total[:, block:]
    odd = idx[1] == 1
    give_ref[0] = jnp.where(odd, first, second).astype(BF16)
    keep_ref[0] = jnp.where(odd, second, first).astype(BF16)


def head_product(idx, h_all, pieces):
    rows, dim = h_all.shape
    block = dim // (2 * HEADS)
    out = jax.ShapeDtypeStruct((HEADS, 3 * HD, block), BF16)
    spec = pl.BlockSpec((1, 3 * HD, block), lambda k, idx: (k, 0, 0))
    return pl.pallas_call(
        head_product_kernel,
        grid_spec=pltpu.PrefetchScalarGridSpec(
            num_scalar_prefetch=1,
            grid=(HEADS,),
            in_specs=[pl.BlockSpec((rows, 2 * block), lambda k, idx: (0, idx[0] ^ k))]
            + [whole((rows // HEADS, 3 * HD))] * HEADS,
            out_specs=[spec, spec],
            scratch_shapes=[pltpu.VMEM((3 * HD, rows), BF16)],
        ),
        out_shape=[out, out],
        compiler_params=params(40),
        cost_estimate=cost(False),
        name="head_product",
    )(idx, h_all, *pieces)


def head_add_kernel(keep_ref, got_ref, after_ref, *outs):
    del after_ref
    for k, out in enumerate(outs):
        out[...] = (keep_ref[k].astype(F32) + got_ref[k].astype(F32)).astype(BF16)


def head_add(keep, got, after):
    return pl.pallas_call(
        head_add_kernel,
        out_shape=[jax.ShapeDtypeStruct(keep.shape[1:], BF16)] * HEADS,
        in_specs=[VMEM, VMEM, ANY],
        out_specs=[VMEM] * HEADS,
        compiler_params=params(24),
        cost_estimate=cost(False),
        name="head_add",
    )(keep, got, after)


def head_place_kernel(idx, *refs):
    pieces, out_ref = refs[:HEADS], refs[HEADS]
    for k, piece in enumerate(pieces):
        for s in range(3):
            out_ref[s, :, pl.ds(pl.multiple_of((idx[0] ^ k) * HD, HD), HD)] = (
                piece[s * HD : (s + 1) * HD, :].astype(F32).T
            )


def head_place(idx, pieces):
    rows, block = pieces[0].shape
    return pl.pallas_call(
        head_place_kernel,
        out_shape=jax.ShapeDtypeStruct((3, block, HEADS * HD), F32),
        in_specs=[SMEM] + [VMEM] * HEADS,
        out_specs=VMEM,
        compiler_params=params(24),
        cost_estimate=cost(False),
        name="head_place",
    )(idx, *pieces)


def project_back_kernel(idx, w_ref, *refs):
    pieces, (keep_ref, give_a_ref, give_b_ref, flat_ref, acc_ref) = refs[:HEADS], refs[HEADS:]
    half = keep_ref.shape[0]
    core = idx[2]
    step = pl.program_id(0)

    for s in range(3):

        @pl.when(step == s)
        def _(s=s):
            for k in range(HEADS):
                lanes = pl.ds(pl.multiple_of((idx[0] ^ k) * HD, HD), HD)
                flat_ref[:, lanes] = pieces[k][:, s * HD : (s + 1) * HD]

    @pl.when(step == 0)
    def _():
        acc_ref[...] = nt(flat_ref[...], w_ref[0])

    @pl.when(step > 0)
    def _():
        acc_ref[...] += nt(flat_ref[...], w_ref[0])

    @pl.when(step == 2)
    def _():
        part = half // 2
        for k, out in enumerate((give_a_ref, give_b_ref)):
            start = pl.multiple_of((1 - core) * half + k * part, part)
            out[...] = acc_ref[pl.ds(start, part), :].astype(BF16)
        keep_ref[...] = acc_ref[pl.ds(pl.multiple_of(core * half, half), half), :].astype(BF16)


def project_back(idx, w_qkv, pieces):
    tok = pieces[0].shape[0]
    _, dim, cols = w_qkv.shape
    return pl.pallas_call(
        project_back_kernel,
        grid_spec=pltpu.PrefetchScalarGridSpec(
            num_scalar_prefetch=1,
            grid=(3,),
            in_specs=[pl.BlockSpec((1, dim, cols), lambda s, idx: (s, 0, 0))]
            + [whole((tok, 3 * HD))] * HEADS,
            out_specs=[whole((tok // 2, dim))] + [whole((tok // 4, dim))] * 2,
            scratch_shapes=[pltpu.VMEM((tok, cols), BF16), pltpu.VMEM((tok, dim), F32)],
        ),
        out_shape=[jax.ShapeDtypeStruct((tok // 2, dim), BF16)]
        + [jax.ShapeDtypeStruct((tok // 4, dim), BF16)] * 2,
        compiler_params=params(40),
        cost_estimate=cost(True),
        name="project_back",
    )(idx, w_qkv, *pieces)


def join_kernel(idx, mine_ref, other_ref, out_ref):
    half = mine_ref.shape[0]
    core = idx[2]
    out_ref[pl.ds(pl.multiple_of(core * half, half), half), :] = mine_ref[...].astype(out_ref.dtype)
    out_ref[pl.ds(pl.multiple_of((1 - core) * half, half), half), :] = other_ref[...].astype(
        out_ref.dtype
    )


def join(idx, mine, other, dtype):
    half, dim = mine.shape
    return pl.pallas_call(
        join_kernel,
        out_shape=jax.ShapeDtypeStruct((2 * half, dim), dtype),
        in_specs=[SMEM, VMEM, VMEM],
        out_specs=VMEM,
        compiler_params=params(24),
        cost_estimate=cost(False),
        name="join",
    )(idx, mine, other)


def body(
    depth,
    layer_input,
    ln1_gain,
    ln1_bias,
    w_qkv,
    w_out,
    ln2_gain,
    ln2_bias,
    w_up,
    w_down,
    buckets,
    lengths,
    block_order,
    grad_out,
):
    tok, dim = layer_input.shape
    half = tok // 2
    scale = 1.0 / math.sqrt(HD)
    r, h, y, x, c = (lax.axis_index(a) for a in ("r", PLANE, "y") + TP)
    blk = lax.axis_index(BLK)
    tp = lax.axis_index(TP)
    idx_rows = jnp.stack([h, y, c, c, 1 - c]).astype(jnp.int32)
    idx = jnp.stack([h, y, c, jnp.zeros_like(c), jnp.ones_like(c), tp]).astype(jnp.int32)
    gains = [v.reshape(1, dim) for v in (ln1_gain, ln1_bias, ln2_gain, ln2_bias)]

    def half_of(values, which):
        return lax.dynamic_slice_in_dim(values, which * half, half, 0)

    def regroup(values):
        if depth == 1:
            return values
        rows = values.shape[0]
        split = values[:, :dim].reshape(rows, depth, HEADS, 2, dim // (2 * HEADS * depth))
        return split.transpose(0, 2, 3, 1, 4).reshape(rows, dim)

    def scatter(values):
        if depth > 1:
            split = values.reshape(HEADS, depth, -1, values.shape[1])
            values = split.transpose(1, 0, 2, 3).reshape(values.shape)
        return lax.psum_scatter(values, ("r",) + PLANE, scatter_dimension=0, tiled=True)

    starts = jnp.cumsum(lengths) - lengths

    def firsts_of(places):
        return jnp.max(jnp.where(starts <= places[..., None], starts, 0), axis=-1)

    inside = jnp.arange(half, dtype=jnp.int32)
    own_places = (
        lax.dynamic_slice_in_dim(block_order, 2 * blk, 2, 0)[:, None] * half + inside
    ).reshape(tok)
    cosine, sine = rotary_tables(own_places - firsts_of(own_places))

    def chip_sum(keep, give):
        return (keep.astype(F32) + swap(give, "c").astype(F32)).astype(BF16)

    grad_mine, grad_other = half_of(grad_out, c), half_of(grad_out, 1 - c)
    own_rows, *projected = project(idx, layer_input, gains[0], gains[1], cosine, sine, w_qkv)
    queries, near_kv = list(projected[:HEADS]), list(projected[HEADS:])
    near_kv = [near_kv[0]] + [plane_swap(near_kv[k], k) for k in range(1, HEADS)]
    *queries[1:], near_kv[2] = ordered(*queries[1:], near_kv[2])
    queries = [queries[0]] + [plane_swap(queries[k], k) for k in range(1, HEADS)]
    y_grad = swap(grad_mine, "y")

    relative = h ^ jnp.arange(HEADS, dtype=jnp.int32)
    group_order = lax.dynamic_index_in_dim(
        block_order.reshape(depth, HEADS, 2, 2), r, 0, keepdims=False
    )
    group_order = lax.dynamic_index_in_dim(group_order, y, 1, keepdims=False)
    chosen = relative[:, None] == jnp.arange(HEADS, dtype=jnp.int32)[None, :]
    query_at = jnp.sum(jnp.where(chosen[:, :, None], group_order[None], 0), axis=1).reshape(-1)
    query_places = query_at[:, None] * half + inside
    query_firsts = firsts_of(query_places)
    query_low = query_firsts[:, 0] // half
    query_full = jnp.minimum((query_firsts[:, -1] + half - 1) // half, query_at)
    block_count = block_order.shape[0]
    slots = jnp.argmax(
        block_order[None, :] == jnp.arange(block_count, dtype=jnp.int32)[:, None], axis=1
    ).astype(jnp.int32)
    slot_dev = slots // 2
    slot_plane = slot_dev // 2
    key_row = (
        jnp.where(slot_dev % 2 == y, 0, block_count // 2)
        + slot_plane // HEADS * (2 * HEADS)
        + ((slot_plane % HEADS) ^ h) * 2
        + slots % 2
    )
    group_cos, group_sin = rotary_tables((query_places - query_firsts).reshape(2 * HEADS * half))
    tables = (query_at, query_low, query_full, key_row, query_firsts.reshape(2 * HEADS, 1, half))

    grad_act = back_act(grad_mine, grad_other, w_down)
    far_first = swap(near_kv[0], "y")
    far_first, y_grad, grad_act, group_cos, group_sin, *near_kv[1:] = ordered(
        far_first, y_grad, grad_act, group_cos, group_sin, *near_kv[1:]
    )
    if depth == 1:
        keys_values = near_kv + [far_first, swap(jnp.concatenate(near_kv[1:]), "y")]
    else:
        near_all = lax.all_gather(jnp.concatenate(near_kv), "r", axis=0, tiled=True)
        keys_values = [near_all, swap(near_all, "y")]
    y_grad_other = swap(y_grad, "c")
    y_grad_other, *queries[1:], keys_values[-1] = ordered(
        y_grad_other, *queries[1:], keys_values[-1]
    )

    *attended, lse = attend(half, scale, tables, queries, keys_values)
    pieces = [attended[0]] + [plane_swap(attended[k], k) for k in range(1, HEADS)]
    flat, keep, give = out_project(idx, w_out, pieces)
    chip = chip_sum(keep, give)
    chip_far = swap(chip, "x")
    y_grad, flat = ordered(y_grad, flat)
    y_grad_act = back_act(y_grad, y_grad_other, w_down)
    y_grad_act, chip_far = ordered(y_grad_act, chip_far)

    own_rows, flat = ordered(own_rows, flat)
    h_all = lax.all_gather(own_rows, PLANE + ("c",), axis=0, tiled=True)
    y_flat = swap(flat, "y")
    y_flat, chip_far = ordered(y_flat, chip_far)
    my_buckets = half_of(buckets, c).reshape(half, 1)
    x_mid, h_mine = norm(
        half_of(layer_input, c), chip, chip_far, gains[2], gains[3], my_buckets
    )
    h_other = swap(h_mine, "c")
    y_h = swap(h_mine, "y")
    act, du, keep, give = feed_forward(
        idx, h_mine, h_other, w_up, grad_act, True, True
    )
    chip = chip_sum(keep, give)
    chip_far = swap(chip, "x")

    y_h_other = swap(y_h, "c")
    y_act, y_du = feed_forward(idx, y_h, y_h_other, w_up, y_grad_act, True, False)
    pair_grads = [regroup(v) for v in (grad_mine, grad_other, y_grad, y_grad_other)]
    down_sum = product(idx, pair_grads, act, y_act, dim)
    down_sum, h_all, chip_far = ordered(down_sum, h_all, chip_far)
    down_part = scatter(down_sum)

    grad_mid, dy_mine, gain_two_grad, bias_two_grad = norm_back(
        chip, chip_far, x_mid, grad_mine, gains[2]
    )
    dy_other = swap(dy_mine, "c")
    grads = list(out_back(idx, w_out, dy_mine, dy_other))
    grads = [grads[0]] + [plane_swap(grads[k], k) for k in range(1, HEADS)]

    y_dy = swap(dy_mine, "y")
    for_up, dy_other = ordered(h_mine, dy_other)
    up_sum = product(idx, [regroup(v) for v in (for_up, h_other, y_h, y_h_other)], du, y_du, dim)
    up_sum, y_dy, *grads[1:] = ordered(up_sum, y_dy, *grads[1:])
    y_dy_other = swap(y_dy, "c")

    *dq, near, far = attend_back(
        half, scale, tables, lse, queries, keys_values, attended, grads
    )
    got = swap(far, "y")

    for_feed, near = ordered(act, near)
    feed = list(feed_down(for_feed, w_down))
    wout_cols = [regroup(v) for v in (dy_mine, dy_other, y_dy, y_dy_other)]
    wout_cols[0], near = ordered(wout_cols[0], near)
    wout_sum = product(idx_rows, wout_cols, flat, y_flat, dim)
    wout_sum, down_part, feed[1], got = ordered(wout_sum, down_part, feed[1], got)
    if depth > 1:
        near = lax.psum_scatter(near, "r", scatter_dimension=0, tiled=True)
        got = lax.psum_scatter(got, "r", scatter_dimension=0, tiled=True)
    mixed = list(settle(near, got, group_cos, group_sin, dq))
    pieces = [mixed[0]] + [plane_swap(mixed[k], k) for k in range(1, HEADS)]
    feed_chip = [chip_sum(feed[k], feed[k + 2]) for k in range(2)]
    feed_far = [swap(v, "x") for v in feed_chip]

    head_give, head_keep = head_product(idx, regroup(h_all), mixed)
    wout_sum, up_sum, mixed[1] = ordered(wout_sum, up_sum, mixed[1])
    late_sum = jnp.concatenate([up_sum, wout_sum], axis=1)
    feed_far[0], feed_far[1], head_give, late_sum, *pieces[1:] = ordered(
        *feed_far, head_give, late_sum, *pieces[1:]
    )
    late_part = scatter(late_sum)
    keep, *gives = project_back(idx, w_qkv, pieces)
    chip = jnp.concatenate([swap(v, "c") for v in gives])
    chip = (keep.astype(F32) + chip.astype(F32)).astype(BF16)
    chip_far = swap(chip, "x")

    head_got = swap(head_give, "y")
    feed_chip, feed_far = jnp.concatenate(feed_chip), jnp.concatenate(feed_far)
    out_mine = (x_mid + (feed_chip.astype(F32) + feed_far.astype(F32))).astype(BF16)
    out_mine, chip = ordered(out_mine, chip)
    out_other = swap(out_mine, "c")
    out_other, chip_far = ordered(out_other, chip_far)
    layer_output = join(idx, out_mine, out_other, BF16)
    head_got, chip_far = ordered(head_got, chip_far)

    _, grad_low, gain_one_grad, bias_one_grad = norm_back(
        chip, chip_far, half_of(layer_input, c), grad_mid, gains[0]
    )
    head_sum = list(head_add(head_keep, head_got, grad_low))
    if depth > 1:
        head_sum = [lax.psum_scatter(v, "r", scatter_dimension=1, tiled=True) for v in head_sum]
    head_pieces = [head_sum[0]] + [plane_swap(head_sum[k], k) for k in range(1, HEADS)]
    grad_input = join(idx, grad_low, swap(grad_low, "c"), F32)

    counts = jnp.sum(
        (half_of(buckets, c)[:, None] == jnp.arange(NB, dtype=jnp.int32)[None, :]).astype(F32),
        axis=0,
    )
    sums = jnp.concatenate(
        [v.reshape(dim) for v in (gain_one_grad, bias_one_grad, gain_two_grad, bias_two_grad)]
        + [counts]
    )
    if depth > 1:
        sums = lax.psum(sums, "r")
    one, two, three = (plane_swap(sums, k) for k in range(1, HEADS))
    sums = (sums + one) + (two + three)
    sums = sums + swap(sums, "y")
    qkv_part = head_place(idx, head_pieces)
    sums, late_part, grad_input, layer_output, qkv_part = ordered(
        sums, late_part, grad_input, layer_output, qkv_part
    )
    hidden = w_up.shape[1]
    up_part, wout_part = late_part[:, :hidden], late_part[:, hidden:]
    sums = sums + swap(sums, "c")
    return (
        layer_output,
        grad_input,
        sums[:dim],
        sums[dim : 2 * dim],
        qkv_part,
        wout_part.astype(F32).T,
        sums[2 * dim : 3 * dim],
        sums[3 * dim : 4 * dim],
        up_part.astype(F32),
        down_part.astype(F32).T,
        sums[4 * dim :].astype(jnp.int32),
    )


def solution(mesh):
    depth = mesh.shape["blk"] // (2 * HEADS)
    fine = Mesh(mesh.devices.reshape(depth, 2, 2, 2, 2, 2), BLK + TP)
    return jax.shard_map(
        functools.partial(body, depth),
        mesh=fine,
        in_specs=(
            P(BLK, None),
            P(),
            P(),
            P(None, None, TP),
            P(TP, None),
            P(),
            P(),
            P(None, TP),
            P(TP, None),
            P(BLK),
            P(),
            P(),
            P(BLK, None),
        ),
        out_specs=(
            P(BLK, None),
            P(BLK, None),
            P(),
            P(),
            P(None, BLK, TP),
            P(TP, BLK),
            P(),
            P(),
            P(BLK, TP),
            P(TP, BLK),
            P(),
        ),
        check_vma=False,
    )
```

```python
import functools
import math

import jax
import jax.numpy as jnp
from jax import lax
from jax.experimental import pallas as pl
from jax.experimental.pallas import tpu as pltpu
from jax.sharding import Mesh
from jax.sharding import PartitionSpec as P

HD = 128
FF = 8192
NB = 4
HEADS = 4
EPSILON = 1e-05
ROPE_BASE = 10000.0
PLANE = ("hh", "hl")
LOG_E = math.log2(math.e)
HIDDEN = -1e30
GROUPS = (4, 2)
BLK = ("r", "hh", "hl", "y")
TP = ("x", "c")
F32 = jnp.float32
BF16 = jnp.bfloat16
SMEM = pl.BlockSpec(memory_space=pltpu.SMEM)
VMEM = pl.BlockSpec(memory_space=pltpu.VMEM)
ANY = pl.BlockSpec(memory_space=pl.ANY)


def swap(value, axis):
    return lax.ppermute(value, axis, [(0, 1), (1, 0)])


def plane_swap(value, k):
    return lax.ppermute(value, PLANE, [(i, i ^ k) for i in range(HEADS)])


def ordered(*values):
    return lax.optimization_barrier(values)


def nt(lhs, rhs):
    return lax.dot_general(lhs, rhs, (((1,), (1,)), ((), ())), preferred_element_type=F32)


def tn(lhs, rhs):
    return lax.dot_general(lhs, rhs, (((0,), (0,)), ((), ())), preferred_element_type=F32)


def nn(lhs, rhs):
    return lax.dot_general(lhs, rhs, (((1,), (0,)), ((), ())), preferred_element_type=F32)


def params(mib):
    return pltpu.CompilerParams(vmem_limit_bytes=60 * 2**20)


def cost(on_path):
    return pl.CostEstimate(flops=10**9 if on_path else 1, bytes_accessed=1, transcendentals=0)


def whole(shape):
    return pl.BlockSpec(shape, lambda *_: (0,) * len(shape))


def normalise(values):
    centre = values - jnp.mean(values, axis=-1, keepdims=True)
    inverse = lax.rsqrt(jnp.mean(centre * centre, axis=-1, keepdims=True) + EPSILON)
    return (centre * inverse, inverse)


def rotary_tables(positions):
    freqs = ROPE_BASE ** (-(jnp.arange(HD // 2, dtype=F32) * 2.0 / HD))
    angles = positions.astype(F32)[:, None] * freqs[None, :]
    cosine, sine = jnp.cos(angles), jnp.sin(angles)
    return (
        jnp.concatenate([cosine, cosine], axis=-1),
        jnp.concatenate([-sine, sine], axis=-1),
    )


def rotate(values, cosine, sine):
    return values * cosine + pltpu.roll(values, HD // 2, 1) * sine


def project_kernel(idx, x_ref, gain_ref, bias_ref, cos_ref, sin_ref, w_ref, *refs):
    part_ref, q_outs, kv_outs = refs[0], refs[1 : 1 + HEADS], refs[1 + HEADS : 1 + 2 * HEADS]
    h_ref = refs[1 + 2 * HEADS]
    step = pl.program_id(0)

    @pl.when(step == 0)
    def _():
        normed, _ = normalise(x_ref[...].astype(F32))
        h_ref[...] = (normed * gain_ref[...] + bias_ref[...]).astype(BF16)
        rows = part_ref.shape[0]
        part_ref[...] = h_ref[pl.ds(pl.multiple_of(idx[5] * rows, rows), rows), :]

    both = nn(h_ref[...], jnp.concatenate([w_ref[0], w_ref[1]], axis=1))
    cosine, sine = cos_ref[...], sin_ref[...]
    queries = rotate(both[:, :HD], cosine, sine).astype(BF16)
    keys = rotate(both[:, HD:], cosine, sine).astype(BF16)
    values = nn(h_ref[...], w_ref[2]).astype(BF16)
    for k in range(HEADS):

        @pl.when(step == k)
        def _(k=k):
            q_outs[k][...] = queries
            kv_outs[k][:, :HD] = keys
            kv_outs[k][:, HD:] = values


def project(idx, x, gain, bias, cosine, sine, w_qkv):
    tok, dim = x.shape
    return pl.pallas_call(
        project_kernel,
        grid_spec=pltpu.PrefetchScalarGridSpec(
            num_scalar_prefetch=1,
            grid=(HEADS,),
            in_specs=[
                whole((tok, dim)),
                whole((1, dim)),
                whole((1, dim)),
                whole((tok, HD)),
                whole((tok, HD)),
                pl.BlockSpec((3, dim, HD), lambda k, idx: (0, 0, idx[0] ^ k)),
            ],
            out_specs=[whole((tok // 4, dim))]
            + [whole((tok, HD))] * HEADS
            + [whole((tok, 2 * HD))] * HEADS,
            scratch_shapes=[pltpu.VMEM((tok, dim), BF16)],
        ),
        out_shape=[jax.ShapeDtypeStruct((tok // 4, dim), BF16)]
        + [jax.ShapeDtypeStruct((tok, HD), BF16)] * HEADS
        + [jax.ShapeDtypeStruct((tok, 2 * HD), BF16)] * HEADS,
        compiler_params=params(40),
        cost_estimate=cost(True),
        name="project",
    )(idx, x, gain, bias, cosine, sine, w_qkv)


def visible_of(tile, key_block, query_places, query_firsts):
    key_places = key_block * tile + lax.broadcasted_iota(jnp.int32, (tile, 1), 0)
    return (key_places <= query_places) & (key_places >= query_firsts)


def gather_refs(refs, whole_ref):
    at = 0
    for ref in refs:
        whole_ref[at : at + ref.shape[0], :] = ref[...]
        at += ref.shape[0]


def over_blocks(low, full, at, masked, group, state):
    state = lax.fori_loop(low, full, masked, state)
    for size in GROUPS:
        count = lax.div(at - full, size)
        start = full
        state = lax.fori_loop(
            0, count, lambda j, st, s=size, a=start: group(a + s * j, s, st), state
        )
        full = full + size * count
    return lax.fori_loop(full, at + 1, masked, state)


def attend_kernel(tile, scale, n_kv, at_ref, low_ref, full_ref, row_ref, first_ref, *refs):
    q_refs, kv_refs, refs = refs[:HEADS], refs[HEADS : HEADS + n_kv], refs[HEADS + n_kv :]
    outs, (lse_ref, q_all, kv_all) = refs[:HEADS], refs[HEADS:]
    gather_refs(q_refs, q_all)
    gather_refs(kv_refs, kv_all)
    lanes = lax.broadcasted_iota(jnp.int32, (1, tile), 1)
    per_out = outs[0].shape[0] // tile
    scale_two = scale * LOG_E

    def one_block(i, carry):
        rows = pl.ds(pl.multiple_of(i * tile, tile), tile)
        queries = q_all[rows, :]
        firsts = first_ref[i]
        places = at_ref[i] * tile + lanes

        def key_rows(b):
            return pl.ds(pl.multiple_of(row_ref[b] * tile, tile), tile)

        def absorb(state, scores, values):
            run_max, run_sum, run_acc = state
            new_max = run_max
            for part in scores:
                new_max = jnp.maximum(new_max, jnp.max(part, axis=0, keepdims=True))
            factor = jnp.exp2(run_max - new_max)
            new_sum = run_sum * factor
            new_acc = run_acc * factor
            for part, rows in zip(scores, values, strict=True):
                probs = jnp.exp2(part - new_max)
                new_sum = new_sum + jnp.sum(probs, axis=0, keepdims=True)
                new_acc = new_acc + tn(rows, probs.astype(BF16))
            return (new_max, new_sum, new_acc)

        def masked(b, state):
            krows = key_rows(b)
            scores = nt(kv_all[krows, :HD], queries) * scale_two
            scores = jnp.where(visible_of(tile, b, places, firsts), scores, HIDDEN)
            return absorb(state, [scores], [kv_all[krows, HD:]])

        def group(b, size, state):
            rows = [key_rows(b + k) for k in range(size)]
            scores = [nt(kv_all[k, :HD], queries) * scale_two for k in rows]
            return absorb(state, scores, [kv_all[k, HD:] for k in rows])

        run_max, run_sum, run_acc = over_blocks(
            low_ref[i],
            full_ref[i],
            at_ref[i],
            masked,
            group,
            (
                jnp.full((1, tile), HIDDEN / 10, F32),
                jnp.zeros((1, tile), F32),
                jnp.zeros((HD, tile), F32),
            ),
        )
        q_all[rows, :] = (run_acc / run_sum).T.astype(BF16)
        lse_ref[i] = run_max + jnp.log2(run_sum)
        return carry

    lax.fori_loop(0, HEADS * per_out, one_block, 0)
    for k, out in enumerate(outs):
        out[...] = q_all[k * per_out * tile : (k + 1) * per_out * tile, :]


def attend_back_kernel(
    tile,
    scale,
    n_kv,
    at_ref,
    low_ref,
    full_ref,
    row_ref,
    first_ref,
    lse_ref,
    *refs,
):
    q_refs, kv_refs, refs = refs[:HEADS], refs[HEADS : HEADS + n_kv], refs[HEADS + n_kv :]
    o_refs, do_refs, dq_refs = refs[:HEADS], refs[HEADS : 2 * HEADS], refs[2 * HEADS : 3 * HEADS]
    near_ref, far_ref, q_all, kv_all, do_all, dot_all, acc_ref = refs[3 * HEADS :]
    gather_refs(q_refs, q_all)
    gather_refs(kv_refs, kv_all)
    gather_refs(do_refs, do_all)
    acc_ref[...] = jnp.zeros_like(acc_ref)
    lanes = lax.broadcasted_iota(jnp.int32, (1, tile), 1)
    per_out = dq_refs[0].shape[0] // tile
    scale_two = scale * LOG_E
    for k in range(HEADS):
        for j in range(per_out):
            piece = slice(j * tile, (j + 1) * tile)
            products = do_refs[k][piece, :].astype(F32) * o_refs[k][piece, :].astype(F32)
            dot_all[k * per_out + j] = jnp.sum(products.T, axis=0, keepdims=True)

    def one_block(i, carry):
        rows = pl.ds(pl.multiple_of(i * tile, tile), tile)
        queries = q_all[rows, :]
        grads = do_all[rows, :]
        firsts = first_ref[i]
        places = at_ref[i] * tile + lanes
        log_sums = lse_ref[i]
        deltas = dot_all[i]

        def one(b, grad_q, hide):
            krows = pl.ds(pl.multiple_of(row_ref[b] * tile, tile), tile)
            keys = kv_all[krows, :HD]
            probs = jnp.exp2(nt(keys, queries) * scale_two - log_sums)
            if hide:
                probs = jnp.where(visible_of(tile, b, places, firsts), probs, 0.0)
            grad_probs = nt(kv_all[krows, HD:], grads)
            grad_scores = (probs * (grad_probs - deltas)).astype(BF16)
            acc_ref[krows, HD:] += nn(probs.astype(BF16), grads)
            acc_ref[krows, :HD] += nn(grad_scores, queries)
            return grad_q + tn(keys, grad_scores)

        def group(b, size, grad_q):
            for k in range(size):
                grad_q = one(b + k, grad_q, False)
            return grad_q

        grad_q = over_blocks(
            low_ref[i],
            full_ref[i],
            at_ref[i],
            lambda b, grad_q: one(b, grad_q, True),
            group,
            jnp.zeros((HD, tile), F32),
        )
        do_all[rows, :] = (grad_q * scale).T.astype(BF16)
        return carry

    lax.fori_loop(0, HEADS * per_out, one_block, 0)
    for k, out in enumerate(dq_refs):
        out[...] = do_all[k * per_out * tile : (k + 1) * per_out * tile, :]
    near = near_ref.shape[0]
    near_ref[:, :HD] = (acc_ref[:near, :HD] * scale).astype(BF16)
    near_ref[:, HD:] = acc_ref[:near, HD:].astype(BF16)
    far_ref[:, :HD] = (acc_ref[near:, :HD] * scale).astype(BF16)
    far_ref[:, HD:] = acc_ref[near:, HD:].astype(BF16)


def attend(tile, scale, tables, pieces, keys_values):
    rows = HEADS * pieces[0].shape[0]
    kv_rows = sum(a.shape[0] for a in keys_values)
    operands = pieces + keys_values
    return pl.pallas_call(
        functools.partial(attend_kernel, tile, scale, len(keys_values)),
        out_shape=[jax.ShapeDtypeStruct((rows // HEADS, HD), BF16)] * HEADS
        + [jax.ShapeDtypeStruct((rows // tile, 1, tile), F32)],
        in_specs=[SMEM] * 4 + [VMEM] * (1 + len(operands)),
        out_specs=[VMEM] * (HEADS + 1),
        scratch_shapes=[pltpu.VMEM((rows, HD), BF16), pltpu.VMEM((kv_rows, 2 * HD), BF16)],
        compiler_params=params(50),
        cost_estimate=cost(True),
        name="attend",
    )(*tables, *operands)


def attend_back(tile, scale, tables, lse, pieces, keys_values, outs, grads):
    rows = HEADS * pieces[0].shape[0]
    kv_rows = sum(a.shape[0] for a in keys_values)
    operands = pieces + keys_values + outs + grads
    return pl.pallas_call(
        functools.partial(attend_back_kernel, tile, scale, len(keys_values)),
        out_shape=[jax.ShapeDtypeStruct((rows // HEADS, HD), BF16)] * HEADS
        + [jax.ShapeDtypeStruct((kv_rows // 2, 2 * HD), BF16)] * 2,
        in_specs=[SMEM] * 4 + [VMEM] * (2 + len(operands)),
        out_specs=[VMEM] * (HEADS + 2),
        scratch_shapes=[
            pltpu.VMEM((rows, HD), BF16),
            pltpu.VMEM((kv_rows, 2 * HD), BF16),
            pltpu.VMEM((rows, HD), BF16),
            pltpu.VMEM((rows // tile, 1, tile), F32),
            pltpu.VMEM((kv_rows, 2 * HD), F32),
        ],
        compiler_params=params(56),
        cost_estimate=cost(True),
        name="attend_back",
    )(*tables, lse, *operands)


def settle_kernel(near_ref, got_ref, cos_ref, sin_ref, *refs):
    dq_refs, outs = refs[:HEADS], refs[HEADS:]
    total = near_ref[...].astype(F32) + got_ref[...].astype(F32)
    for k, out in enumerate(outs):

        @pl.when(pl.program_id(0) == k)
        def _(k=k, out=out):
            cosine, sine = cos_ref[...], -sin_ref[...]
            out[:, :HD] = rotate(dq_refs[k][...].astype(F32), cosine, sine).astype(BF16)
            out[:, HD : 2 * HD] = rotate(total[:, :HD], cosine, sine).astype(BF16)
            out[:, 2 * HD :] = total[:, HD:].astype(BF16)


def settle(near, got, cosine, sine, dq_pieces):
    rows = near.shape[0]
    tile = rows // HEADS
    spec = pl.BlockSpec((tile, 2 * HD), lambda k: (k, 0))
    table = pl.BlockSpec((tile, HD), lambda k: (k, 0))
    return pl.pallas_call(
        settle_kernel,
        grid=(HEADS,),
        out_shape=[jax.ShapeDtypeStruct((tile, 3 * HD), BF16)] * HEADS,
        in_specs=[spec, spec, table, table] + [whole((tile, HD))] * HEADS,
        out_specs=[whole((tile, 3 * HD))] * HEADS,
        compiler_params=params(24),
        cost_estimate=cost(True),
        name="settle",
    )(near, got, cosine, sine, *dq_pieces)


def out_project_kernel(idx, w_ref, *refs):
    pieces, (flat_ref, keep_ref, give_ref) = refs[:HEADS], refs[HEADS:]
    for k, piece in enumerate(pieces):
        flat_ref[:, pl.ds(pl.multiple_of((idx[0] ^ k) * HD, HD), HD)] = piece[...]
    half = keep_ref.shape[0]
    core = idx[2]
    mine = flat_ref[pl.ds(pl.multiple_of(core * half, half), half), :]
    other = flat_ref[pl.ds(pl.multiple_of((1 - core) * half, half), half), :]
    give_ref[...] = nn(other, w_ref[...]).astype(BF16)
    keep_ref[...] = nn(mine, w_ref[...]).astype(BF16)


def out_project(idx, w_out, pieces):
    cols, dim = w_out.shape
    tok = pieces[0].shape[0]
    half = jax.ShapeDtypeStruct((tok // 2, dim), BF16)
    return pl.pallas_call(
        out_project_kernel,
        out_shape=[jax.ShapeDtypeStruct((tok, cols), BF16), half, half],
        in_specs=[SMEM] + [VMEM] * (1 + HEADS),
        out_specs=[VMEM] * 3,
        compiler_params=params(40),
        cost_estimate=cost(True),
        name="out_project",
    )(idx, w_out, *pieces)


def out_back_kernel(idx, w_ref, mine_ref, other_ref, *outs):
    half = mine_ref.shape[0]
    core = idx[2]
    for k, out in enumerate(outs):
        weights = w_ref[pl.ds(pl.multiple_of((idx[0] ^ k) * HD, HD), HD), :]
        out[pl.ds(pl.multiple_of(core * half, half), half), :] = nt(mine_ref[...], weights).astype(BF16)
        out[pl.ds(pl.multiple_of((1 - core) * half, half), half), :] = nt(
            other_ref[...], weights
        ).astype(BF16)


def out_back(idx, w_out, mine, other):
    half, dim = mine.shape
    return pl.pallas_call(
        out_back_kernel,
        out_shape=[jax.ShapeDtypeStruct((2 * half, HD), BF16)] * HEADS,
        in_specs=[SMEM] + [VMEM] * 3,
        out_specs=[VMEM] * HEADS,
        compiler_params=params(40),
        cost_estimate=cost(True),
        name="out_back",
    )(idx, w_out, mine, other)


def norm_kernel(x_ref, chip_ref, far_ref, gain_ref, bias_ref, bucket_ref, sum_ref, out_ref):
    dim = x_ref.shape[1]
    total = x_ref[...].astype(F32) + (chip_ref[...].astype(F32) + far_ref[...].astype(F32))
    sum_ref[...] = total
    normed, _ = normalise(total)
    out_ref[:, :dim] = (normed * gain_ref[...] + bias_ref[...]).astype(BF16)
    out_ref[:, dim:] = jnp.broadcast_to(bucket_ref[...], (total.shape[0], HD)).astype(BF16)


def norm(x, chip, far, gain, bias, buckets):
    rows, dim = x.shape
    tile = rows // 4
    spec = pl.BlockSpec((tile, dim), lambda i: (i, 0))
    wide = pl.BlockSpec((tile, dim + HD), lambda i: (i, 0))
    return pl.pallas_call(
        norm_kernel,
        grid=(4,),
        out_shape=[
            jax.ShapeDtypeStruct((rows, dim), F32),
            jax.ShapeDtypeStruct((rows, dim + HD), BF16),
        ],
        in_specs=[spec, spec, spec, whole((1, dim)), whole((1, dim))]
        + [pl.BlockSpec((tile, 1), lambda i: (i, 0))],
        out_specs=[spec, wide],
        compiler_params=params(24),
        cost_estimate=cost(True),
        name="norm",
    )(x, chip, far, gain, bias, buckets)


def norm_back_kernel(chip_ref, far_ref, x_ref, base_ref, gain_ref, wide_ref, low_ref, dg_ref, db_ref):
    grad = chip_ref[...].astype(F32) + far_ref[...].astype(F32)
    normed, inverse = normalise(x_ref[...].astype(F32))
    scaled = grad * gain_ref[...]
    back = inverse * (
        scaled
        - jnp.mean(scaled, axis=-1, keepdims=True)
        - normed * jnp.mean(scaled * normed, axis=-1, keepdims=True)
    )
    total = base_ref[...].astype(F32) + back
    wide_ref[...] = total
    low_ref[...] = total.astype(BF16)

    @pl.when(pl.program_id(0) == 0)
    def _():
        dg_ref[...] = jnp.zeros_like(dg_ref)
        db_ref[...] = jnp.zeros_like(db_ref)

    dg_ref[...] += jnp.sum(grad * normed, axis=0, keepdims=True)
    db_ref[...] += jnp.sum(grad, axis=0, keepdims=True)


def norm_back(chip, far, x, base, gain):
    rows, dim = chip.shape
    tile = rows // 4
    spec = pl.BlockSpec((tile, dim), lambda i: (i, 0))
    row = whole((1, dim))
    return pl.pallas_call(
        norm_back_kernel,
        grid=(4,),
        out_shape=[
            jax.ShapeDtypeStruct((rows, dim), F32),
            jax.ShapeDtypeStruct((rows, dim), BF16),
            jax.ShapeDtypeStruct((1, dim), F32),
            jax.ShapeDtypeStruct((1, dim), F32),
        ],
        in_specs=[spec] * 4 + [row],
        out_specs=[spec, spec, row, row],
        compiler_params=params(24),
        cost_estimate=cost(True),
        name="norm_back",
    )(chip, far, x, base, gain)


def relu_of(idx, ref, weights):
    dim = weights.shape[0]
    kept = ref[:, dim : dim + 1].astype(F32) >= idx[5].astype(F32)
    return jnp.where(kept, jnp.maximum(nn(ref[:, :dim], weights), 0.0), 0.0)


def feed_kernel(with_act, with_back, idx, mine_ref, other_ref, w_ref, gact_ref, *refs):
    half = mine_ref.shape[0]
    weights = w_ref[...]
    act_ref = refs[0] if with_act else None
    du_ref = refs[1 if with_act else 0]
    for at, ref in ((0, mine_ref), (half, other_ref)):
        rows = slice(at, at + half)
        relu = relu_of(idx, ref, weights)
        if with_act:
            act_ref[rows, :] = (relu * relu).astype(BF16)
        du_ref[rows, :] = (gact_ref[rows, :].astype(F32) * 2.0 * relu).astype(BF16)
    if with_back:
        keep_out, give_out, acc_ref = refs[2:]
        step = pl.program_id(0)

        @pl.when(step == 0)
        def _():
            acc_ref[...] = nt(du_ref[...], weights)

        @pl.when(step > 0)
        def _():
            acc_ref[...] += nt(du_ref[...], weights)

        @pl.when(step == pl.num_programs(0) - 1)
        def _():
            keep_out[...] = acc_ref[:half, :].astype(BF16)
            give_out[...] = acc_ref[half:, :].astype(BF16)


def feed_forward(idx, mine, other, w_up, gact, with_act, with_back):
    half, wide = mine.shape
    dim, hidden = w_up.shape
    tile = min(hidden, 512)
    tall = jax.ShapeDtypeStruct((2 * half, hidden), BF16)
    part = jax.ShapeDtypeStruct((half, dim), BF16)
    spec = pl.BlockSpec((2 * half, tile), lambda i, idx: (0, i))
    n_tall = 2 if with_act else 1
    return pl.pallas_call(
        functools.partial(feed_kernel, with_act, with_back),
        grid_spec=pltpu.PrefetchScalarGridSpec(
            num_scalar_prefetch=1,
            grid=(hidden // tile,),
            in_specs=[
                whole((half, wide)),
                whole((half, wide)),
                pl.BlockSpec((dim, tile), lambda i, idx: (0, i)),
                spec,
            ],
            out_specs=[spec] * n_tall + ([whole((half, dim))] * 2 if with_back else []),
            scratch_shapes=[pltpu.VMEM((2 * half, dim), F32)] if with_back else [],
        ),
        out_shape=[tall] * n_tall + ([part, part] if with_back else []),
        compiler_params=params(48),
        cost_estimate=cost(with_back),
        name="feed_own" if with_back else "feed_far",
    )(idx, mine, other, w_up, gact)


def feed_down_kernel(act_ref, w_ref, *refs):
    outs, acc_ref = refs[:4], refs[4]
    step = pl.program_id(0)

    @pl.when(step == 0)
    def _():
        acc_ref[...] = nn(act_ref[...], w_ref[...])

    @pl.when(step > 0)
    def _():
        acc_ref[...] += nn(act_ref[...], w_ref[...])

    @pl.when(step == pl.num_programs(0) - 1)
    def _():
        rows = outs[0].shape[0]
        for k, out in enumerate(outs):
            out[...] = acc_ref[k * rows : (k + 1) * rows, :].astype(BF16)


def feed_down(act, w_down):
    tok, hidden = act.shape
    dim = w_down.shape[1]
    tile = min(hidden, 1024)
    part = (tok // 4, dim)
    return pl.pallas_call(
        feed_down_kernel,
        grid=(hidden // tile,),
        out_shape=[jax.ShapeDtypeStruct(part, BF16)] * 4,
        in_specs=[
            pl.BlockSpec((tok, tile), lambda i: (0, i)),
            pl.BlockSpec((tile, dim), lambda i: (i, 0)),
        ],
        out_specs=[whole(part)] * 4,
        scratch_shapes=[pltpu.VMEM((tok, dim), F32)],
        compiler_params=params(40),
        cost_estimate=cost(False),
        name="feed_down",
    )(act, w_down)


def back_act_kernel(mine_ref, other_ref, w_ref, out_ref):
    half = mine_ref.shape[0]
    out_ref[:half, :] = nt(mine_ref[...], w_ref[...]).astype(BF16)
    out_ref[half:, :] = nt(other_ref[...], w_ref[...]).astype(BF16)


def back_act(mine, other, w_down):
    half, dim = mine.shape
    hidden = w_down.shape[0]
    tile = min(hidden, 512)
    return pl.pallas_call(
        back_act_kernel,
        grid=(hidden // tile,),
        out_shape=jax.ShapeDtypeStruct((2 * half, hidden), BF16),
        in_specs=[
            whole((half, dim)),
            whole((half, dim)),
            pl.BlockSpec((tile, dim), lambda i: (i, 0)),
        ],
        out_specs=pl.BlockSpec((2 * half, tile), lambda i: (0, i)),
        compiler_params=params(40),
        cost_estimate=cost(False),
        name="back_act",
    )(mine, other, w_down)


def product_kernel(idx, *refs):
    cols, near_ref, far_ref, out_ref, turn_ref = refs[:4], refs[4], refs[5], refs[6], refs[7]
    half = cols[0].shape[0]
    for k, ref in enumerate(cols):
        turn_ref[:, k * half : (k + 1) * half] = ref[...].astype(F32).T.astype(BF16)
    width = out_ref.shape[1]
    tile = min(width, 512)
    starts = [pl.multiple_of(idx[3 + j] * half, half) for j in range(2)]
    for at in range(0, width, tile):
        lanes = slice(at, at + tile)
        total = None
        for k in range(4):
            rows = (near_ref, far_ref)[k // 2][pl.ds(starts[k % 2], half), lanes]
            term = nn(turn_ref[:, k * half : (k + 1) * half], rows)
            total = term if total is None else total + term
        out_ref[:, lanes] = total.astype(BF16)


def product(idx, cols, near, far, dim):
    half = cols[0].shape[0]
    tok, width = near.shape
    block = dim // (2 * HEADS)
    spec = pl.BlockSpec((half, block), lambda k, idx: (0, 2 * k + idx[1]))
    return pl.pallas_call(
        product_kernel,
        grid_spec=pltpu.PrefetchScalarGridSpec(
            num_scalar_prefetch=1,
            grid=(HEADS,),
            in_specs=[spec] * 4 + [whole((tok, width))] * 2,
            out_specs=pl.BlockSpec((block, width), lambda k, idx: (k, 0)),
            scratch_shapes=[pltpu.VMEM((block, 4 * half), BF16)],
        ),
        out_shape=jax.ShapeDtypeStruct((HEADS * block, width), BF16),
        compiler_params=params(40),
        cost_estimate=cost(False),
        name="product",
    )(idx, *cols, near, far)


def plane_product_kernel(idx, *refs):
    cols, near_ref, far_ref, outs, turn_ref = refs[:4], refs[4], refs[5], refs[6:10], refs[10]
    half = cols[0].shape[0]
    tok = 2 * half
    for k, ref in enumerate(cols):
        turn_ref[:, k * half : (k + 1) * half] = ref[...].astype(F32).T.astype(BF16)
    width = near_ref.shape[1]
    tile = min(width, 512)
    for k, out in enumerate(outs):

        @pl.when(pl.program_id(0) == k)
        def _(out=out):
            for at in range(0, width, tile):
                lanes = slice(at, at + tile)
                total = nn(turn_ref[:, :tok], near_ref[:, lanes])
                total = total + nn(turn_ref[:, tok:], far_ref[:, lanes])
                out[:, lanes] = total.astype(BF16)


def plane_product(idx, cols, near, far, dim):
    half = cols[0].shape[0]
    tok, width = near.shape
    block = dim // (2 * HEADS)

    def columns(k, idx):
        parity = jnp.where(k < 2, 1 - idx[1], idx[1])
        return (0, 2 * (2 * (k % 2) + (idx[0] & 1)) + parity)

    return pl.pallas_call(
        plane_product_kernel,
        grid_spec=pltpu.PrefetchScalarGridSpec(
            num_scalar_prefetch=1,
            grid=(4,),
            in_specs=[pl.BlockSpec((half, block), columns)] * 4 + [whole((tok, width))] * 2,
            out_specs=[whole((block, width))] * 4,
            scratch_shapes=[pltpu.VMEM((block, 2 * tok), BF16)],
        ),
        out_shape=[jax.ShapeDtypeStruct((block, width), BF16)] * 4,
        compiler_params=params(40),
        cost_estimate=cost(False),
        name="plane_product",
    )(idx, *cols, near, far)


def head_product_kernel(idx, h_ref, *refs):
    pieces, (give_ref, keep_ref, turn_ref) = refs[:HEADS], refs[HEADS:]
    tok = pieces[0].shape[0]
    block = h_ref.shape[1] // 2

    @pl.when(pl.program_id(0) == 0)
    def _():
        for k in range(HEADS):
            turn_ref[:, k * tok : (k + 1) * tok] = pieces[k][...].astype(F32).T.astype(BF16)

    total = None
    for k in range(HEADS):
        rows = h_ref[pl.ds(pl.multiple_of((idx[0] ^ k) * tok, tok), tok), :]
        term = nn(turn_ref[:, k * tok : (k + 1) * tok], rows)
        total = term if total is None else total + term
    first, second = total[:, :block], total[:, block:]
    odd = idx[1] == 1
    give_ref[0] = jnp.where(odd, first, second).astype(BF16)
    keep_ref[0] = jnp.where(odd, second, first).astype(BF16)


def head_product(idx, h_all, pieces):
    rows, dim = h_all.shape
    block = dim // (2 * HEADS)
    out = jax.ShapeDtypeStruct((HEADS, 3 * HD, block), BF16)
    spec = pl.BlockSpec((1, 3 * HD, block), lambda k, idx: (k, 0, 0))
    return pl.pallas_call(
        head_product_kernel,
        grid_spec=pltpu.PrefetchScalarGridSpec(
            num_scalar_prefetch=1,
            grid=(HEADS,),
            in_specs=[pl.BlockSpec((rows, 2 * block), lambda k, idx: (0, idx[0] ^ k))]
            + [whole((rows // HEADS, 3 * HD))] * HEADS,
            out_specs=[spec, spec],
            scratch_shapes=[pltpu.VMEM((3 * HD, rows), BF16)],
        ),
        out_shape=[out, out],
        compiler_params=params(40),
        cost_estimate=cost(False),
        name="head_product",
    )(idx, h_all, *pieces)


def head_add_kernel(keep_ref, got_ref, after_ref, *outs):
    del after_ref
    for k, out in enumerate(outs):
        out[...] = (keep_ref[k].astype(F32) + got_ref[k].astype(F32)).astype(BF16)


def head_add(keep, got, after):
    return pl.pallas_call(
        head_add_kernel,
        out_shape=[jax.ShapeDtypeStruct(keep.shape[1:], BF16)] * HEADS,
        in_specs=[VMEM, VMEM, ANY],
        out_specs=[VMEM] * HEADS,
        compiler_params=params(24),
        cost_estimate=cost(False),
        name="head_add",
    )(keep, got, after)


def head_place_kernel(idx, *refs):
    pieces, out_ref = refs[:HEADS], refs[HEADS]
    for k, piece in enumerate(pieces):
        for s in range(3):
            out_ref[s, :, pl.ds(pl.multiple_of((idx[0] ^ k) * HD, HD), HD)] = (
                piece[s * HD : (s + 1) * HD, :].astype(F32).T
            )


def head_place(idx, pieces):
    rows, block = pieces[0].shape
    return pl.pallas_call(
        head_place_kernel,
        out_shape=jax.ShapeDtypeStruct((3, block, HEADS * HD), F32),
        in_specs=[SMEM] + [VMEM] * HEADS,
        out_specs=VMEM,
        compiler_params=params(24),
        cost_estimate=cost(False),
        name="head_place",
    )(idx, *pieces)


def project_back_kernel(idx, w_ref, *refs):
    pieces, (keep_ref, give_a_ref, give_b_ref, flat_ref, acc_ref) = refs[:HEADS], refs[HEADS:]
    half = keep_ref.shape[0]
    core = idx[2]
    step = pl.program_id(0)

    for s in range(3):

        @pl.when(step == s)
        def _(s=s):
            for k in range(HEADS):
                lanes = pl.ds(pl.multiple_of((idx[0] ^ k) * HD, HD), HD)
                flat_ref[:, lanes] = pieces[k][:, s * HD : (s + 1) * HD]

    @pl.when(step == 0)
    def _():
        acc_ref[...] = nt(flat_ref[...], w_ref[0])

    @pl.when(step > 0)
    def _():
        acc_ref[...] += nt(flat_ref[...], w_ref[0])

    @pl.when(step == 2)
    def _():
        part = half // 2
        for k, out in enumerate((give_a_ref, give_b_ref)):
            start = pl.multiple_of((1 - core) * half + k * part, part)
            out[...] = acc_ref[pl.ds(start, part), :].astype(BF16)
        keep_ref[...] = acc_ref[pl.ds(pl.multiple_of(core * half, half), half), :].astype(BF16)


def project_back(idx, w_qkv, pieces):
    tok = pieces[0].shape[0]
    _, dim, cols = w_qkv.shape
    return pl.pallas_call(
        project_back_kernel,
        grid_spec=pltpu.PrefetchScalarGridSpec(
            num_scalar_prefetch=1,
            grid=(3,),
            in_specs=[pl.BlockSpec((1, dim, cols), lambda s, idx: (s, 0, 0))]
            + [whole((tok, 3 * HD))] * HEADS,
            out_specs=[whole((tok // 2, dim))] + [whole((tok // 4, dim))] * 2,
            scratch_shapes=[pltpu.VMEM((tok, cols), BF16), pltpu.VMEM((tok, dim), F32)],
        ),
        out_shape=[jax.ShapeDtypeStruct((tok // 2, dim), BF16)]
        + [jax.ShapeDtypeStruct((tok // 4, dim), BF16)] * 2,
        compiler_params=params(40),
        cost_estimate=cost(True),
        name="project_back",
    )(idx, w_qkv, *pieces)


def join_kernel(idx, mine_ref, other_ref, out_ref):
    half = mine_ref.shape[0]
    core = idx[2]
    out_ref[pl.ds(pl.multiple_of(core * half, half), half), :] = mine_ref[...].astype(out_ref.dtype)
    out_ref[pl.ds(pl.multiple_of((1 - core) * half, half), half), :] = other_ref[...].astype(
        out_ref.dtype
    )


def join(idx, mine, other, dtype):
    half, dim = mine.shape
    return pl.pallas_call(
        join_kernel,
        out_shape=jax.ShapeDtypeStruct((2 * half, dim), dtype),
        in_specs=[SMEM, VMEM, VMEM],
        out_specs=VMEM,
        compiler_params=params(24),
        cost_estimate=cost(False),
        name="join",
    )(idx, mine, other)


def body(
    depth,
    layer_input,
    ln1_gain,
    ln1_bias,
    w_qkv,
    w_out,
    ln2_gain,
    ln2_bias,
    w_up,
    w_down,
    buckets,
    lengths,
    block_order,
    grad_out,
):
    tok, dim = layer_input.shape
    half = tok // 2
    scale = 1.0 / math.sqrt(HD)
    r, h, y, x, c = (lax.axis_index(a) for a in ("r", PLANE, "y") + TP)
    blk = lax.axis_index(BLK)
    tp = lax.axis_index(TP)
    idx_rows = jnp.stack([h, y, c, c, 1 - c]).astype(jnp.int32)
    idx = jnp.stack([h, y, c, jnp.zeros_like(c), jnp.ones_like(c), tp]).astype(jnp.int32)
    gains = [v.reshape(1, dim) for v in (ln1_gain, ln1_bias, ln2_gain, ln2_bias)]

    def half_of(values, which):
        return lax.dynamic_slice_in_dim(values, which * half, half, 0)

    def regroup(values):
        if depth == 1:
            return values
        rows = values.shape[0]
        split = values[:, :dim].reshape(rows, depth, HEADS, 2, dim // (2 * HEADS * depth))
        return split.transpose(0, 2, 3, 1, 4).reshape(rows, dim)

    def scatter(values):
        if depth > 1:
            split = values.reshape(HEADS, depth, -1, values.shape[1])
            values = split.transpose(1, 0, 2, 3).reshape(values.shape)
        return lax.psum_scatter(values, ("r",) + PLANE, scatter_dimension=0, tiled=True)

    starts = jnp.cumsum(lengths) - lengths

    def firsts_of(places):
        return jnp.max(jnp.where(starts <= places[..., None], starts, 0), axis=-1)

    inside = jnp.arange(half, dtype=jnp.int32)
    own_places = (
        lax.dynamic_slice_in_dim(block_order, 2 * blk, 2, 0)[:, None] * half + inside
    ).reshape(tok)
    cosine, sine = rotary_tables(own_places - firsts_of(own_places))

    def half_scatter(values):
        if depth > 1:
            split = values.reshape(2, depth, -1, values.shape[1])
            values = split.transpose(1, 0, 2, 3).reshape(values.shape)
        return lax.psum_scatter(values, ("r", "hh"), scatter_dimension=0, tiled=True)

    def chip_sum(keep, give):
        return (keep.astype(F32) + swap(give, "c").astype(F32)).astype(BF16)

    grad_mine, grad_other = half_of(grad_out, c), half_of(grad_out, 1 - c)
    own_rows, *projected = project(idx, layer_input, gains[0], gains[1], cosine, sine, w_qkv)
    queries, near_kv = list(projected[:HEADS]), list(projected[HEADS:])
    z_grad = plane_swap(grad_mine, 1)
    z_grad, near_kv[1] = ordered(z_grad, near_kv[1])
    near_kv = [near_kv[0]] + [plane_swap(near_kv[k], k) for k in range(1, HEADS)]
    *queries[1:], near_kv[2] = ordered(*queries[1:], near_kv[2])
    queries = [queries[0]] + [plane_swap(queries[k], k) for k in range(1, HEADS)]
    y_grad = swap(grad_mine, "y")

    relative = h ^ jnp.arange(HEADS, dtype=jnp.int32)
    group_order = lax.dynamic_index_in_dim(
        block_order.reshape(depth, HEADS, 2, 2), r, 0, keepdims=False
    )
    group_order = lax.dynamic_index_in_dim(group_order, y, 1, keepdims=False)
    chosen = relative[:, None] == jnp.arange(HEADS, dtype=jnp.int32)[None, :]
    query_at = jnp.sum(jnp.where(chosen[:, :, None], group_order[None], 0), axis=1).reshape(-1)
    query_places = query_at[:, None] * half + inside
    query_firsts = firsts_of(query_places)
    query_low = query_firsts[:, 0] // half
    query_full = jnp.minimum((query_firsts[:, -1] + half - 1) // half, query_at)
    block_count = block_order.shape[0]
    slots = jnp.argmax(
        block_order[None, :] == jnp.arange(block_count, dtype=jnp.int32)[:, None], axis=1
    ).astype(jnp.int32)
    slot_dev = slots // 2
    slot_plane = slot_dev // 2
    key_row = (
        jnp.where(slot_dev % 2 == y, 0, block_count // 2)
        + slot_plane // HEADS * (2 * HEADS)
        + ((slot_plane % HEADS) ^ h) * 2
        + slots % 2
    )
    group_cos, group_sin = rotary_tables((query_places - query_firsts).reshape(2 * HEADS * half))
    tables = (query_at, query_low, query_full, key_row, query_firsts.reshape(2 * HEADS, 1, half))

    grad_act = back_act(grad_mine, grad_other, w_down)
    far_first = swap(near_kv[0], "y")
    far_first, y_grad, grad_act, group_cos, group_sin, *near_kv[1:] = ordered(
        far_first, y_grad, grad_act, group_cos, group_sin, *near_kv[1:]
    )
    if depth == 1:
        keys_values = near_kv + [far_first, swap(jnp.concatenate(near_kv[1:]), "y")]
    else:
        near_all = lax.all_gather(jnp.concatenate(near_kv), "r", axis=0, tiled=True)
        keys_values = [near_all, swap(near_all, "y")]
    y_grad_other = swap(y_grad, "c")
    y_grad_other, *queries[1:], keys_values[-1] = ordered(
        y_grad_other, *queries[1:], keys_values[-1]
    )

    *attended, lse = attend(half, scale, tables, queries, keys_values)
    pieces = [attended[0]] + [plane_swap(attended[k], k) for k in range(1, HEADS)]
    z_grad, lse = ordered(z_grad, lse)
    z_grad_other = swap(z_grad, "c")
    z_grad_other, *pieces[1:] = ordered(z_grad_other, *pieces[1:])
    flat, keep, give = out_project(idx, w_out, pieces)
    own_rows, flat = ordered(own_rows, flat)
    h_all = lax.all_gather(own_rows, PLANE + TP, axis=0, tiled=True)
    chip = chip_sum(keep, give)
    chip_far = swap(chip, "x")
    y_grad, flat = ordered(y_grad, flat)
    z_grad, flat = ordered(z_grad, flat)
    y_grad_act = back_act(y_grad, y_grad_other, w_down)
    z_grad_act = back_act(z_grad, z_grad_other, w_down)
    y_grad_act, z_grad_act, chip_far = ordered(y_grad_act, z_grad_act, chip_far)

    y_flat = swap(flat, "y")
    y_flat, chip_far = ordered(y_flat, chip_far)
    my_buckets = half_of(buckets, c).reshape(half, 1)
    x_mid, h_mine = norm(
        half_of(layer_input, c), chip, chip_far, gains[2], gains[3], my_buckets
    )
    h_other = swap(h_mine, "c")
    y_h = swap(h_mine, "y")
    act, du, keep, give = feed_forward(
        idx, h_mine, h_other, w_up, grad_act, True, True
    )
    chip = chip_sum(keep, give)
    chip_far = swap(chip, "x")

    for_plane, act = ordered(h_mine, act)
    z_h = plane_swap(for_plane, 1)

    y_h_other = swap(y_h, "c")
    y_act, y_du = feed_forward(idx, y_h, y_h_other, w_up, y_grad_act, True, False)
    pair_grads = [regroup(v) for v in (grad_mine, grad_other, y_grad, y_grad_other)]
    down_sum = product(idx, pair_grads, act, y_act, dim)
    down_sum, h_all, z_h, chip_far = ordered(down_sum, h_all, z_h, chip_far)
    down_part = scatter(down_sum)

    grad_mid, dy_mine, gain_two_grad, bias_two_grad = norm_back(
        chip, chip_far, x_mid, grad_mine, gains[2]
    )
    dy_other = swap(dy_mine, "c")
    z_h_other = swap(z_h, "c")
    grads = list(out_back(idx, w_out, dy_mine, dy_other))
    grads = [grads[0]] + [plane_swap(grads[k], k) for k in range(1, HEADS)]

    y_dy = swap(dy_mine, "y")
    z_h_other, dy_other = ordered(z_h_other, dy_other)
    (z_du,) = feed_forward(idx, z_h, z_h_other, w_up, z_grad_act, False, False)
    plane_rows = [regroup(v) for v in (h_mine, h_other, z_h, z_h_other)]
    *up_give, up_keep, up_last = plane_product(idx, plane_rows, du, z_du, dim)
    up_give[0], y_dy, *grads[1:] = ordered(up_give[0], y_dy, *grads[1:])
    up_got = [swap(up_give[0], "y")]
    y_dy_other = swap(y_dy, "c")

    *dq, near, far = attend_back(
        half, scale, tables, lse, queries, keys_values, attended, grads
    )
    far, up_got[0] = ordered(far, up_got[0])
    got = swap(far, "y")

    for_feed, near = ordered(act, near)
    feed = list(feed_down(for_feed, w_down))
    wout_cols = [regroup(v) for v in (dy_mine, dy_other, y_dy, y_dy_other)]
    wout_cols[0], near = ordered(wout_cols[0], near)
    wout_sum = product(idx_rows, wout_cols, flat, y_flat, dim)
    wout_sum, down_part, feed[1], got = ordered(wout_sum, down_part, feed[1], got)
    if depth > 1:
        near = lax.psum_scatter(near, "r", scatter_dimension=0, tiled=True)
        got = lax.psum_scatter(got, "r", scatter_dimension=0, tiled=True)
    mixed = list(settle(near, got, group_cos, group_sin, dq))
    pieces = [mixed[0]] + [plane_swap(mixed[k], k) for k in range(1, HEADS)]
    feed_chip = [chip_sum(feed[k], feed[k + 2]) for k in range(2)]
    feed_far = [swap(v, "x") for v in feed_chip]

    head_give, head_keep = head_product(idx, regroup(h_all), mixed)
    up_give[1], mixed[2] = ordered(up_give[1], mixed[2])
    up_got.append(swap(up_give[1], "y"))
    feed_far[0], feed_far[1], head_give, wout_sum, up_got[1], *pieces[1:] = ordered(
        *feed_far, head_give, wout_sum, up_got[1], *pieces[1:]
    )
    up_sum = [
        (mine.astype(F32) + got.astype(F32)).astype(BF16)
        for mine, got in zip((up_keep, up_last), up_got, strict=True)
    ]
    up_part = half_scatter(jnp.concatenate(up_sum))
    keep, *gives = project_back(idx, w_qkv, pieces)
    chip = jnp.concatenate([swap(v, "c") for v in gives])
    chip = (keep.astype(F32) + chip.astype(F32)).astype(BF16)
    chip_far = swap(chip, "x")

    head_got = swap(head_give, "y")
    feed_chip, feed_far = jnp.concatenate(feed_chip), jnp.concatenate(feed_far)
    out_mine = (x_mid + (feed_chip.astype(F32) + feed_far.astype(F32))).astype(BF16)
    out_mine, wout_sum, chip = ordered(out_mine, wout_sum, chip)
    wout_part = scatter(wout_sum)
    out_other = swap(out_mine, "c")
    out_other, chip_far = ordered(out_other, chip_far)
    layer_output = join(idx, out_mine, out_other, BF16)
    head_got, chip_far = ordered(head_got, chip_far)

    _, grad_low, gain_one_grad, bias_one_grad = norm_back(
        chip, chip_far, half_of(layer_input, c), grad_mid, gains[0]
    )
    head_sum = list(head_add(head_keep, head_got, grad_low))
    if depth > 1:
        head_sum = [lax.psum_scatter(v, "r", scatter_dimension=1, tiled=True) for v in head_sum]
    head_pieces = [head_sum[0]] + [plane_swap(head_sum[k], k) for k in range(1, HEADS)]
    grad_input = join(idx, grad_low, swap(grad_low, "c"), F32)

    counts = jnp.sum(
        (half_of(buckets, c)[:, None] == jnp.arange(NB, dtype=jnp.int32)[None, :]).astype(F32),
        axis=0,
    )
    sums = jnp.concatenate(
        [v.reshape(dim) for v in (gain_one_grad, bias_one_grad, gain_two_grad, bias_two_grad)]
        + [counts]
    )
    if depth > 1:
        sums = lax.psum(sums, "r")
    one, two, three = (plane_swap(sums, k) for k in range(1, HEADS))
    sums = (sums + one) + (two + three)
    sums = sums + swap(sums, "y")
    qkv_part = head_place(idx, head_pieces)
    sums, up_part, grad_input, layer_output, qkv_part = ordered(
        sums, up_part, grad_input, layer_output, qkv_part
    )
    sums = sums + swap(sums, "c")
    return (
        layer_output,
        grad_input,
        sums[:dim],
        sums[dim : 2 * dim],
        qkv_part,
        wout_part.astype(F32).T,
        sums[2 * dim : 3 * dim],
        sums[3 * dim : 4 * dim],
        up_part.astype(F32),
        down_part.astype(F32).T,
        sums[4 * dim :].astype(jnp.int32),
    )


def solution(mesh):
    depth = mesh.shape["blk"] // (2 * HEADS)
    fine = Mesh(mesh.devices.reshape(depth, 2, 2, 2, 2, 2), BLK + TP)
    return jax.shard_map(
        functools.partial(body, depth),
        mesh=fine,
        in_specs=(
            P(BLK, None),
            P(),
            P(),
            P(None, None, TP),
            P(TP, None),
            P(),
            P(),
            P(None, TP),
            P(TP, None),
            P(BLK),
            P(),
            P(),
            P(BLK, None),
        ),
        out_specs=(
            P(BLK, None),
            P(BLK, None),
            P(),
            P(),
            P(None, BLK, TP),
            P(TP, BLK),
            P(),
            P(),
            P(BLK, TP),
            P(TP, BLK),
            P(),
        ),
        check_vma=False,
    )
```

```python
import functools
import math

import jax
import jax.numpy as jnp
from jax import lax
from jax.experimental import pallas as pl
from jax.experimental.pallas import tpu as pltpu
from jax.sharding import Mesh
from jax.sharding import PartitionSpec as P

HD = 128
FF = 8192
NB = 4
HEADS = 4
EPSILON = 1e-05
ROPE_BASE = 10000.0
PLANE = ("hh", "hl")
LOG_E = math.log2(math.e)
HIDDEN = -1e30
GROUPS = (4, 2)
BLK = ("r", "hh", "hl", "y")
TP = ("x", "c")
F32 = jnp.float32
BF16 = jnp.bfloat16
SMEM = pl.BlockSpec(memory_space=pltpu.SMEM)
VMEM = pl.BlockSpec(memory_space=pltpu.VMEM)
ANY = pl.BlockSpec(memory_space=pl.ANY)


def swap(value, axis):
    return lax.ppermute(value, axis, [(0, 1), (1, 0)])


def plane_swap(value, k):
    return lax.ppermute(value, PLANE, [(i, i ^ k) for i in range(HEADS)])


def ordered(*values):
    return lax.optimization_barrier(values)


def nt(lhs, rhs):
    return lax.dot_general(lhs, rhs, (((1,), (1,)), ((), ())), preferred_element_type=F32)


def tn(lhs, rhs):
    return lax.dot_general(lhs, rhs, (((0,), (0,)), ((), ())), preferred_element_type=F32)


def nn(lhs, rhs):
    return lax.dot_general(lhs, rhs, (((1,), (0,)), ((), ())), preferred_element_type=F32)


def params(mib):
    return pltpu.CompilerParams(vmem_limit_bytes=60 * 2**20)


def cost(on_path):
    return pl.CostEstimate(flops=10**9 if on_path else 1, bytes_accessed=1, transcendentals=0)


def whole(shape):
    return pl.BlockSpec(shape, lambda *_: (0,) * len(shape))


def normalise(values):
    centre = values - jnp.mean(values, axis=-1, keepdims=True)
    inverse = lax.rsqrt(jnp.mean(centre * centre, axis=-1, keepdims=True) + EPSILON)
    return (centre * inverse, inverse)


def rotary_tables(positions):
    freqs = ROPE_BASE ** (-(jnp.arange(HD // 2, dtype=F32) * 2.0 / HD))
    angles = positions.astype(F32)[:, None] * freqs[None, :]
    cosine, sine = jnp.cos(angles), jnp.sin(angles)
    return (
        jnp.concatenate([cosine, cosine], axis=-1),
        jnp.concatenate([-sine, sine], axis=-1),
    )


def rotate(values, cosine, sine):
    return values * cosine + pltpu.roll(values, HD // 2, 1) * sine


def project_kernel(idx, x_ref, gain_ref, bias_ref, cos_ref, sin_ref, w_ref, *refs):
    part_ref, q_outs, kv_outs = refs[0], refs[1 : 1 + HEADS], refs[1 + HEADS : 1 + 2 * HEADS]
    h_ref = refs[1 + 2 * HEADS]
    step = pl.program_id(0)

    @pl.when(step == 0)
    def _():
        normed, _ = normalise(x_ref[...].astype(F32))
        h_ref[...] = (normed * gain_ref[...] + bias_ref[...]).astype(BF16)
        rows = part_ref.shape[0]
        part_ref[...] = h_ref[pl.ds(pl.multiple_of(idx[5] * rows, rows), rows), :]

    both = nn(h_ref[...], jnp.concatenate([w_ref[0], w_ref[1]], axis=1))
    cosine, sine = cos_ref[...], sin_ref[...]
    queries = rotate(both[:, :HD], cosine, sine).astype(BF16)
    keys = rotate(both[:, HD:], cosine, sine).astype(BF16)
    values = nn(h_ref[...], w_ref[2]).astype(BF16)
    for k in range(HEADS):

        @pl.when(step == k)
        def _(k=k):
            q_outs[k][...] = queries
            kv_outs[k][:, :HD] = keys
            kv_outs[k][:, HD:] = values


def project(idx, x, gain, bias, cosine, sine, w_qkv):
    tok, dim = x.shape
    return pl.pallas_call(
        project_kernel,
        grid_spec=pltpu.PrefetchScalarGridSpec(
            num_scalar_prefetch=1,
            grid=(HEADS,),
            in_specs=[
                whole((tok, dim)),
                whole((1, dim)),
                whole((1, dim)),
                whole((tok, HD)),
                whole((tok, HD)),
                pl.BlockSpec((3, dim, HD), lambda k, idx: (0, 0, idx[0] ^ k)),
            ],
            out_specs=[whole((tok // 4, dim))]
            + [whole((tok, HD))] * HEADS
            + [whole((tok, 2 * HD))] * HEADS,
            scratch_shapes=[pltpu.VMEM((tok, dim), BF16)],
        ),
        out_shape=[jax.ShapeDtypeStruct((tok // 4, dim), BF16)]
        + [jax.ShapeDtypeStruct((tok, HD), BF16)] * HEADS
        + [jax.ShapeDtypeStruct((tok, 2 * HD), BF16)] * HEADS,
        compiler_params=params(40),
        cost_estimate=cost(True),
        name="project",
    )(idx, x, gain, bias, cosine, sine, w_qkv)


def visible_of(tile, key_block, query_places, query_firsts):
    key_places = key_block * tile + lax.broadcasted_iota(jnp.int32, (tile, 1), 0)
    return (key_places <= query_places) & (key_places >= query_firsts)


def gather_refs(refs, whole_ref):
    at = 0
    for ref in refs:
        whole_ref[at : at + ref.shape[0], :] = ref[...]
        at += ref.shape[0]


def over_blocks(low, full, at, masked, group, state):
    state = lax.fori_loop(low, full, masked, state)
    for size in GROUPS:
        count = lax.div(at - full, size)
        start = full
        state = lax.fori_loop(
            0, count, lambda j, st, s=size, a=start: group(a + s * j, s, st), state
        )
        full = full + size * count
    return lax.fori_loop(full, at + 1, masked, state)


def attend_kernel(tile, scale, n_kv, at_ref, low_ref, full_ref, row_ref, first_ref, *refs):
    q_refs, kv_refs, refs = refs[:HEADS], refs[HEADS : HEADS + n_kv], refs[HEADS + n_kv :]
    outs, (lse_ref, q_all, kv_all) = refs[:HEADS], refs[HEADS:]
    gather_refs(q_refs, q_all)
    gather_refs(kv_refs, kv_all)
    lanes = lax.broadcasted_iota(jnp.int32, (1, tile), 1)
    per_out = outs[0].shape[0] // tile
    scale_two = scale * LOG_E

    def one_block(i, carry):
        rows = pl.ds(pl.multiple_of(i * tile, tile), tile)
        queries = q_all[rows, :]
        firsts = first_ref[i]
        places = at_ref[i] * tile + lanes

        def key_rows(b):
            return pl.ds(pl.multiple_of(row_ref[b] * tile, tile), tile)

        def absorb(state, scores, values):
            run_max, run_sum, run_acc = state
            new_max = run_max
            for part in scores:
                new_max = jnp.maximum(new_max, jnp.max(part, axis=0, keepdims=True))
            factor = jnp.exp2(run_max - new_max)
            new_sum = run_sum * factor
            new_acc = run_acc * factor
            for part, rows in zip(scores, values, strict=True):
                probs = jnp.exp2(part - new_max)
                new_sum = new_sum + jnp.sum(probs, axis=0, keepdims=True)
                new_acc = new_acc + tn(rows, probs.astype(BF16))
            return (new_max, new_sum, new_acc)

        def masked(b, state):
            krows = key_rows(b)
            scores = nt(kv_all[krows, :HD], queries) * scale_two
            scores = jnp.where(visible_of(tile, b, places, firsts), scores, HIDDEN)
            return absorb(state, [scores], [kv_all[krows, HD:]])

        def group(b, size, state):
            rows = [key_rows(b + k) for k in range(size)]
            scores = [nt(kv_all[k, :HD], queries) * scale_two for k in rows]
            return absorb(state, scores, [kv_all[k, HD:] for k in rows])

        run_max, run_sum, run_acc = over_blocks(
            low_ref[i],
            full_ref[i],
            at_ref[i],
            masked,
            group,
            (
                jnp.full((1, tile), HIDDEN / 10, F32),
                jnp.zeros((1, tile), F32),
                jnp.zeros((HD, tile), F32),
            ),
        )
        q_all[rows, :] = (run_acc / run_sum).T.astype(BF16)
        lse_ref[i] = run_max + jnp.log2(run_sum)
        return carry

    lax.fori_loop(0, HEADS * per_out, one_block, 0)
    for k, out in enumerate(outs):
        out[...] = q_all[k * per_out * tile : (k + 1) * per_out * tile, :]


def attend_back_kernel(
    tile,
    scale,
    n_kv,
    at_ref,
    low_ref,
    full_ref,
    row_ref,
    first_ref,
    lse_ref,
    *refs,
):
    q_refs, kv_refs, refs = refs[:HEADS], refs[HEADS : HEADS + n_kv], refs[HEADS + n_kv :]
    o_refs, do_refs, dq_refs = refs[:HEADS], refs[HEADS : 2 * HEADS], refs[2 * HEADS : 3 * HEADS]
    near_ref, far_ref, q_all, kv_all, do_all, dot_all, acc_ref = refs[3 * HEADS :]
    gather_refs(q_refs, q_all)
    gather_refs(kv_refs, kv_all)
    gather_refs(do_refs, do_all)
    acc_ref[...] = jnp.zeros_like(acc_ref)
    lanes = lax.broadcasted_iota(jnp.int32, (1, tile), 1)
    per_out = dq_refs[0].shape[0] // tile
    scale_two = scale * LOG_E
    for k in range(HEADS):
        for j in range(per_out):
            piece = slice(j * tile, (j + 1) * tile)
            products = do_refs[k][piece, :].astype(F32) * o_refs[k][piece, :].astype(F32)
            dot_all[k * per_out + j] = jnp.sum(products.T, axis=0, keepdims=True)

    def one_block(i, carry):
        rows = pl.ds(pl.multiple_of(i * tile, tile), tile)
        queries = q_all[rows, :]
        grads = do_all[rows, :]
        firsts = first_ref[i]
        places = at_ref[i] * tile + lanes
        log_sums = lse_ref[i]
        deltas = dot_all[i]

        def one(b, grad_q, hide):
            krows = pl.ds(pl.multiple_of(row_ref[b] * tile, tile), tile)
            keys = kv_all[krows, :HD]
            probs = jnp.exp2(nt(keys, queries) * scale_two - log_sums)
            if hide:
                probs = jnp.where(visible_of(tile, b, places, firsts), probs, 0.0)
            grad_probs = nt(kv_all[krows, HD:], grads)
            grad_scores = (probs * (grad_probs - deltas)).astype(BF16)
            acc_ref[krows, HD:] += nn(probs.astype(BF16), grads)
            acc_ref[krows, :HD] += nn(grad_scores, queries)
            return grad_q + tn(keys, grad_scores)

        def group(b, size, grad_q):
            for k in range(size):
                grad_q = one(b + k, grad_q, False)
            return grad_q

        grad_q = over_blocks(
            low_ref[i],
            full_ref[i],
            at_ref[i],
            lambda b, grad_q: one(b, grad_q, True),
            group,
            jnp.zeros((HD, tile), F32),
        )
        do_all[rows, :] = (grad_q * scale).T.astype(BF16)
        return carry

    lax.fori_loop(0, HEADS * per_out, one_block, 0)
    for k, out in enumerate(dq_refs):
        out[...] = do_all[k * per_out * tile : (k + 1) * per_out * tile, :]
    near = near_ref.shape[0]
    near_ref[:, :HD] = (acc_ref[:near, :HD] * scale).astype(BF16)
    near_ref[:, HD:] = acc_ref[:near, HD:].astype(BF16)
    far_ref[:, :HD] = (acc_ref[near:, :HD] * scale).astype(BF16)
    far_ref[:, HD:] = acc_ref[near:, HD:].astype(BF16)


def attend(tile, scale, tables, pieces, keys_values):
    rows = HEADS * pieces[0].shape[0]
    kv_rows = sum(a.shape[0] for a in keys_values)
    operands = pieces + keys_values
    return pl.pallas_call(
        functools.partial(attend_kernel, tile, scale, len(keys_values)),
        out_shape=[jax.ShapeDtypeStruct((rows // HEADS, HD), BF16)] * HEADS
        + [jax.ShapeDtypeStruct((rows // tile, 1, tile), F32)],
        in_specs=[SMEM] * 4 + [VMEM] * (1 + len(operands)),
        out_specs=[VMEM] * (HEADS + 1),
        scratch_shapes=[pltpu.VMEM((rows, HD), BF16), pltpu.VMEM((kv_rows, 2 * HD), BF16)],
        compiler_params=params(50),
        cost_estimate=cost(True),
        name="attend",
    )(*tables, *operands)


def attend_back(tile, scale, tables, lse, pieces, keys_values, outs, grads):
    rows = HEADS * pieces[0].shape[0]
    kv_rows = sum(a.shape[0] for a in keys_values)
    operands = pieces + keys_values + outs + grads
    return pl.pallas_call(
        functools.partial(attend_back_kernel, tile, scale, len(keys_values)),
        out_shape=[jax.ShapeDtypeStruct((rows // HEADS, HD), BF16)] * HEADS
        + [jax.ShapeDtypeStruct((kv_rows // 2, 2 * HD), BF16)] * 2,
        in_specs=[SMEM] * 4 + [VMEM] * (2 + len(operands)),
        out_specs=[VMEM] * (HEADS + 2),
        scratch_shapes=[
            pltpu.VMEM((rows, HD), BF16),
            pltpu.VMEM((kv_rows, 2 * HD), BF16),
            pltpu.VMEM((rows, HD), BF16),
            pltpu.VMEM((rows // tile, 1, tile), F32),
            pltpu.VMEM((kv_rows, 2 * HD), F32),
        ],
        compiler_params=params(56),
        cost_estimate=cost(True),
        name="attend_back",
    )(*tables, lse, *operands)


def settle_kernel(near_ref, got_ref, cos_ref, sin_ref, *refs):
    dq_refs, outs = refs[:HEADS], refs[HEADS:]
    total = near_ref[...].astype(F32) + got_ref[...].astype(F32)
    for k, out in enumerate(outs):

        @pl.when(pl.program_id(0) == k)
        def _(k=k, out=out):
            cosine, sine = cos_ref[...], -sin_ref[...]
            out[:, :HD] = rotate(dq_refs[k][...].astype(F32), cosine, sine).astype(BF16)
            out[:, HD : 2 * HD] = rotate(total[:, :HD], cosine, sine).astype(BF16)
            out[:, 2 * HD :] = total[:, HD:].astype(BF16)


def settle(near, got, cosine, sine, dq_pieces):
    rows = near.shape[0]
    tile = rows // HEADS
    spec = pl.BlockSpec((tile, 2 * HD), lambda k: (k, 0))
    table = pl.BlockSpec((tile, HD), lambda k: (k, 0))
    return pl.pallas_call(
        settle_kernel,
        grid=(HEADS,),
        out_shape=[jax.ShapeDtypeStruct((tile, 3 * HD), BF16)] * HEADS,
        in_specs=[spec, spec, table, table] + [whole((tile, HD))] * HEADS,
        out_specs=[whole((tile, 3 * HD))] * HEADS,
        compiler_params=params(24),
        cost_estimate=cost(True),
        name="settle",
    )(near, got, cosine, sine, *dq_pieces)


def out_project_kernel(idx, w_ref, *refs):
    pieces, (flat_ref, keep_ref, give_ref) = refs[:HEADS], refs[HEADS:]
    for k, piece in enumerate(pieces):
        flat_ref[:, pl.ds(pl.multiple_of((idx[0] ^ k) * HD, HD), HD)] = piece[...]
    half = keep_ref.shape[0]
    core = idx[2]
    mine = flat_ref[pl.ds(pl.multiple_of(core * half, half), half), :]
    other = flat_ref[pl.ds(pl.multiple_of((1 - core) * half, half), half), :]
    give_ref[...] = nn(other, w_ref[...]).astype(BF16)
    keep_ref[...] = nn(mine, w_ref[...]).astype(BF16)


def out_project(idx, w_out, pieces):
    cols, dim = w_out.shape
    tok = pieces[0].shape[0]
    half = jax.ShapeDtypeStruct((tok // 2, dim), BF16)
    return pl.pallas_call(
        out_project_kernel,
        out_shape=[jax.ShapeDtypeStruct((tok, cols), BF16), half, half],
        in_specs=[SMEM] + [VMEM] * (1 + HEADS),
        out_specs=[VMEM] * 3,
        compiler_params=params(40),
        cost_estimate=cost(True),
        name="out_project",
    )(idx, w_out, *pieces)


def out_back_kernel(idx, w_ref, mine_ref, other_ref, *outs):
    half = mine_ref.shape[0]
    core = idx[2]
    for k, out in enumerate(outs):
        weights = w_ref[pl.ds(pl.multiple_of((idx[0] ^ k) * HD, HD), HD), :]
        out[pl.ds(pl.multiple_of(core * half, half), half), :] = nt(mine_ref[...], weights).astype(BF16)
        out[pl.ds(pl.multiple_of((1 - core) * half, half), half), :] = nt(
            other_ref[...], weights
        ).astype(BF16)


def out_back(idx, w_out, mine, other):
    half, dim = mine.shape
    return pl.pallas_call(
        out_back_kernel,
        out_shape=[jax.ShapeDtypeStruct((2 * half, HD), BF16)] * HEADS,
        in_specs=[SMEM] + [VMEM] * 3,
        out_specs=[VMEM] * HEADS,
        compiler_params=params(40),
        cost_estimate=cost(True),
        name="out_back",
    )(idx, w_out, mine, other)


def norm_kernel(x_ref, chip_ref, far_ref, gain_ref, bias_ref, bucket_ref, sum_ref, out_ref):
    dim = x_ref.shape[1]
    total = x_ref[...].astype(F32) + (chip_ref[...].astype(F32) + far_ref[...].astype(F32))
    sum_ref[...] = total
    normed, _ = normalise(total)
    out_ref[:, :dim] = (normed * gain_ref[...] + bias_ref[...]).astype(BF16)
    out_ref[:, dim:] = jnp.broadcast_to(bucket_ref[...], (total.shape[0], HD)).astype(BF16)


def norm(x, chip, far, gain, bias, buckets):
    rows, dim = x.shape
    tile = rows // 4
    spec = pl.BlockSpec((tile, dim), lambda i: (i, 0))
    wide = pl.BlockSpec((tile, dim + HD), lambda i: (i, 0))
    return pl.pallas_call(
        norm_kernel,
        grid=(4,),
        out_shape=[
            jax.ShapeDtypeStruct((rows, dim), F32),
            jax.ShapeDtypeStruct((rows, dim + HD), BF16),
        ],
        in_specs=[spec, spec, spec, whole((1, dim)), whole((1, dim))]
        + [pl.BlockSpec((tile, 1), lambda i: (i, 0))],
        out_specs=[spec, wide],
        compiler_params=params(24),
        cost_estimate=cost(True),
        name="norm",
    )(x, chip, far, gain, bias, buckets)


def norm_back_kernel(chip_ref, far_ref, x_ref, base_ref, gain_ref, wide_ref, low_ref, dg_ref, db_ref):
    grad = chip_ref[...].astype(F32) + far_ref[...].astype(F32)
    normed, inverse = normalise(x_ref[...].astype(F32))
    scaled = grad * gain_ref[...]
    back = inverse * (
        scaled
        - jnp.mean(scaled, axis=-1, keepdims=True)
        - normed * jnp.mean(scaled * normed, axis=-1, keepdims=True)
    )
    total = base_ref[...].astype(F32) + back
    wide_ref[...] = total
    low_ref[...] = total.astype(BF16)

    @pl.when(pl.program_id(0) == 0)
    def _():
        dg_ref[...] = jnp.zeros_like(dg_ref)
        db_ref[...] = jnp.zeros_like(db_ref)

    dg_ref[...] += jnp.sum(grad * normed, axis=0, keepdims=True)
    db_ref[...] += jnp.sum(grad, axis=0, keepdims=True)


def norm_back(chip, far, x, base, gain):
    rows, dim = chip.shape
    tile = rows // 4
    spec = pl.BlockSpec((tile, dim), lambda i: (i, 0))
    row = whole((1, dim))
    return pl.pallas_call(
        norm_back_kernel,
        grid=(4,),
        out_shape=[
            jax.ShapeDtypeStruct((rows, dim), F32),
            jax.ShapeDtypeStruct((rows, dim), BF16),
            jax.ShapeDtypeStruct((1, dim), F32),
            jax.ShapeDtypeStruct((1, dim), F32),
        ],
        in_specs=[spec] * 4 + [row],
        out_specs=[spec, spec, row, row],
        compiler_params=params(24),
        cost_estimate=cost(True),
        name="norm_back",
    )(chip, far, x, base, gain)


def relu_of(idx, ref, weights):
    dim = weights.shape[0]
    kept = ref[:, dim : dim + 1].astype(F32) >= idx[5].astype(F32)
    return jnp.where(kept, jnp.maximum(nn(ref[:, :dim], weights), 0.0), 0.0)


def feed_kernel(with_act, with_back, idx, mine_ref, other_ref, w_ref, gact_ref, *refs):
    half = mine_ref.shape[0]
    weights = w_ref[...]
    act_ref = refs[0] if with_act else None
    du_ref = refs[1 if with_act else 0]
    for at, ref in ((0, mine_ref), (half, other_ref)):
        rows = slice(at, at + half)
        relu = relu_of(idx, ref, weights)
        if with_act:
            act_ref[rows, :] = (relu * relu).astype(BF16)
        du_ref[rows, :] = (gact_ref[rows, :].astype(F32) * 2.0 * relu).astype(BF16)
    if with_back:
        keep_out, give_out, acc_ref = refs[2:]
        step = pl.program_id(0)

        @pl.when(step == 0)
        def _():
            acc_ref[...] = nt(du_ref[...], weights)

        @pl.when(step > 0)
        def _():
            acc_ref[...] += nt(du_ref[...], weights)

        @pl.when(step == pl.num_programs(0) - 1)
        def _():
            keep_out[...] = acc_ref[:half, :].astype(BF16)
            give_out[...] = acc_ref[half:, :].astype(BF16)


def feed_forward(idx, mine, other, w_up, gact, with_act, with_back):
    half, wide = mine.shape
    dim, hidden = w_up.shape
    tile = min(hidden, 512)
    tall = jax.ShapeDtypeStruct((2 * half, hidden), BF16)
    part = jax.ShapeDtypeStruct((half, dim), BF16)
    spec = pl.BlockSpec((2 * half, tile), lambda i, idx: (0, i))
    n_tall = 2 if with_act else 1
    return pl.pallas_call(
        functools.partial(feed_kernel, with_act, with_back),
        grid_spec=pltpu.PrefetchScalarGridSpec(
            num_scalar_prefetch=1,
            grid=(hidden // tile,),
            in_specs=[
                whole((half, wide)),
                whole((half, wide)),
                pl.BlockSpec((dim, tile), lambda i, idx: (0, i)),
                spec,
            ],
            out_specs=[spec] * n_tall + ([whole((half, dim))] * 2 if with_back else []),
            scratch_shapes=[pltpu.VMEM((2 * half, dim), F32)] if with_back else [],
        ),
        out_shape=[tall] * n_tall + ([part, part] if with_back else []),
        compiler_params=params(48),
        cost_estimate=cost(with_back),
        name="feed_own" if with_back else "feed_far",
    )(idx, mine, other, w_up, gact)


def feed_down_kernel(act_ref, w_ref, *refs):
    outs, acc_ref = refs[:4], refs[4]
    step = pl.program_id(0)

    @pl.when(step == 0)
    def _():
        acc_ref[...] = nn(act_ref[...], w_ref[...])

    @pl.when(step > 0)
    def _():
        acc_ref[...] += nn(act_ref[...], w_ref[...])

    @pl.when(step == pl.num_programs(0) - 1)
    def _():
        rows = outs[0].shape[0]
        for k, out in enumerate(outs):
            out[...] = acc_ref[k * rows : (k + 1) * rows, :].astype(BF16)


def feed_down(act, w_down):
    tok, hidden = act.shape
    dim = w_down.shape[1]
    tile = min(hidden, 1024)
    part = (tok // 4, dim)
    return pl.pallas_call(
        feed_down_kernel,
        grid=(hidden // tile,),
        out_shape=[jax.ShapeDtypeStruct(part, BF16)] * 4,
        in_specs=[
            pl.BlockSpec((tok, tile), lambda i: (0, i)),
            pl.BlockSpec((tile, dim), lambda i: (i, 0)),
        ],
        out_specs=[whole(part)] * 4,
        scratch_shapes=[pltpu.VMEM((tok, dim), F32)],
        compiler_params=params(40),
        cost_estimate=cost(False),
        name="feed_down",
    )(act, w_down)


def back_act_kernel(mine_ref, other_ref, w_ref, out_ref):
    half = mine_ref.shape[0]
    out_ref[:half, :] = nt(mine_ref[...], w_ref[...]).astype(BF16)
    out_ref[half:, :] = nt(other_ref[...], w_ref[...]).astype(BF16)


def back_act(mine, other, w_down):
    half, dim = mine.shape
    hidden = w_down.shape[0]
    tile = min(hidden, 512)
    return pl.pallas_call(
        back_act_kernel,
        grid=(hidden // tile,),
        out_shape=jax.ShapeDtypeStruct((2 * half, hidden), BF16),
        in_specs=[
            whole((half, dim)),
            whole((half, dim)),
            pl.BlockSpec((tile, dim), lambda i: (i, 0)),
        ],
        out_specs=pl.BlockSpec((2 * half, tile), lambda i: (0, i)),
        compiler_params=params(40),
        cost_estimate=cost(False),
        name="back_act",
    )(mine, other, w_down)


def product_kernel(idx, *refs):
    cols, near_ref, far_ref, out_ref, turn_ref = refs[:16], refs[16], refs[17], refs[18], refs[19]
    half, block = cols[0].shape

    @pl.when(pl.program_id(0) == 0)
    def _():
        for k, ref in enumerate(cols):
            rows = slice(k // 4 * block, (k // 4 + 1) * block)
            turn_ref[rows, k % 4 * half : (k % 4 + 1) * half] = ref[...].astype(F32).T.astype(BF16)

    starts = [pl.multiple_of(idx[3 + j] * half, half) for j in range(2)]
    total = None
    for k in range(4):
        rows = (near_ref, far_ref)[k // 2][pl.ds(starts[k % 2], half), :]
        term = nn(turn_ref[:, k * half : (k + 1) * half], rows)
        total = term if total is None else total + term
    out_ref[...] = total.astype(BF16)


def product(idx, cols, near, far, dim):
    half = cols[0].shape[0]
    tok, width = near.shape
    block = dim // (2 * HEADS)
    tile = min(width, 512)

    def columns(b):
        return pl.BlockSpec((half, block), lambda i, idx: (0, 2 * b + idx[1]))

    rows = pl.BlockSpec((tok, tile), lambda i, idx: (0, i))
    return pl.pallas_call(
        product_kernel,
        grid_spec=pltpu.PrefetchScalarGridSpec(
            num_scalar_prefetch=1,
            grid=(width // tile,),
            in_specs=[columns(b) for b in range(HEADS) for _ in range(4)] + [rows] * 2,
            out_specs=pl.BlockSpec((HEADS * block, tile), lambda i, idx: (0, i)),
            scratch_shapes=[pltpu.VMEM((HEADS * block, 2 * tok), BF16)],
        ),
        out_shape=jax.ShapeDtypeStruct((HEADS * block, width), BF16),
        compiler_params=params(40),
        cost_estimate=cost(False),
        name="product",
    )(idx, *(list(cols) * HEADS), near, far)


def plane_product_kernel(idx, *refs):
    cols, near_ref, far_ref, outs, turn_ref = refs[:16], refs[16], refs[17], refs[18:22], refs[22]
    half, block = cols[0].shape
    tok = 2 * half

    @pl.when(pl.program_id(0) == 0)
    def _():
        for k, ref in enumerate(cols):
            rows = slice(k // 4 * block, (k // 4 + 1) * block)
            turn_ref[rows, k % 4 * half : (k % 4 + 1) * half] = ref[...].astype(F32).T.astype(BF16)

    total = nn(turn_ref[:, :tok], near_ref[...]) + nn(turn_ref[:, tok:], far_ref[...])
    for k, out in enumerate(outs):
        out[...] = total[k * block : (k + 1) * block].astype(BF16)


def plane_product(idx, cols, near, far, dim):
    half = cols[0].shape[0]
    tok, width = near.shape
    block = dim // (2 * HEADS)
    tile = min(width, 512)

    def columns(b):
        def at(i, idx):
            parity = 1 - idx[1] if b < 2 else idx[1]
            return (0, 2 * (2 * (b % 2) + (idx[0] & 1)) + parity)

        return pl.BlockSpec((half, block), at)

    rows = pl.BlockSpec((tok, tile), lambda i, idx: (0, i))
    return pl.pallas_call(
        plane_product_kernel,
        grid_spec=pltpu.PrefetchScalarGridSpec(
            num_scalar_prefetch=1,
            grid=(width // tile,),
            in_specs=[columns(b) for b in range(4) for _ in range(4)] + [rows] * 2,
            out_specs=[pl.BlockSpec((block, tile), lambda i, idx: (0, i))] * 4,
            scratch_shapes=[pltpu.VMEM((4 * block, 2 * tok), BF16)],
        ),
        out_shape=[jax.ShapeDtypeStruct((block, width), BF16)] * 4,
        compiler_params=params(40),
        cost_estimate=cost(False),
        name="plane_product",
    )(idx, *(list(cols) * 4), near, far)


def head_product_kernel(idx, h_ref, *refs):
    pieces, (give_ref, keep_ref, turn_ref) = refs[:HEADS], refs[HEADS:]
    tok = pieces[0].shape[0]
    block = h_ref.shape[1] // 2

    @pl.when(pl.program_id(0) == 0)
    def _():
        for k in range(HEADS):
            turn_ref[:, k * tok : (k + 1) * tok] = pieces[k][...].astype(F32).T.astype(BF16)

    total = None
    for k in range(HEADS):
        rows = h_ref[pl.ds(pl.multiple_of((idx[0] ^ k) * tok, tok), tok), :]
        term = nn(turn_ref[:, k * tok : (k + 1) * tok], rows)
        total = term if total is None else total + term
    first, second = total[:, :block], total[:, block:]
    odd = idx[1] == 1
    give_ref[0] = jnp.where(odd, first, second).astype(BF16)
    keep_ref[0] = jnp.where(odd, second, first).astype(BF16)


def head_product(idx, h_all, pieces):
    rows, dim = h_all.shape
    block = dim // (2 * HEADS)
    out = jax.ShapeDtypeStruct((HEADS, 3 * HD, block), BF16)
    spec = pl.BlockSpec((1, 3 * HD, block), lambda k, idx: (k, 0, 0))
    return pl.pallas_call(
        head_product_kernel,
        grid_spec=pltpu.PrefetchScalarGridSpec(
            num_scalar_prefetch=1,
            grid=(HEADS,),
            in_specs=[pl.BlockSpec((rows, 2 * block), lambda k, idx: (0, idx[0] ^ k))]
            + [whole((rows // HEADS, 3 * HD))] * HEADS,
            out_specs=[spec, spec],
            scratch_shapes=[pltpu.VMEM((3 * HD, rows), BF16)],
        ),
        out_shape=[out, out],
        compiler_params=params(40),
        cost_estimate=cost(False),
        name="head_product",
    )(idx, h_all, *pieces)


def head_add_kernel(keep_ref, got_ref, after_ref, *outs):
    del after_ref
    for k, out in enumerate(outs):
        out[...] = (keep_ref[k].astype(F32) + got_ref[k].astype(F32)).astype(BF16)


def head_add(keep, got, after):
    return pl.pallas_call(
        head_add_kernel,
        out_shape=[jax.ShapeDtypeStruct(keep.shape[1:], BF16)] * HEADS,
        in_specs=[VMEM, VMEM, ANY],
        out_specs=[VMEM] * HEADS,
        compiler_params=params(24),
        cost_estimate=cost(False),
        name="head_add",
    )(keep, got, after)


def head_place_kernel(idx, *refs):
    pieces, out_ref = refs[:HEADS], refs[HEADS]
    for k, piece in enumerate(pieces):
        for s in range(3):
            out_ref[s, :, pl.ds(pl.multiple_of((idx[0] ^ k) * HD, HD), HD)] = (
                piece[s * HD : (s + 1) * HD, :].astype(F32).T
            )


def head_place(idx, pieces):
    rows, block = pieces[0].shape
    return pl.pallas_call(
        head_place_kernel,
        out_shape=jax.ShapeDtypeStruct((3, block, HEADS * HD), F32),
        in_specs=[SMEM] + [VMEM] * HEADS,
        out_specs=VMEM,
        compiler_params=params(24),
        cost_estimate=cost(False),
        name="head_place",
    )(idx, *pieces)


def project_back_kernel(idx, w_ref, *refs):
    pieces, (keep_ref, give_a_ref, give_b_ref, flat_ref, acc_ref) = refs[:HEADS], refs[HEADS:]
    half = keep_ref.shape[0]
    core = idx[2]
    step = pl.program_id(0)

    for s in range(3):

        @pl.when(step == s)
        def _(s=s):
            for k in range(HEADS):
                lanes = pl.ds(pl.multiple_of((idx[0] ^ k) * HD, HD), HD)
                flat_ref[:, lanes] = pieces[k][:, s * HD : (s + 1) * HD]

    @pl.when(step == 0)
    def _():
        acc_ref[...] = nt(flat_ref[...], w_ref[0])

    @pl.when(step > 0)
    def _():
        acc_ref[...] += nt(flat_ref[...], w_ref[0])

    @pl.when(step == 2)
    def _():
        part = half // 2
        for k, out in enumerate((give_a_ref, give_b_ref)):
            start = pl.multiple_of((1 - core) * half + k * part, part)
            out[...] = acc_ref[pl.ds(start, part), :].astype(BF16)
        keep_ref[...] = acc_ref[pl.ds(pl.multiple_of(core * half, half), half), :].astype(BF16)


def project_back(idx, w_qkv, pieces):
    tok = pieces[0].shape[0]
    _, dim, cols = w_qkv.shape
    return pl.pallas_call(
        project_back_kernel,
        grid_spec=pltpu.PrefetchScalarGridSpec(
            num_scalar_prefetch=1,
            grid=(3,),
            in_specs=[pl.BlockSpec((1, dim, cols), lambda s, idx: (s, 0, 0))]
            + [whole((tok, 3 * HD))] * HEADS,
            out_specs=[whole((tok // 2, dim))] + [whole((tok // 4, dim))] * 2,
            scratch_shapes=[pltpu.VMEM((tok, cols), BF16), pltpu.VMEM((tok, dim), F32)],
        ),
        out_shape=[jax.ShapeDtypeStruct((tok // 2, dim), BF16)]
        + [jax.ShapeDtypeStruct((tok // 4, dim), BF16)] * 2,
        compiler_params=params(40),
        cost_estimate=cost(True),
        name="project_back",
    )(idx, w_qkv, *pieces)


def join_kernel(idx, mine_ref, other_ref, out_ref):
    half = mine_ref.shape[0]
    core = idx[2]
    out_ref[pl.ds(pl.multiple_of(core * half, half), half), :] = mine_ref[...].astype(out_ref.dtype)
    out_ref[pl.ds(pl.multiple_of((1 - core) * half, half), half), :] = other_ref[...].astype(
        out_ref.dtype
    )


def join(idx, mine, other, dtype):
    half, dim = mine.shape
    return pl.pallas_call(
        join_kernel,
        out_shape=jax.ShapeDtypeStruct((2 * half, dim), dtype),
        in_specs=[SMEM, VMEM, VMEM],
        out_specs=VMEM,
        compiler_params=params(24),
        cost_estimate=cost(False),
        name="join",
    )(idx, mine, other)


def body(
    depth,
    layer_input,
    ln1_gain,
    ln1_bias,
    w_qkv,
    w_out,
    ln2_gain,
    ln2_bias,
    w_up,
    w_down,
    buckets,
    lengths,
    block_order,
    grad_out,
):
    tok, dim = layer_input.shape
    half = tok // 2
    scale = 1.0 / math.sqrt(HD)
    r, h, y, x, c = (lax.axis_index(a) for a in ("r", PLANE, "y") + TP)
    blk = lax.axis_index(BLK)
    tp = lax.axis_index(TP)
    idx_rows = jnp.stack([h, y, c, c, 1 - c]).astype(jnp.int32)
    idx = jnp.stack([h, y, c, jnp.zeros_like(c), jnp.ones_like(c), tp]).astype(jnp.int32)
    gains = [v.reshape(1, dim) for v in (ln1_gain, ln1_bias, ln2_gain, ln2_bias)]

    def half_of(values, which):
        return lax.dynamic_slice_in_dim(values, which * half, half, 0)

    def regroup(values):
        if depth == 1:
            return values
        rows = values.shape[0]
        split = values[:, :dim].reshape(rows, depth, HEADS, 2, dim // (2 * HEADS * depth))
        return split.transpose(0, 2, 3, 1, 4).reshape(rows, dim)

    def scatter(values):
        if depth > 1:
            split = values.reshape(HEADS, depth, -1, values.shape[1])
            values = split.transpose(1, 0, 2, 3).reshape(values.shape)
        return lax.psum_scatter(values, ("r",) + PLANE, scatter_dimension=0, tiled=True)

    starts = jnp.cumsum(lengths) - lengths

    def firsts_of(places):
        return jnp.max(jnp.where(starts <= places[..., None], starts, 0), axis=-1)

    inside = jnp.arange(half, dtype=jnp.int32)
    own_places = (
        lax.dynamic_slice_in_dim(block_order, 2 * blk, 2, 0)[:, None] * half + inside
    ).reshape(tok)
    cosine, sine = rotary_tables(own_places - firsts_of(own_places))

    def half_scatter(values):
        if depth > 1:
            split = values.reshape(2, depth, -1, values.shape[1])
            values = split.transpose(1, 0, 2, 3).reshape(values.shape)
        return lax.psum_scatter(values, ("r", "hh"), scatter_dimension=0, tiled=True)

    def chip_sum(keep, give):
        return (keep.astype(F32) + swap(give, "c").astype(F32)).astype(BF16)

    grad_mine, grad_other = half_of(grad_out, c), half_of(grad_out, 1 - c)
    own_rows, *projected = project(idx, layer_input, gains[0], gains[1], cosine, sine, w_qkv)
    queries, near_kv = list(projected[:HEADS]), list(projected[HEADS:])
    z_grad = plane_swap(grad_mine, 1)
    z_grad, near_kv[1] = ordered(z_grad, near_kv[1])
    near_kv = [near_kv[0]] + [plane_swap(near_kv[k], k) for k in range(1, HEADS)]
    *queries[1:], near_kv[2] = ordered(*queries[1:], near_kv[2])
    queries = [queries[0]] + [plane_swap(queries[k], k) for k in range(1, HEADS)]
    y_grad = swap(grad_mine, "y")

    relative = h ^ jnp.arange(HEADS, dtype=jnp.int32)
    group_order = lax.dynamic_index_in_dim(
        block_order.reshape(depth, HEADS, 2, 2), r, 0, keepdims=False
    )
    group_order = lax.dynamic_index_in_dim(group_order, y, 1, keepdims=False)
    chosen = relative[:, None] == jnp.arange(HEADS, dtype=jnp.int32)[None, :]
    query_at = jnp.sum(jnp.where(chosen[:, :, None], group_order[None], 0), axis=1).reshape(-1)
    query_places = query_at[:, None] * half + inside
    query_firsts = firsts_of(query_places)
    query_low = query_firsts[:, 0] // half
    query_full = jnp.minimum((query_firsts[:, -1] + half - 1) // half, query_at)
    block_count = block_order.shape[0]
    slots = jnp.argmax(
        block_order[None, :] == jnp.arange(block_count, dtype=jnp.int32)[:, None], axis=1
    ).astype(jnp.int32)
    slot_dev = slots // 2
    slot_plane = slot_dev // 2
    key_row = (
        jnp.where(slot_dev % 2 == y, 0, block_count // 2)
        + slot_plane // HEADS * (2 * HEADS)
        + ((slot_plane % HEADS) ^ h) * 2
        + slots % 2
    )
    group_cos, group_sin = rotary_tables((query_places - query_firsts).reshape(2 * HEADS * half))
    tables = (query_at, query_low, query_full, key_row, query_firsts.reshape(2 * HEADS, 1, half))

    grad_act = back_act(grad_mine, grad_other, w_down)
    far_first = swap(near_kv[0], "y")
    far_first, y_grad, grad_act, group_cos, group_sin, *near_kv[1:] = ordered(
        far_first, y_grad, grad_act, group_cos, group_sin, *near_kv[1:]
    )
    if depth == 1:
        keys_values = near_kv + [far_first, swap(jnp.concatenate(near_kv[1:]), "y")]
    else:
        near_all = lax.all_gather(jnp.concatenate(near_kv), "r", axis=0, tiled=True)
        keys_values = [near_all, swap(near_all, "y")]
    y_grad_other = swap(y_grad, "c")
    y_grad_other, *queries[1:], keys_values[-1] = ordered(
        y_grad_other, *queries[1:], keys_values[-1]
    )

    *attended, lse = attend(half, scale, tables, queries, keys_values)
    pieces = [attended[0]] + [plane_swap(attended[k], k) for k in range(1, HEADS)]
    z_grad, lse = ordered(z_grad, lse)
    z_grad_other = swap(z_grad, "c")
    z_grad_other, *pieces[1:] = ordered(z_grad_other, *pieces[1:])
    own_rows, pieces[1] = ordered(own_rows, pieces[1])
    flat, keep, give = out_project(idx, w_out, pieces)
    h_all = lax.all_gather(own_rows, PLANE + TP, axis=0, tiled=True)
    chip = chip_sum(keep, give)
    chip_far = swap(chip, "x")
    y_grad, flat = ordered(y_grad, flat)
    z_grad, flat = ordered(z_grad, flat)
    y_grad_act = back_act(y_grad, y_grad_other, w_down)
    z_grad_act = back_act(z_grad, z_grad_other, w_down)
    y_grad_act, z_grad_act, chip_far = ordered(y_grad_act, z_grad_act, chip_far)

    y_flat = swap(flat, "y")
    y_flat, chip_far = ordered(y_flat, chip_far)
    my_buckets = half_of(buckets, c).reshape(half, 1)
    x_mid, h_mine = norm(
        half_of(layer_input, c), chip, chip_far, gains[2], gains[3], my_buckets
    )
    h_other = swap(h_mine, "c")
    y_h = swap(h_mine, "y")
    act, du, keep, give = feed_forward(
        idx, h_mine, h_other, w_up, grad_act, True, True
    )
    chip = chip_sum(keep, give)
    chip_far = swap(chip, "x")

    for_plane, act = ordered(h_mine, act)
    z_h = plane_swap(for_plane, 1)

    y_h_other = swap(y_h, "c")
    y_act, y_du = feed_forward(idx, y_h, y_h_other, w_up, y_grad_act, True, False)
    pair_grads = [regroup(v) for v in (grad_mine, grad_other, y_grad, y_grad_other)]
    down_sum = product(idx, pair_grads, act, y_act, dim)
    down_sum, h_all, z_h, chip_far = ordered(down_sum, h_all, z_h, chip_far)
    down_part = scatter(down_sum)

    grad_mid, dy_mine, gain_two_grad, bias_two_grad = norm_back(
        chip, chip_far, x_mid, grad_mine, gains[2]
    )
    dy_other = swap(dy_mine, "c")
    z_h_other = swap(z_h, "c")
    grads = list(out_back(idx, w_out, dy_mine, dy_other))
    grads = [grads[0]] + [plane_swap(grads[k], k) for k in range(1, HEADS)]

    y_dy = swap(dy_mine, "y")
    z_h_other, dy_other = ordered(z_h_other, dy_other)
    (z_du,) = feed_forward(idx, z_h, z_h_other, w_up, z_grad_act, False, False)
    plane_rows = [regroup(v) for v in (h_mine, h_other, z_h, z_h_other)]
    *up_give, up_keep, up_last = plane_product(idx, plane_rows, du, z_du, dim)
    up_give[0], y_dy, *grads[1:] = ordered(up_give[0], y_dy, *grads[1:])
    up_got = [swap(up_give[0], "y")]
    y_dy_other = swap(y_dy, "c")

    *dq, near, far = attend_back(
        half, scale, tables, lse, queries, keys_values, attended, grads
    )
    got = swap(far, "y")

    for_feed, up_got[0], near = ordered(act, up_got[0], near)
    feed = list(feed_down(for_feed, w_down))
    wout_cols = [regroup(v) for v in (dy_mine, dy_other, y_dy, y_dy_other)]
    wout_cols[0], near = ordered(wout_cols[0], near)
    wout_sum = product(idx_rows, wout_cols, flat, y_flat, dim)
    wout_sum, down_part, feed[1], got = ordered(wout_sum, down_part, feed[1], got)
    if depth > 1:
        near = lax.psum_scatter(near, "r", scatter_dimension=0, tiled=True)
        got = lax.psum_scatter(got, "r", scatter_dimension=0, tiled=True)
    mixed = list(settle(near, got, group_cos, group_sin, dq))
    pieces = [mixed[0]] + [plane_swap(mixed[k], k) for k in range(1, HEADS)]
    feed_chip = [chip_sum(feed[k], feed[k + 2]) for k in range(2)]
    feed_far = [swap(v, "x") for v in feed_chip]

    head_give, head_keep = head_product(idx, regroup(h_all), mixed)
    up_give[1], mixed[2] = ordered(up_give[1], mixed[2])
    up_got.append(swap(up_give[1], "y"))
    feed_far[0], feed_far[1], head_give, wout_sum, up_got[1], *pieces[1:] = ordered(
        *feed_far, head_give, wout_sum, up_got[1], *pieces[1:]
    )
    up_sum = [
        (mine.astype(F32) + got.astype(F32)).astype(BF16)
        for mine, got in zip((up_keep, up_last), up_got, strict=True)
    ]
    up_part = half_scatter(jnp.concatenate(up_sum))
    keep, *gives = project_back(idx, w_qkv, pieces)
    chip = jnp.concatenate([swap(v, "c") for v in gives])
    chip = (keep.astype(F32) + chip.astype(F32)).astype(BF16)
    chip_far = swap(chip, "x")

    head_got = swap(head_give, "y")
    feed_chip, feed_far = jnp.concatenate(feed_chip), jnp.concatenate(feed_far)
    out_mine = (x_mid + (feed_chip.astype(F32) + feed_far.astype(F32))).astype(BF16)
    out_mine, wout_sum, chip = ordered(out_mine, wout_sum, chip)
    wout_part = scatter(wout_sum)
    out_other = swap(out_mine, "c")
    out_other, chip_far = ordered(out_other, chip_far)
    layer_output = join(idx, out_mine, out_other, BF16)
    head_got, chip_far = ordered(head_got, chip_far)

    _, grad_low, gain_one_grad, bias_one_grad = norm_back(
        chip, chip_far, half_of(layer_input, c), grad_mid, gains[0]
    )
    head_sum = list(head_add(head_keep, head_got, grad_low))
    if depth > 1:
        head_sum = [lax.psum_scatter(v, "r", scatter_dimension=1, tiled=True) for v in head_sum]
    head_pieces = [head_sum[0]] + [plane_swap(head_sum[k], k) for k in range(1, HEADS)]
    grad_input = join(idx, grad_low, swap(grad_low, "c"), F32)

    counts = jnp.sum(
        (half_of(buckets, c)[:, None] == jnp.arange(NB, dtype=jnp.int32)[None, :]).astype(F32),
        axis=0,
    )
    sums = jnp.concatenate(
        [v.reshape(dim) for v in (gain_one_grad, bias_one_grad, gain_two_grad, bias_two_grad)]
        + [counts]
    )
    if depth > 1:
        sums = lax.psum(sums, "r")
    one, two, three = (plane_swap(sums, k) for k in range(1, HEADS))
    sums = (sums + one) + (two + three)
    sums = sums + swap(sums, "y")
    qkv_part = head_place(idx, head_pieces)
    sums, up_part, grad_input, layer_output, qkv_part = ordered(
        sums, up_part, grad_input, layer_output, qkv_part
    )
    sums = sums + swap(sums, "c")
    return (
        layer_output,
        grad_input,
        sums[:dim],
        sums[dim : 2 * dim],
        qkv_part,
        wout_part.astype(F32).T,
        sums[2 * dim : 3 * dim],
        sums[3 * dim : 4 * dim],
        up_part.astype(F32),
        down_part.astype(F32).T,
        sums[4 * dim :].astype(jnp.int32),
    )


def solution(mesh):
    depth = mesh.shape["blk"] // (2 * HEADS)
    fine = Mesh(mesh.devices.reshape(depth, 2, 2, 2, 2, 2), BLK + TP)
    return jax.shard_map(
        functools.partial(body, depth),
        mesh=fine,
        in_specs=(
            P(BLK, None),
            P(),
            P(),
            P(None, None, TP),
            P(TP, None),
            P(),
            P(),
            P(None, TP),
            P(TP, None),
            P(BLK),
            P(),
            P(),
            P(BLK, None),
        ),
        out_specs=(
            P(BLK, None),
            P(BLK, None),
            P(),
            P(),
            P(None, BLK, TP),
            P(TP, BLK),
            P(),
            P(),
            P(BLK, TP),
            P(TP, BLK),
            P(),
        ),
        check_vma=False,
    )
```

```python
import functools
import math

import jax
import jax.numpy as jnp
from jax import lax
from jax.experimental import pallas as pl
from jax.experimental.pallas import tpu as pltpu
from jax.sharding import Mesh
from jax.sharding import PartitionSpec as P

HD = 128
FF = 8192
NB = 4
HEADS = 4
EPSILON = 1e-05
ROPE_BASE = 10000.0
PLANE = ("hh", "hl")
LOG_E = math.log2(math.e)
HIDDEN = -1e30
GROUPS = (4, 2)
BLK = ("r", "hh", "hl", "y")
TP = ("x", "c")
F32 = jnp.float32
BF16 = jnp.bfloat16
SMEM = pl.BlockSpec(memory_space=pltpu.SMEM)
VMEM = pl.BlockSpec(memory_space=pltpu.VMEM)
ANY = pl.BlockSpec(memory_space=pl.ANY)


def swap(value, axis):
    return lax.ppermute(value, axis, [(0, 1), (1, 0)])


def plane_swap(value, k):
    return lax.ppermute(value, PLANE, [(i, i ^ k) for i in range(HEADS)])


def ordered(*values):
    return lax.optimization_barrier(values)


def nt(lhs, rhs):
    return lax.dot_general(lhs, rhs, (((1,), (1,)), ((), ())), preferred_element_type=F32)


def tn(lhs, rhs):
    return lax.dot_general(lhs, rhs, (((0,), (0,)), ((), ())), preferred_element_type=F32)


def nn(lhs, rhs):
    return lax.dot_general(lhs, rhs, (((1,), (0,)), ((), ())), preferred_element_type=F32)


def params(mib):
    return pltpu.CompilerParams(vmem_limit_bytes=60 * 2**20)


def cost(on_path):
    return pl.CostEstimate(flops=10**9 if on_path else 1, bytes_accessed=1, transcendentals=0)


def whole(shape):
    return pl.BlockSpec(shape, lambda *_: (0,) * len(shape))


def normalise(values):
    centre = values - jnp.mean(values, axis=-1, keepdims=True)
    inverse = lax.rsqrt(jnp.mean(centre * centre, axis=-1, keepdims=True) + EPSILON)
    return (centre * inverse, inverse)


def rotary_tables(positions):
    freqs = ROPE_BASE ** (-(jnp.arange(HD // 2, dtype=F32) * 2.0 / HD))
    angles = positions.astype(F32)[:, None] * freqs[None, :]
    cosine, sine = jnp.cos(angles), jnp.sin(angles)
    return (
        jnp.concatenate([cosine, cosine], axis=-1),
        jnp.concatenate([-sine, sine], axis=-1),
    )


def rotate(values, cosine, sine):
    return values * cosine + pltpu.roll(values, HD // 2, 1) * sine


def project_kernel(idx, x_ref, gain_ref, bias_ref, cos_ref, sin_ref, w_ref, *refs):
    part_ref, q_outs, kv_outs = refs[0], refs[1 : 1 + HEADS], refs[1 + HEADS : 1 + 2 * HEADS]
    h_ref = refs[1 + 2 * HEADS]
    step = pl.program_id(0)

    @pl.when(step == 0)
    def _():
        normed, _ = normalise(x_ref[...].astype(F32))
        h_ref[...] = (normed * gain_ref[...] + bias_ref[...]).astype(BF16)
        rows = part_ref.shape[0]
        part_ref[...] = h_ref[pl.ds(pl.multiple_of(idx[5] * rows, rows), rows), :]

    both = nn(h_ref[...], jnp.concatenate([w_ref[0], w_ref[1]], axis=1))
    cosine, sine = cos_ref[...], sin_ref[...]
    queries = rotate(both[:, :HD], cosine, sine).astype(BF16)
    keys = rotate(both[:, HD:], cosine, sine).astype(BF16)
    values = nn(h_ref[...], w_ref[2]).astype(BF16)
    for k in range(HEADS):

        @pl.when(step == k)
        def _(k=k):
            q_outs[k][...] = queries
            kv_outs[k][:, :HD] = keys
            kv_outs[k][:, HD:] = values


def project(idx, x, gain, bias, cosine, sine, w_qkv):
    tok, dim = x.shape
    return pl.pallas_call(
        project_kernel,
        grid_spec=pltpu.PrefetchScalarGridSpec(
            num_scalar_prefetch=1,
            grid=(HEADS,),
            in_specs=[
                whole((tok, dim)),
                whole((1, dim)),
                whole((1, dim)),
                whole((tok, HD)),
                whole((tok, HD)),
                pl.BlockSpec((3, dim, HD), lambda k, idx: (0, 0, idx[0] ^ k)),
            ],
            out_specs=[whole((tok // 4, dim))]
            + [whole((tok, HD))] * HEADS
            + [whole((tok, 2 * HD))] * HEADS,
            scratch_shapes=[pltpu.VMEM((tok, dim), BF16)],
        ),
        out_shape=[jax.ShapeDtypeStruct((tok // 4, dim), BF16)]
        + [jax.ShapeDtypeStruct((tok, HD), BF16)] * HEADS
        + [jax.ShapeDtypeStruct((tok, 2 * HD), BF16)] * HEADS,
        compiler_params=params(40),
        cost_estimate=cost(True),
        name="project",
    )(idx, x, gain, bias, cosine, sine, w_qkv)


def visible_of(tile, key_block, query_places, query_firsts):
    key_places = key_block * tile + lax.broadcasted_iota(jnp.int32, (tile, 1), 0)
    return (key_places <= query_places) & (key_places >= query_firsts)


def gather_refs(refs, whole_ref):
    at = 0
    for ref in refs:
        whole_ref[at : at + ref.shape[0], :] = ref[...]
        at += ref.shape[0]


def over_blocks(low, full, at, masked, group, state):
    state = lax.fori_loop(low, full, masked, state)
    for size in GROUPS:
        count = lax.div(at - full, size)
        start = full
        state = lax.fori_loop(
            0, count, lambda j, st, s=size, a=start: group(a + s * j, s, st), state
        )
        full = full + size * count
    return lax.fori_loop(full, at + 1, masked, state)


def attend_kernel(tile, scale, n_kv, at_ref, low_ref, full_ref, row_ref, first_ref, *refs):
    q_refs, kv_refs, refs = refs[:HEADS], refs[HEADS : HEADS + n_kv], refs[HEADS + n_kv :]
    outs, (lse_ref, q_all, kv_all) = refs[:HEADS], refs[HEADS:]
    gather_refs(q_refs, q_all)
    gather_refs(kv_refs, kv_all)
    lanes = lax.broadcasted_iota(jnp.int32, (1, tile), 1)
    per_out = outs[0].shape[0] // tile
    scale_two = scale * LOG_E

    def one_block(i, carry):
        rows = pl.ds(pl.multiple_of(i * tile, tile), tile)
        queries = q_all[rows, :]
        firsts = first_ref[i]
        places = at_ref[i] * tile + lanes

        def key_rows(b):
            return pl.ds(pl.multiple_of(row_ref[b] * tile, tile), tile)

        def absorb(state, scores, values):
            run_max, run_sum, run_acc = state
            new_max = run_max
            for part in scores:
                new_max = jnp.maximum(new_max, jnp.max(part, axis=0, keepdims=True))
            factor = jnp.exp2(run_max - new_max)
            new_sum = run_sum * factor
            new_acc = run_acc * factor
            for part, rows in zip(scores, values, strict=True):
                probs = jnp.exp2(part - new_max)
                new_sum = new_sum + jnp.sum(probs, axis=0, keepdims=True)
                new_acc = new_acc + tn(rows, probs.astype(BF16))
            return (new_max, new_sum, new_acc)

        def masked(b, state):
            krows = key_rows(b)
            scores = nt(kv_all[krows, :HD], queries) * scale_two
            scores = jnp.where(visible_of(tile, b, places, firsts), scores, HIDDEN)
            return absorb(state, [scores], [kv_all[krows, HD:]])

        def group(b, size, state):
            rows = [key_rows(b + k) for k in range(size)]
            scores = [nt(kv_all[k, :HD], queries) * scale_two for k in rows]
            return absorb(state, scores, [kv_all[k, HD:] for k in rows])

        run_max, run_sum, run_acc = over_blocks(
            low_ref[i],
            full_ref[i],
            at_ref[i],
            masked,
            group,
            (
                jnp.full((1, tile), HIDDEN / 10, F32),
                jnp.zeros((1, tile), F32),
                jnp.zeros((HD, tile), F32),
            ),
        )
        q_all[rows, :] = (run_acc / run_sum).T.astype(BF16)
        lse_ref[i] = run_max + jnp.log2(run_sum)
        return carry

    lax.fori_loop(0, HEADS * per_out, one_block, 0)
    for k, out in enumerate(outs):
        out[...] = q_all[k * per_out * tile : (k + 1) * per_out * tile, :]


def attend_back_kernel(
    tile,
    scale,
    n_kv,
    at_ref,
    low_ref,
    full_ref,
    row_ref,
    first_ref,
    lse_ref,
    *refs,
):
    q_refs, kv_refs, refs = refs[:HEADS], refs[HEADS : HEADS + n_kv], refs[HEADS + n_kv :]
    o_refs, do_refs, dq_refs = refs[:HEADS], refs[HEADS : 2 * HEADS], refs[2 * HEADS : 3 * HEADS]
    near_ref, far_ref, q_all, kv_all, do_all, dot_all, acc_ref = refs[3 * HEADS :]
    gather_refs(q_refs, q_all)
    gather_refs(kv_refs, kv_all)
    gather_refs(do_refs, do_all)
    acc_ref[...] = jnp.zeros_like(acc_ref)
    lanes = lax.broadcasted_iota(jnp.int32, (1, tile), 1)
    per_out = dq_refs[0].shape[0] // tile
    scale_two = scale * LOG_E
    for k in range(HEADS):
        for j in range(per_out):
            piece = slice(j * tile, (j + 1) * tile)
            products = do_refs[k][piece, :].astype(F32) * o_refs[k][piece, :].astype(F32)
            dot_all[k * per_out + j] = jnp.sum(products.T, axis=0, keepdims=True)

    def one_block(i, carry):
        rows = pl.ds(pl.multiple_of(i * tile, tile), tile)
        queries = q_all[rows, :]
        grads = do_all[rows, :]
        firsts = first_ref[i]
        places = at_ref[i] * tile + lanes
        log_sums = lse_ref[i]
        deltas = dot_all[i]

        def one(b, grad_q, hide):
            krows = pl.ds(pl.multiple_of(row_ref[b] * tile, tile), tile)
            keys = kv_all[krows, :HD]
            probs = jnp.exp2(nt(keys, queries) * scale_two - log_sums)
            if hide:
                probs = jnp.where(visible_of(tile, b, places, firsts), probs, 0.0)
            grad_probs = nt(kv_all[krows, HD:], grads)
            grad_scores = (probs * (grad_probs - deltas)).astype(BF16)
            acc_ref[krows, HD:] += nn(probs.astype(BF16), grads)
            acc_ref[krows, :HD] += nn(grad_scores, queries)
            return grad_q + tn(keys, grad_scores)

        def group(b, size, grad_q):
            for k in range(size):
                grad_q = one(b + k, grad_q, False)
            return grad_q

        grad_q = over_blocks(
            low_ref[i],
            full_ref[i],
            at_ref[i],
            lambda b, grad_q: one(b, grad_q, True),
            group,
            jnp.zeros((HD, tile), F32),
        )
        do_all[rows, :] = (grad_q * scale).T.astype(BF16)
        return carry

    lax.fori_loop(0, HEADS * per_out, one_block, 0)
    for k, out in enumerate(dq_refs):
        out[...] = do_all[k * per_out * tile : (k + 1) * per_out * tile, :]
    near = near_ref.shape[0]
    near_ref[:, :HD] = (acc_ref[:near, :HD] * scale).astype(BF16)
    near_ref[:, HD:] = acc_ref[:near, HD:].astype(BF16)
    far_ref[:, :HD] = (acc_ref[near:, :HD] * scale).astype(BF16)
    far_ref[:, HD:] = acc_ref[near:, HD:].astype(BF16)


def attend(tile, scale, tables, pieces, keys_values):
    rows = HEADS * pieces[0].shape[0]
    kv_rows = sum(a.shape[0] for a in keys_values)
    operands = pieces + keys_values
    return pl.pallas_call(
        functools.partial(attend_kernel, tile, scale, len(keys_values)),
        out_shape=[jax.ShapeDtypeStruct((rows // HEADS, HD), BF16)] * HEADS
        + [jax.ShapeDtypeStruct((rows // tile, 1, tile), F32)],
        in_specs=[SMEM] * 4 + [VMEM] * (1 + len(operands)),
        out_specs=[VMEM] * (HEADS + 1),
        scratch_shapes=[pltpu.VMEM((rows, HD), BF16), pltpu.VMEM((kv_rows, 2 * HD), BF16)],
        compiler_params=params(50),
        cost_estimate=cost(True),
        name="attend",
    )(*tables, *operands)


def attend_back(tile, scale, tables, lse, pieces, keys_values, outs, grads):
    rows = HEADS * pieces[0].shape[0]
    kv_rows = sum(a.shape[0] for a in keys_values)
    operands = pieces + keys_values + outs + grads
    return pl.pallas_call(
        functools.partial(attend_back_kernel, tile, scale, len(keys_values)),
        out_shape=[jax.ShapeDtypeStruct((rows // HEADS, HD), BF16)] * HEADS
        + [jax.ShapeDtypeStruct((kv_rows // 2, 2 * HD), BF16)] * 2,
        in_specs=[SMEM] * 4 + [VMEM] * (2 + len(operands)),
        out_specs=[VMEM] * (HEADS + 2),
        scratch_shapes=[
            pltpu.VMEM((rows, HD), BF16),
            pltpu.VMEM((kv_rows, 2 * HD), BF16),
            pltpu.VMEM((rows, HD), BF16),
            pltpu.VMEM((rows // tile, 1, tile), F32),
            pltpu.VMEM((kv_rows, 2 * HD), F32),
        ],
        compiler_params=params(56),
        cost_estimate=cost(True),
        name="attend_back",
    )(*tables, lse, *operands)


def settle_kernel(near_ref, got_ref, cos_ref, sin_ref, *refs):
    dq_refs, outs = refs[:HEADS], refs[HEADS:]
    total = near_ref[...].astype(F32) + got_ref[...].astype(F32)
    tile = outs[0].shape[0]
    for k, out in enumerate(outs):

        @pl.when(pl.program_id(0) == k // 2)
        def _(k=k, out=out):
            rows = slice(k % 2 * tile, (k % 2 + 1) * tile)
            cosine, sine = cos_ref[rows, :], -sin_ref[rows, :]
            out[:, :HD] = rotate(dq_refs[k][...].astype(F32), cosine, sine).astype(BF16)
            out[:, HD : 2 * HD] = rotate(total[rows, :HD], cosine, sine).astype(BF16)
            out[:, 2 * HD :] = total[rows, HD:].astype(BF16)


def settle(near, got, cosine, sine, dq_pieces):
    rows = near.shape[0]
    tile = rows // HEADS
    spec = pl.BlockSpec((2 * tile, 2 * HD), lambda k: (k, 0))
    table = pl.BlockSpec((2 * tile, HD), lambda k: (k, 0))
    return pl.pallas_call(
        settle_kernel,
        grid=(HEADS // 2,),
        out_shape=[jax.ShapeDtypeStruct((tile, 3 * HD), BF16)] * HEADS,
        in_specs=[spec, spec, table, table] + [whole((tile, HD))] * HEADS,
        out_specs=[whole((tile, 3 * HD))] * HEADS,
        compiler_params=params(24),
        cost_estimate=cost(True),
        name="settle",
    )(near, got, cosine, sine, *dq_pieces)


def out_project_kernel(idx, w_ref, *refs):
    pieces, (flat_ref, keep_ref, give_ref) = refs[:HEADS], refs[HEADS:]
    for k, piece in enumerate(pieces):
        flat_ref[:, pl.ds(pl.multiple_of((idx[0] ^ k) * HD, HD), HD)] = piece[...]
    half = keep_ref.shape[0]
    core = idx[2]
    mine = flat_ref[pl.ds(pl.multiple_of(core * half, half), half), :]
    other = flat_ref[pl.ds(pl.multiple_of((1 - core) * half, half), half), :]
    give_ref[...] = nn(other, w_ref[...]).astype(BF16)
    keep_ref[...] = nn(mine, w_ref[...]).astype(BF16)


def out_project(idx, w_out, pieces):
    cols, dim = w_out.shape
    tok = pieces[0].shape[0]
    half = jax.ShapeDtypeStruct((tok // 2, dim), BF16)
    return pl.pallas_call(
        out_project_kernel,
        out_shape=[jax.ShapeDtypeStruct((tok, cols), BF16), half, half],
        in_specs=[SMEM] + [VMEM] * (1 + HEADS),
        out_specs=[VMEM] * 3,
        compiler_params=params(40),
        cost_estimate=cost(True),
        name="out_project",
    )(idx, w_out, *pieces)


def out_back_kernel(idx, w_ref, mine_ref, other_ref, *outs):
    half = mine_ref.shape[0]
    core = idx[2]
    for k, out in enumerate(outs):
        weights = w_ref[pl.ds(pl.multiple_of((idx[0] ^ k) * HD, HD), HD), :]
        out[pl.ds(pl.multiple_of(core * half, half), half), :] = nt(mine_ref[...], weights).astype(BF16)
        out[pl.ds(pl.multiple_of((1 - core) * half, half), half), :] = nt(
            other_ref[...], weights
        ).astype(BF16)


def out_back(idx, w_out, mine, other):
    half, dim = mine.shape
    return pl.pallas_call(
        out_back_kernel,
        out_shape=[jax.ShapeDtypeStruct((2 * half, HD), BF16)] * HEADS,
        in_specs=[SMEM] + [VMEM] * 3,
        out_specs=[VMEM] * HEADS,
        compiler_params=params(40),
        cost_estimate=cost(True),
        name="out_back",
    )(idx, w_out, mine, other)


def norm_kernel(x_ref, chip_ref, far_ref, gain_ref, bias_ref, bucket_ref, sum_ref, out_ref):
    dim = x_ref.shape[1]
    total = x_ref[...].astype(F32) + (chip_ref[...].astype(F32) + far_ref[...].astype(F32))
    sum_ref[...] = total
    normed, _ = normalise(total)
    out_ref[:, :dim] = (normed * gain_ref[...] + bias_ref[...]).astype(BF16)
    out_ref[:, dim:] = jnp.broadcast_to(bucket_ref[...], (total.shape[0], HD)).astype(BF16)


def norm(x, chip, far, gain, bias, buckets):
    rows, dim = x.shape
    tile = rows // 2
    spec = pl.BlockSpec((tile, dim), lambda i: (i, 0))
    wide = pl.BlockSpec((tile, dim + HD), lambda i: (i, 0))
    return pl.pallas_call(
        norm_kernel,
        grid=(2,),
        out_shape=[
            jax.ShapeDtypeStruct((rows, dim), F32),
            jax.ShapeDtypeStruct((rows, dim + HD), BF16),
        ],
        in_specs=[spec, spec, spec, whole((1, dim)), whole((1, dim))]
        + [pl.BlockSpec((tile, 1), lambda i: (i, 0))],
        out_specs=[spec, wide],
        compiler_params=params(24),
        cost_estimate=cost(True),
        name="norm",
    )(x, chip, far, gain, bias, buckets)


def norm_back_kernel(chip_ref, far_ref, x_ref, base_ref, gain_ref, wide_ref, low_ref, dg_ref, db_ref):
    grad = chip_ref[...].astype(F32) + far_ref[...].astype(F32)
    normed, inverse = normalise(x_ref[...].astype(F32))
    scaled = grad * gain_ref[...]
    back = inverse * (
        scaled
        - jnp.mean(scaled, axis=-1, keepdims=True)
        - normed * jnp.mean(scaled * normed, axis=-1, keepdims=True)
    )
    total = base_ref[...].astype(F32) + back
    wide_ref[...] = total
    low_ref[...] = total.astype(BF16)

    @pl.when(pl.program_id(0) == 0)
    def _():
        dg_ref[...] = jnp.zeros_like(dg_ref)
        db_ref[...] = jnp.zeros_like(db_ref)

    dg_ref[...] += jnp.sum(grad * normed, axis=0, keepdims=True)
    db_ref[...] += jnp.sum(grad, axis=0, keepdims=True)


def norm_back(chip, far, x, base, gain):
    rows, dim = chip.shape
    tile = rows // 2
    spec = pl.BlockSpec((tile, dim), lambda i: (i, 0))
    row = whole((1, dim))
    return pl.pallas_call(
        norm_back_kernel,
        grid=(2,),
        out_shape=[
            jax.ShapeDtypeStruct((rows, dim), F32),
            jax.ShapeDtypeStruct((rows, dim), BF16),
            jax.ShapeDtypeStruct((1, dim), F32),
            jax.ShapeDtypeStruct((1, dim), F32),
        ],
        in_specs=[spec] * 4 + [row],
        out_specs=[spec, spec, row, row],
        compiler_params=params(24),
        cost_estimate=cost(True),
        name="norm_back",
    )(chip, far, x, base, gain)


def relu_of(idx, ref, weights):
    dim = weights.shape[0]
    kept = ref[:, dim : dim + 1].astype(F32) >= idx[5].astype(F32)
    return jnp.where(kept, jnp.maximum(nn(ref[:, :dim], weights), 0.0), 0.0)


def feed_kernel(with_act, with_back, idx, mine_ref, other_ref, w_ref, gact_ref, *refs):
    half = mine_ref.shape[0]
    weights = w_ref[...]
    act_ref = refs[0] if with_act else None
    du_ref = refs[1 if with_act else 0]
    for at, ref in ((0, mine_ref), (half, other_ref)):
        rows = slice(at, at + half)
        relu = relu_of(idx, ref, weights)
        if with_act:
            act_ref[rows, :] = (relu * relu).astype(BF16)
        du_ref[rows, :] = (gact_ref[rows, :].astype(F32) * 2.0 * relu).astype(BF16)
    if with_back:
        keep_out, give_out, acc_ref = refs[2:]
        step = pl.program_id(0)

        @pl.when(step == 0)
        def _():
            acc_ref[...] = nt(du_ref[...], weights)

        @pl.when(step > 0)
        def _():
            acc_ref[...] += nt(du_ref[...], weights)

        @pl.when(step == pl.num_programs(0) - 1)
        def _():
            keep_out[...] = acc_ref[:half, :].astype(BF16)
            give_out[...] = acc_ref[half:, :].astype(BF16)


def feed_forward(idx, mine, other, w_up, gact, with_act, with_back):
    half, wide = mine.shape
    dim, hidden = w_up.shape
    tile = min(hidden, 512)
    tall = jax.ShapeDtypeStruct((2 * half, hidden), BF16)
    part = jax.ShapeDtypeStruct((half, dim), BF16)
    spec = pl.BlockSpec((2 * half, tile), lambda i, idx: (0, i))
    n_tall = 2 if with_act else 1
    return pl.pallas_call(
        functools.partial(feed_kernel, with_act, with_back),
        grid_spec=pltpu.PrefetchScalarGridSpec(
            num_scalar_prefetch=1,
            grid=(hidden // tile,),
            in_specs=[
                whole((half, wide)),
                whole((half, wide)),
                pl.BlockSpec((dim, tile), lambda i, idx: (0, i)),
                spec,
            ],
            out_specs=[spec] * n_tall + ([whole((half, dim))] * 2 if with_back else []),
            scratch_shapes=[pltpu.VMEM((2 * half, dim), F32)] if with_back else [],
        ),
        out_shape=[tall] * n_tall + ([part, part] if with_back else []),
        compiler_params=params(48),
        cost_estimate=cost(with_back),
        name="feed_own" if with_back else "feed_far",
    )(idx, mine, other, w_up, gact)


def feed_down_kernel(act_ref, w_ref, *refs):
    outs, acc_ref = refs[:4], refs[4]
    step = pl.program_id(0)

    @pl.when(step == 0)
    def _():
        acc_ref[...] = nn(act_ref[...], w_ref[...])

    @pl.when(step > 0)
    def _():
        acc_ref[...] += nn(act_ref[...], w_ref[...])

    @pl.when(step == pl.num_programs(0) - 1)
    def _():
        rows = outs[0].shape[0]
        for k, out in enumerate(outs):
            out[...] = acc_ref[k * rows : (k + 1) * rows, :].astype(BF16)


def feed_down(act, w_down):
    tok, hidden = act.shape
    dim = w_down.shape[1]
    tile = min(hidden, 1024)
    part = (tok // 4, dim)
    return pl.pallas_call(
        feed_down_kernel,
        grid=(hidden // tile,),
        out_shape=[jax.ShapeDtypeStruct(part, BF16)] * 4,
        in_specs=[
            pl.BlockSpec((tok, tile), lambda i: (0, i)),
            pl.BlockSpec((tile, dim), lambda i: (i, 0)),
        ],
        out_specs=[whole(part)] * 4,
        scratch_shapes=[pltpu.VMEM((tok, dim), F32)],
        compiler_params=params(40),
        cost_estimate=cost(False),
        name="feed_down",
    )(act, w_down)


def back_act_kernel(mine_ref, other_ref, w_ref, out_ref):
    half = mine_ref.shape[0]
    out_ref[:half, :] = nt(mine_ref[...], w_ref[...]).astype(BF16)
    out_ref[half:, :] = nt(other_ref[...], w_ref[...]).astype(BF16)


def back_act(mine, other, w_down):
    half, dim = mine.shape
    hidden = w_down.shape[0]
    tile = min(hidden, 512)
    return pl.pallas_call(
        back_act_kernel,
        grid=(hidden // tile,),
        out_shape=jax.ShapeDtypeStruct((2 * half, hidden), BF16),
        in_specs=[
            whole((half, dim)),
            whole((half, dim)),
            pl.BlockSpec((tile, dim), lambda i: (i, 0)),
        ],
        out_specs=pl.BlockSpec((2 * half, tile), lambda i: (0, i)),
        compiler_params=params(40),
        cost_estimate=cost(False),
        name="back_act",
    )(mine, other, w_down)


def product_kernel(idx, *refs):
    cols, near_ref, far_ref, out_ref, turn_ref = refs[:16], refs[16], refs[17], refs[18], refs[19]
    half, block = cols[0].shape

    @pl.when(pl.program_id(0) == 0)
    def _():
        for k, ref in enumerate(cols):
            rows = slice(k // 4 * block, (k // 4 + 1) * block)
            turn_ref[rows, k % 4 * half : (k % 4 + 1) * half] = ref[...].astype(F32).T.astype(BF16)

    starts = [pl.multiple_of(idx[3 + j] * half, half) for j in range(2)]
    total = None
    for k in range(4):
        rows = (near_ref, far_ref)[k // 2][pl.ds(starts[k % 2], half), :]
        term = nn(turn_ref[:, k * half : (k + 1) * half], rows)
        total = term if total is None else total + term
    out_ref[...] = total.astype(BF16)


def product(idx, cols, near, far, dim):
    half = cols[0].shape[0]
    tok, width = near.shape
    block = dim // (2 * HEADS)
    tile = min(width, 512)

    def columns(b):
        return pl.BlockSpec((half, block), lambda i, idx: (0, 2 * b + idx[1]))

    rows = pl.BlockSpec((tok, tile), lambda i, idx: (0, i))
    return pl.pallas_call(
        product_kernel,
        grid_spec=pltpu.PrefetchScalarGridSpec(
            num_scalar_prefetch=1,
            grid=(width // tile,),
            in_specs=[columns(b) for b in range(HEADS) for _ in range(4)] + [rows] * 2,
            out_specs=pl.BlockSpec((HEADS * block, tile), lambda i, idx: (0, i)),
            scratch_shapes=[pltpu.VMEM((HEADS * block, 2 * tok), BF16)],
        ),
        out_shape=jax.ShapeDtypeStruct((HEADS * block, width), BF16),
        compiler_params=params(40),
        cost_estimate=cost(False),
        name="product",
    )(idx, *(list(cols) * HEADS), near, far)


def plane_product_kernel(idx, *refs):
    cols, near_ref, far_ref, outs, turn_ref = refs[:16], refs[16], refs[17], refs[18:22], refs[22]
    half, block = cols[0].shape
    tok = 2 * half

    @pl.when(pl.program_id(0) == 0)
    def _():
        for k, ref in enumerate(cols):
            rows = slice(k // 4 * block, (k // 4 + 1) * block)
            turn_ref[rows, k % 4 * half : (k % 4 + 1) * half] = ref[...].astype(F32).T.astype(BF16)

    total = nn(turn_ref[:, :tok], near_ref[...]) + nn(turn_ref[:, tok:], far_ref[...])
    for k, out in enumerate(outs):
        out[...] = total[k * block : (k + 1) * block].astype(BF16)


def plane_product(idx, cols, near, far, dim):
    half = cols[0].shape[0]
    tok, width = near.shape
    block = dim // (2 * HEADS)
    tile = min(width, 512)

    def columns(b):
        def at(i, idx):
            parity = 1 - idx[1] if b < 2 else idx[1]
            return (0, 2 * (2 * (b % 2) + (idx[0] & 1)) + parity)

        return pl.BlockSpec((half, block), at)

    rows = pl.BlockSpec((tok, tile), lambda i, idx: (0, i))
    return pl.pallas_call(
        plane_product_kernel,
        grid_spec=pltpu.PrefetchScalarGridSpec(
            num_scalar_prefetch=1,
            grid=(width // tile,),
            in_specs=[columns(b) for b in range(4) for _ in range(4)] + [rows] * 2,
            out_specs=[pl.BlockSpec((block, tile), lambda i, idx: (0, i))] * 4,
            scratch_shapes=[pltpu.VMEM((4 * block, 2 * tok), BF16)],
        ),
        out_shape=[jax.ShapeDtypeStruct((block, width), BF16)] * 4,
        compiler_params=params(40),
        cost_estimate=cost(False),
        name="plane_product",
    )(idx, *(list(cols) * 4), near, far)


def head_product_kernel(idx, h_ref, *refs):
    pieces, (give_ref, keep_ref, turn_ref) = refs[:HEADS], refs[HEADS:]
    tok = pieces[0].shape[0]
    block = h_ref.shape[1] // 2

    @pl.when(pl.program_id(0) == 0)
    def _():
        for k in range(HEADS):
            turn_ref[:, k * tok : (k + 1) * tok] = pieces[k][...].astype(F32).T.astype(BF16)

    total = None
    for k in range(HEADS):
        rows = h_ref[pl.ds(pl.multiple_of((idx[0] ^ k) * tok, tok), tok), :]
        term = nn(turn_ref[:, k * tok : (k + 1) * tok], rows)
        total = term if total is None else total + term
    first, second = total[:, :block], total[:, block:]
    odd = idx[1] == 1
    give_ref[0] = jnp.where(odd, first, second).astype(BF16)
    keep_ref[0] = jnp.where(odd, second, first).astype(BF16)


def head_product(idx, h_all, pieces):
    rows, dim = h_all.shape
    block = dim // (2 * HEADS)
    out = jax.ShapeDtypeStruct((HEADS, 3 * HD, block), BF16)
    spec = pl.BlockSpec((1, 3 * HD, block), lambda k, idx: (k, 0, 0))
    return pl.pallas_call(
        head_product_kernel,
        grid_spec=pltpu.PrefetchScalarGridSpec(
            num_scalar_prefetch=1,
            grid=(HEADS,),
            in_specs=[pl.BlockSpec((rows, 2 * block), lambda k, idx: (0, idx[0] ^ k))]
            + [whole((rows // HEADS, 3 * HD))] * HEADS,
            out_specs=[spec, spec],
            scratch_shapes=[pltpu.VMEM((3 * HD, rows), BF16)],
        ),
        out_shape=[out, out],
        compiler_params=params(40),
        cost_estimate=cost(False),
        name="head_product",
    )(idx, h_all, *pieces)


def head_add_kernel(keep_ref, got_ref, after_ref, *outs):
    del after_ref
    for k, out in enumerate(outs):
        out[...] = (keep_ref[k].astype(F32) + got_ref[k].astype(F32)).astype(BF16)


def head_add(keep, got, after):
    return pl.pallas_call(
        head_add_kernel,
        out_shape=[jax.ShapeDtypeStruct(keep.shape[1:], BF16)] * HEADS,
        in_specs=[VMEM, VMEM, ANY],
        out_specs=[VMEM] * HEADS,
        compiler_params=params(24),
        cost_estimate=cost(False),
        name="head_add",
    )(keep, got, after)


def head_place_kernel(idx, *refs):
    pieces, out_ref = refs[:HEADS], refs[HEADS]
    for k, piece in enumerate(pieces):
        for s in range(3):
            out_ref[s, :, pl.ds(pl.multiple_of((idx[0] ^ k) * HD, HD), HD)] = (
                piece[s * HD : (s + 1) * HD, :].astype(F32).T
            )


def head_place(idx, pieces):
    rows, block = pieces[0].shape
    return pl.pallas_call(
        head_place_kernel,
        out_shape=jax.ShapeDtypeStruct((3, block, HEADS * HD), F32),
        in_specs=[SMEM] + [VMEM] * HEADS,
        out_specs=VMEM,
        compiler_params=params(24),
        cost_estimate=cost(False),
        name="head_place",
    )(idx, *pieces)


def project_back_kernel(idx, w_ref, *refs):
    pieces, (keep_ref, give_a_ref, give_b_ref, flat_ref, acc_ref) = refs[:HEADS], refs[HEADS:]
    half = keep_ref.shape[0]
    core = idx[2]
    step = pl.program_id(0)

    for s in range(3):

        @pl.when(step == s)
        def _(s=s):
            for k in range(HEADS):
                lanes = pl.ds(pl.multiple_of((idx[0] ^ k) * HD, HD), HD)
                flat_ref[:, lanes] = pieces[k][:, s * HD : (s + 1) * HD]

    @pl.when(step == 0)
    def _():
        acc_ref[...] = nt(flat_ref[...], w_ref[0])

    @pl.when(step > 0)
    def _():
        acc_ref[...] += nt(flat_ref[...], w_ref[0])

    @pl.when(step == 2)
    def _():
        part = half // 2
        for k, out in enumerate((give_a_ref, give_b_ref)):
            start = pl.multiple_of((1 - core) * half + k * part, part)
            out[...] = acc_ref[pl.ds(start, part), :].astype(BF16)
        keep_ref[...] = acc_ref[pl.ds(pl.multiple_of(core * half, half), half), :].astype(BF16)


def project_back(idx, w_qkv, pieces):
    tok = pieces[0].shape[0]
    _, dim, cols = w_qkv.shape
    return pl.pallas_call(
        project_back_kernel,
        grid_spec=pltpu.PrefetchScalarGridSpec(
            num_scalar_prefetch=1,
            grid=(3,),
            in_specs=[pl.BlockSpec((1, dim, cols), lambda s, idx: (s, 0, 0))]
            + [whole((tok, 3 * HD))] * HEADS,
            out_specs=[whole((tok // 2, dim))] + [whole((tok // 4, dim))] * 2,
            scratch_shapes=[pltpu.VMEM((tok, cols), BF16), pltpu.VMEM((tok, dim), F32)],
        ),
        out_shape=[jax.ShapeDtypeStruct((tok // 2, dim), BF16)]
        + [jax.ShapeDtypeStruct((tok // 4, dim), BF16)] * 2,
        compiler_params=params(40),
        cost_estimate=cost(True),
        name="project_back",
    )(idx, w_qkv, *pieces)


def join_kernel(idx, mine_ref, other_ref, out_ref):
    half = mine_ref.shape[0]
    core = idx[2]
    out_ref[pl.ds(pl.multiple_of(core * half, half), half), :] = mine_ref[...].astype(out_ref.dtype)
    out_ref[pl.ds(pl.multiple_of((1 - core) * half, half), half), :] = other_ref[...].astype(
        out_ref.dtype
    )


def join(idx, mine, other, dtype):
    half, dim = mine.shape
    return pl.pallas_call(
        join_kernel,
        out_shape=jax.ShapeDtypeStruct((2 * half, dim), dtype),
        in_specs=[SMEM, VMEM, VMEM],
        out_specs=VMEM,
        compiler_params=params(24),
        cost_estimate=cost(False),
        name="join",
    )(idx, mine, other)


def body(
    depth,
    layer_input,
    ln1_gain,
    ln1_bias,
    w_qkv,
    w_out,
    ln2_gain,
    ln2_bias,
    w_up,
    w_down,
    buckets,
    lengths,
    block_order,
    grad_out,
):
    tok, dim = layer_input.shape
    half = tok // 2
    scale = 1.0 / math.sqrt(HD)
    r, h, y, x, c = (lax.axis_index(a) for a in ("r", PLANE, "y") + TP)
    blk = lax.axis_index(BLK)
    tp = lax.axis_index(TP)
    idx_rows = jnp.stack([h, y, c, c, 1 - c]).astype(jnp.int32)
    idx = jnp.stack([h, y, c, jnp.zeros_like(c), jnp.ones_like(c), tp]).astype(jnp.int32)
    gains = [v.reshape(1, dim) for v in (ln1_gain, ln1_bias, ln2_gain, ln2_bias)]

    def half_of(values, which):
        return lax.dynamic_slice_in_dim(values, which * half, half, 0)

    def regroup(values):
        if depth == 1:
            return values
        rows = values.shape[0]
        split = values[:, :dim].reshape(rows, depth, HEADS, 2, dim // (2 * HEADS * depth))
        return split.transpose(0, 2, 3, 1, 4).reshape(rows, dim)

    def scatter(values):
        if depth > 1:
            split = values.reshape(HEADS, depth, -1, values.shape[1])
            values = split.transpose(1, 0, 2, 3).reshape(values.shape)
        return lax.psum_scatter(values, ("r",) + PLANE, scatter_dimension=0, tiled=True)

    starts = jnp.cumsum(lengths) - lengths

    def firsts_of(places):
        return jnp.max(jnp.where(starts <= places[..., None], starts, 0), axis=-1)

    inside = jnp.arange(half, dtype=jnp.int32)
    own_places = (
        lax.dynamic_slice_in_dim(block_order, 2 * blk, 2, 0)[:, None] * half + inside
    ).reshape(tok)
    cosine, sine = rotary_tables(own_places - firsts_of(own_places))

    def half_scatter(values):
        if depth > 1:
            split = values.reshape(2, depth, -1, values.shape[1])
            values = split.transpose(1, 0, 2, 3).reshape(values.shape)
        return lax.psum_scatter(values, ("r", "hh"), scatter_dimension=0, tiled=True)

    def chip_sum(keep, give):
        return (keep.astype(F32) + swap(give, "c").astype(F32)).astype(BF16)

    grad_mine, grad_other = half_of(grad_out, c), half_of(grad_out, 1 - c)
    own_rows, *projected = project(idx, layer_input, gains[0], gains[1], cosine, sine, w_qkv)
    queries, near_kv = list(projected[:HEADS]), list(projected[HEADS:])
    z_grad = plane_swap(grad_mine, 1)
    z_grad, near_kv[1] = ordered(z_grad, near_kv[1])
    near_kv = [near_kv[0]] + [plane_swap(near_kv[k], k) for k in range(1, HEADS)]
    *queries[1:], near_kv[2] = ordered(*queries[1:], near_kv[2])
    queries = [queries[0]] + [plane_swap(queries[k], k) for k in range(1, HEADS)]
    y_grad = swap(grad_mine, "y")

    relative = h ^ jnp.arange(HEADS, dtype=jnp.int32)
    group_order = lax.dynamic_index_in_dim(
        block_order.reshape(depth, HEADS, 2, 2), r, 0, keepdims=False
    )
    group_order = lax.dynamic_index_in_dim(group_order, y, 1, keepdims=False)
    chosen = relative[:, None] == jnp.arange(HEADS, dtype=jnp.int32)[None, :]
    query_at = jnp.sum(jnp.where(chosen[:, :, None], group_order[None], 0), axis=1).reshape(-1)
    query_places = query_at[:, None] * half + inside
    query_firsts = firsts_of(query_places)
    query_low = query_firsts[:, 0] // half
    query_full = jnp.minimum((query_firsts[:, -1] + half - 1) // half, query_at)
    block_count = block_order.shape[0]
    slots = jnp.argmax(
        block_order[None, :] == jnp.arange(block_count, dtype=jnp.int32)[:, None], axis=1
    ).astype(jnp.int32)
    slot_dev = slots // 2
    slot_plane = slot_dev // 2
    key_row = (
        jnp.where(slot_dev % 2 == y, 0, block_count // 2)
        + slot_plane // HEADS * (2 * HEADS)
        + ((slot_plane % HEADS) ^ h) * 2
        + slots % 2
    )
    group_cos, group_sin = rotary_tables((query_places - query_firsts).reshape(2 * HEADS * half))
    tables = (query_at, query_low, query_full, key_row, query_firsts.reshape(2 * HEADS, 1, half))

    grad_act = back_act(grad_mine, grad_other, w_down)
    far_first = swap(near_kv[0], "y")
    far_first, y_grad, grad_act, group_cos, group_sin, *near_kv[1:] = ordered(
        far_first, y_grad, grad_act, group_cos, group_sin, *near_kv[1:]
    )
    if depth == 1:
        keys_values = near_kv + [far_first, swap(jnp.concatenate(near_kv[1:]), "y")]
    else:
        near_all = lax.all_gather(jnp.concatenate(near_kv), "r", axis=0, tiled=True)
        keys_values = [near_all, swap(near_all, "y")]
    y_grad_other = swap(y_grad, "c")
    y_grad_other, *queries[1:], keys_values[-1] = ordered(
        y_grad_other, *queries[1:], keys_values[-1]
    )

    *attended, lse = attend(half, scale, tables, queries, keys_values)
    pieces = [attended[0]] + [plane_swap(attended[k], k) for k in range(1, HEADS)]
    z_grad, lse = ordered(z_grad, lse)
    z_grad_other = swap(z_grad, "c")
    z_grad_other, *pieces[1:] = ordered(z_grad_other, *pieces[1:])
    own_rows, pieces[1] = ordered(own_rows, pieces[1])
    flat, keep, give = out_project(idx, w_out, pieces)
    h_all = lax.all_gather(own_rows, PLANE + TP, axis=0, tiled=True)
    chip = chip_sum(keep, give)
    chip_far = swap(chip, "x")
    y_grad, flat = ordered(y_grad, flat)
    z_grad, flat = ordered(z_grad, flat)
    y_grad_act = back_act(y_grad, y_grad_other, w_down)
    z_grad_act = back_act(z_grad, z_grad_other, w_down)
    y_grad_act, z_grad_act, chip_far = ordered(y_grad_act, z_grad_act, chip_far)

    y_flat = swap(flat, "y")
    y_flat, chip_far = ordered(y_flat, chip_far)
    my_buckets = half_of(buckets, c).reshape(half, 1)
    x_mid, h_mine = norm(
        half_of(layer_input, c), chip, chip_far, gains[2], gains[3], my_buckets
    )
    h_other = swap(h_mine, "c")
    y_h = swap(h_mine, "y")
    act, du, keep, give = feed_forward(
        idx, h_mine, h_other, w_up, grad_act, True, True
    )
    chip = chip_sum(keep, give)
    chip_far = swap(chip, "x")

    for_plane, act = ordered(h_mine, act)
    z_h = plane_swap(for_plane, 1)

    y_h_other = swap(y_h, "c")
    y_act, y_du = feed_forward(idx, y_h, y_h_other, w_up, y_grad_act, True, False)
    pair_grads = [regroup(v) for v in (grad_mine, grad_other, y_grad, y_grad_other)]
    down_sum = product(idx, pair_grads, act, y_act, dim)
    down_sum, h_all, z_h, chip_far = ordered(down_sum, h_all, z_h, chip_far)
    down_part = scatter(down_sum)

    grad_mid, dy_mine, gain_two_grad, bias_two_grad = norm_back(
        chip, chip_far, x_mid, grad_mine, gains[2]
    )
    dy_other = swap(dy_mine, "c")
    z_h_other = swap(z_h, "c")
    grads = list(out_back(idx, w_out, dy_mine, dy_other))
    grads = [grads[0]] + [plane_swap(grads[k], k) for k in range(1, HEADS)]

    y_dy = swap(dy_mine, "y")
    z_h_other, dy_other = ordered(z_h_other, dy_other)
    (z_du,) = feed_forward(idx, z_h, z_h_other, w_up, z_grad_act, False, False)
    plane_rows = [regroup(v) for v in (h_mine, h_other, z_h, z_h_other)]
    *up_give, up_keep, up_last = plane_product(idx, plane_rows, du, z_du, dim)
    up_give[0], y_dy, *grads[1:] = ordered(up_give[0], y_dy, *grads[1:])
    up_got = [swap(up_give[0], "y")]
    y_dy_other = swap(y_dy, "c")

    *dq, near, far = attend_back(
        half, scale, tables, lse, queries, keys_values, attended, grads
    )
    got = swap(far, "y")

    for_feed, up_got[0], near = ordered(act, up_got[0], near)
    feed = list(feed_down(for_feed, w_down))
    wout_cols = [regroup(v) for v in (dy_mine, dy_other, y_dy, y_dy_other)]
    wout_cols[0], near = ordered(wout_cols[0], near)
    wout_sum = product(idx_rows, wout_cols, flat, y_flat, dim)
    wout_sum, down_part, feed[1], got = ordered(wout_sum, down_part, feed[1], got)
    if depth > 1:
        near = lax.psum_scatter(near, "r", scatter_dimension=0, tiled=True)
        got = lax.psum_scatter(got, "r", scatter_dimension=0, tiled=True)
    mixed = list(settle(near, got, group_cos, group_sin, dq))
    pieces = [mixed[0]] + [plane_swap(mixed[k], k) for k in range(1, HEADS)]
    feed_chip = [chip_sum(feed[k], feed[k + 2]) for k in range(2)]
    feed_far = [swap(v, "x") for v in feed_chip]

    head_give, head_keep = head_product(idx, regroup(h_all), mixed)
    up_give[1], mixed[2] = ordered(up_give[1], mixed[2])
    up_got.append(swap(up_give[1], "y"))
    feed_far[0], feed_far[1], head_give, wout_sum, up_got[1], *pieces[1:] = ordered(
        *feed_far, head_give, wout_sum, up_got[1], *pieces[1:]
    )
    up_sum = [
        (mine.astype(F32) + got.astype(F32)).astype(BF16)
        for mine, got in zip((up_keep, up_last), up_got, strict=True)
    ]
    up_part = half_scatter(jnp.concatenate(up_sum))
    keep, *gives = project_back(idx, w_qkv, pieces)
    chip = jnp.concatenate([swap(v, "c") for v in gives])
    chip = (keep.astype(F32) + chip.astype(F32)).astype(BF16)
    chip_far = swap(chip, "x")

    head_got = swap(head_give, "y")
    feed_chip, feed_far = jnp.concatenate(feed_chip), jnp.concatenate(feed_far)
    out_mine = (x_mid + (feed_chip.astype(F32) + feed_far.astype(F32))).astype(BF16)
    out_mine, wout_sum, chip = ordered(out_mine, wout_sum, chip)
    wout_part = scatter(wout_sum)
    out_other = swap(out_mine, "c")
    out_other, chip_far = ordered(out_other, chip_far)
    layer_output = join(idx, out_mine, out_other, BF16)
    head_got, chip_far = ordered(head_got, chip_far)

    _, grad_low, gain_one_grad, bias_one_grad = norm_back(
        chip, chip_far, half_of(layer_input, c), grad_mid, gains[0]
    )
    head_sum = list(head_add(head_keep, head_got, grad_low))
    if depth > 1:
        head_sum = [lax.psum_scatter(v, "r", scatter_dimension=1, tiled=True) for v in head_sum]
    head_pieces = [head_sum[0]] + [plane_swap(head_sum[k], k) for k in range(1, HEADS)]
    grad_input = join(idx, grad_low, swap(grad_low, "c"), F32)

    counts = jnp.sum(
        (half_of(buckets, c)[:, None] == jnp.arange(NB, dtype=jnp.int32)[None, :]).astype(F32),
        axis=0,
    )
    sums = jnp.concatenate(
        [v.reshape(dim) for v in (gain_one_grad, bias_one_grad, gain_two_grad, bias_two_grad)]
        + [counts]
    )
    if depth > 1:
        sums = lax.psum(sums, "r")
    one, two, three = (plane_swap(sums, k) for k in range(1, HEADS))
    sums = (sums + one) + (two + three)
    sums = sums + swap(sums, "y")
    qkv_part = head_place(idx, head_pieces)
    sums, up_part, grad_input, layer_output, qkv_part = ordered(
        sums, up_part, grad_input, layer_output, qkv_part
    )
    sums = sums + swap(sums, "c")
    return (
        layer_output,
        grad_input,
        sums[:dim],
        sums[dim : 2 * dim],
        qkv_part,
        wout_part.astype(F32).T,
        sums[2 * dim : 3 * dim],
        sums[3 * dim : 4 * dim],
        up_part.astype(F32),
        down_part.astype(F32).T,
        sums[4 * dim :].astype(jnp.int32),
    )


def solution(mesh):
    depth = mesh.shape["blk"] // (2 * HEADS)
    fine = Mesh(mesh.devices.reshape(depth, 2, 2, 2, 2, 2), BLK + TP)
    return jax.shard_map(
        functools.partial(body, depth),
        mesh=fine,
        in_specs=(
            P(BLK, None),
            P(),
            P(),
            P(None, None, TP),
            P(TP, None),
            P(),
            P(),
            P(None, TP),
            P(TP, None),
            P(BLK),
            P(),
            P(),
            P(BLK, None),
        ),
        out_specs=(
            P(BLK, None),
            P(BLK, None),
            P(),
            P(),
            P(None, BLK, TP),
            P(TP, BLK),
            P(),
            P(),
            P(BLK, TP),
            P(TP, BLK),
            P(),
        ),
        check_vma=False,
    )
```
